512 devices in a mesh: prompt: 32 (over z, core), rollout: 16 (over y, x).
Axes of the slice: x: 4, y: 4, z: 16, core: 2. Of those that a mesh axis runs over, the one named last changes fastest.
Arguments:
- row_grads: bfloat16 [32, 16, 50, 8192], P('prompt', 'rollout'), may hold values from -6 to 6
- used_ids: int32 [32, 16, 50], P('prompt', 'rollout'), may hold values from 0 to 383, as said below
- used_count: int32 [32, 16], P('prompt', 'rollout'), may hold values from 20 to 50
- pre_act: bfloat16 [12288, 5120], P('prompt', 'rollout'), may hold values from -8 to 8
- patches: bfloat16 [12288, 5120], P(('prompt', 'rollout')), may hold values from -6 to 6
- ln_gain: float32 [1280], replicated, may hold values from 0.25 to 1.75
- w_fc2: bfloat16 [5120, 8192], P('rollout', 'prompt'), may hold values from -0.078125 to 0.078125
- w_fc1: bfloat16 [5120, 5120], P('prompt', 'rollout'), may hold values from -0.078125 to 0.078125
Outputs:
- patch_grads: bfloat16 [12288, 5120], P(('prompt', 'rollout'))
The draws below stay inside these ranges and needn't reach their ends.
Inputs may be any that keep to these rules, and one draw needn't show every extreme that they name: `used_ids`: the first used_count entries of each rollout's list are distinct; at most 5 of them lie in one block of 24 rows r * 24 to r * 24 + 23; later entries are ignored.
All inputs are finite; a program needn't handle non-finite values.
Results may differ from the reference program's by a relative error of at most 0.0056.
Values may be sent and summed in bfloat16 or wider, within the bound.
No kernel may reach another device: no remote copies, remote signals or barrier semaphores. Data moves between devices by JAX's collectives and lax.ppermute only.
A program may use at most 64 MiB of HBM per device.

```python
import jax
import jax.numpy as jnp
from jax import lax

D_LLM = 8192
VIT = 1280
MERGE = 4
CAP = 5
ROWS_OWN = 24
HID = 5120
ROLLOUTS = 16
PROMPTS = 32
SLOTS = 50
GROUP_ROWS = 384


def route_plan(key):
    hottest = jax.random.randint(jax.random.fold_in(key, 11), (PROMPTS,), 0, ROLLOUTS)
    fullest = jax.random.randint(jax.random.fold_in(key, 12), (PROMPTS,), 0, ROLLOUTS)
    takes = jax.random.randint(jax.random.fold_in(key, 13), (PROMPTS, ROLLOUTS, ROLLOUTS), 1, 4)
    owner_axis = jnp.arange(ROLLOUTS, dtype=jnp.int32)[None, None, :]
    roll_axis = jnp.arange(ROLLOUTS, dtype=jnp.int32)[None, :, None]
    takes = jnp.where(roll_axis == fullest[:, None, None], 3, takes)
    takes = jnp.where(owner_axis == hottest[:, None, None], CAP, takes)
    totals = jnp.sum(takes, axis=-1).astype(jnp.int32)
    scores = jax.random.randint(jax.random.fold_in(key, 14), (PROMPTS, ROLLOUTS, ROLLOUTS, ROWS_OWN), 0, 1 << 20)
    scores = scores * ROWS_OWN + jnp.arange(ROWS_OWN, dtype=jnp.int32)
    picks = jnp.argsort(scores, axis=-1, stable=True)[..., :CAP].astype(jnp.int32)
    candidate = owner_axis[..., None] * ROWS_OWN + picks
    usable = jnp.arange(CAP, dtype=jnp.int32)[None, None, None, :] < takes[..., None]
    width = ROLLOUTS * CAP
    ranking = jax.random.randint(jax.random.fold_in(key, 15), (PROMPTS, ROLLOUTS, width), 0, 1 << 20)
    ranking = ranking * width + jnp.arange(width, dtype=jnp.int32)
    ranking = ranking + (1 - usable.reshape(PROMPTS, ROLLOUTS, width).astype(jnp.int32)) * (1 << 28)
    order = jnp.argsort(ranking, axis=-1, stable=True)[..., :SLOTS]
    chosen = jnp.take_along_axis(candidate.reshape(PROMPTS, ROLLOUTS, width), order, axis=-1)
    return (chosen.astype(jnp.int32), totals)


def draw_used_ids(key, part):
    return route_plan(key)[0]


def draw_used_count(key, part):
    return route_plan(key)[1]


def steps_of(stream_key, dims, shards, least, high):
    def one(axis_at, shards_of):
        steps = jax.random.uniform(jax.random.fold_in(jax.random.fold_in(stream_key, 6), axis_at), (shards_of,), jnp.float32, least / len(shards), high / len(shards))
        return jnp.repeat(jnp.exp(steps), dims[axis_at] // shards_of).reshape((-1,) + (1,) * (len(dims) - axis_at - 1))

    loudness = one(*shards[0])
    for cut in shards[1:]:
        loudness = loudness * one(*cut)
    return loudness


def centred(rng, extent, spread, bound, shards=(), kind=jnp.bfloat16):
    loudness = steps_of(rng, extent, shards, -0.22, 0.18) if shards else 1.0
    values = jax.random.normal(rng, extent, jnp.float32) * spread * loudness
    return jnp.minimum(jnp.maximum(values, -bound), bound).astype(kind)


def setup_inputs(seed: int = 0) -> dict:
    keys = jax.random.split(jax.random.key(seed), 9)
    row_grads = centred(keys[0], (PROMPTS, ROLLOUTS, SLOTS, D_LLM), 1.0, 6.0, ((0, 32), (1, 16)))
    used_ids = draw_used_ids(jax.random.fold_in(keys[8], 71), 0)
    used_count = draw_used_count(jax.random.fold_in(keys[8], 71), 0)
    pre_act = centred(keys[3], (PROMPTS * GROUP_ROWS, HID), 1.5, 8.0, ((0, 32), (1, 16)))
    patches = centred(keys[4], (PROMPTS * GROUP_ROWS, HID), 1.0, 6.0, ((0, 512),))
    ln_gain = jnp.clip(1.0 + 0.15 * jax.random.normal(keys[5], (VIT,), jnp.float32), 0.25, 1.75)
    w_fc2 = centred(keys[6], (HID, D_LLM), HID ** -0.5, 0.078125, ((0, 16), (1, 32)))
    w_fc1 = centred(keys[7], (HID, HID), HID ** -0.5, 0.078125, ((0, 32), (1, 16)))
    return dict(row_grads=row_grads, used_ids=used_ids, used_count=used_count, pre_act=pre_act, patches=patches, ln_gain=ln_gain, w_fc2=w_fc2, w_fc1=w_fc1)


def gelu_slope(value):
    return 0.5 * (1.0 + jax.scipy.special.erf(value * 0.7071067811865476)) + value * jnp.exp(-0.5 * value * value) * 0.3989422804014327

def prompt_sum(operands):
    slot_grads, slot_ids, slot_count = operands
    usable = jnp.arange(SLOTS, dtype=jnp.int32)[None, :] < slot_count[:, None]
    values = jnp.where(usable[:, :, None], slot_grads.astype(jnp.float32), jnp.float32(0.0))
    start = jnp.zeros((GROUP_ROWS, D_LLM), jnp.float32)
    return start.at[slot_ids.reshape(-1)].add(values.reshape(-1, D_LLM))

def reference(row_grads, used_ids, used_count, pre_act, patches, ln_gain, w_fc2, w_fc1):
    summed = lax.map(prompt_sum, (row_grads, used_ids, used_count))
    summed = summed.reshape(PROMPTS * GROUP_ROWS, D_LLM).astype(jnp.bfloat16)
    hidden_grad = jnp.dot(summed, w_fc2.T, preferred_element_type=jnp.float32)
    act_grad = (hidden_grad * gelu_slope(pre_act.astype(jnp.float32))).astype(jnp.bfloat16)
    upstream = jnp.dot(act_grad, w_fc1.T, preferred_element_type=jnp.float32)
    inputs = patches.astype(jnp.float32).reshape(-1, MERGE, VIT)
    scaled = upstream.reshape(-1, MERGE, VIT) * ln_gain
    inverse = lax.rsqrt(lax.optimization_barrier(jnp.mean(inputs * inputs, axis=-1, keepdims=True)) + 1e-06)
    inner = lax.optimization_barrier(jnp.mean(scaled * inputs, axis=-1, keepdims=True))
    result = inverse * scaled - inputs * inverse * inverse * inverse * inner
    return result.reshape(-1, HID).astype(jnp.bfloat16)
```

```python
import jax
import jax.numpy as jnp
from jax import lax
from jax.experimental import pallas as pl
from jax.experimental.pallas import tpu as pltpu
from jax.sharding import PartitionSpec as P

VIT = 1280
MERGE = 4
PROMPTS = 32
ROLLOUTS = 16
SIDE = 4
SLOTS = 50
PAD_SLOTS = 64
OWN = 24
ROWS = OWN * ROLLOUTS
D_LLM = 8192
COLS = D_LLM // ROLLOUTS
HID = 5120
HID_OWN = HID // ROLLOUTS
IN_OWN = HID // PROMPTS
W2_COLS = D_LLM // PROMPTS
TAIL = IN_OWN // 2
W_ROWS = HID_OWN + IN_OWN + TAIL
AXES = ("prompt", "rollout")
F32 = jnp.float32
BF16 = jnp.bfloat16


def gelu_slope(value):
    return (
        0.5 * (1.0 + jax.scipy.special.erf(value * 0.7071067811865476))
        + value * jnp.exp(-0.5 * value * value) * 0.3989422804014327
    )


def dot_t(left, right):
    return lax.dot_general(left, right, (((1,), (1,)), ((), ())), preferred_element_type=F32)


def line_groups(phase):
    groups = []
    for prompt in range(PROMPTS):
        for other in range(SIDE):
            along_x = (prompt % 2 == 0) == (phase == 0)
            line = [(other * SIDE + i) if along_x else (i * SIDE + other) for i in range(SIDE)]
            groups.append([prompt * ROLLOUTS + r for r in line])
    return groups


def exchange(blocks, phase):
    return lax.all_to_all(
        blocks, AXES, split_axis=0, concat_axis=0, axis_index_groups=line_groups(phase), tiled=True
    )


def pack_kernel(grads_ref, meta_ref, out_ref):
    for k in range(ROLLOUTS):
        cols = pl.ds(k * COLS, COLS)
        out_ref[k, 0:48, :] = grads_ref[0:48, cols]
        out_ref[k, 48:64, :] = (grads_ref[48:64, cols].astype(F32) + meta_ref[...]).astype(BF16)


def sum_kernel(recv_ref, out_ref):
    rows = (lax.broadcasted_iota(jnp.int32, (ROWS, 4 * PAD_SLOTS), 0) + 1).astype(F32)
    total = jnp.zeros((ROWS, COLS), F32)
    for g in range(ROLLOUTS // 4):
        codes = jnp.zeros((8, 4 * PAD_SLOTS), F32)
        for k in range(4):
            tile = recv_ref[4 * g + k, 48:64, 0 : 4 * PAD_SLOTS].astype(F32)[0:8]
            codes = codes + (pltpu.roll(tile, PAD_SLOTS * k, 1) if k else tile)
        row = codes[2:3] * 16.0 + codes[3:4]
        onehot = jnp.where(rows == row, 1.0, 0.0).astype(BF16)
        block = recv_ref[4 * g : 4 * g + 4].reshape(4 * PAD_SLOTS, COLS)
        total = total + jnp.dot(onehot, block, preferred_element_type=F32)
    value = total.astype(BF16)
    for k in range(SIDE):
        out_ref[k] = value


def mlp_kernel(core_ref, w_ref, s_ref, slope_ref, out_ref, w2, w1a, w1b, sems):
    copies = []
    parts = 4
    step = PROMPTS // parts
    for i in range(parts):
        span = pl.ds(i * step, step)
        copies.append(pltpu.make_async_copy(w_ref.at[span, 0:HID_OWN], w2.at[span], sems.at[i]))
    copies.append(pltpu.make_async_copy(w_ref.at[:, HID_OWN : HID_OWN + IN_OWN], w1a, sems.at[parts]))
    copies.append(pltpu.make_async_copy(w_ref.at[:, HID_OWN + IN_OWN : W_ROWS], w1b, sems.at[parts + 1]))
    for copy in copies:
        copy.start()
    for copy in copies[:parts]:
        copy.wait()
    even = core_ref[0] == 0

    def add(slot, hidden):
        j, k = slot // SIDE, slot % SIDE
        block = jnp.where(even, j * SIDE + k, k * SIDE + j)
        s = s_ref[slot]
        hidden = hidden + dot_t(s[:, :W2_COLS], w2[2 * block])
        return hidden + dot_t(s[:, W2_COLS:], w2[2 * block + 1])

    hidden = lax.fori_loop(0, ROLLOUTS, add, jnp.zeros((ROWS, HID_OWN), F32))
    act = (hidden * slope_ref[...]).astype(BF16)
    for copy in copies[parts:]:
        copy.wait()
    four = 4
    for g in range(PROMPTS // four):
        a = w1a[four * g : four * (g + 1)].reshape(four * IN_OWN, 256)
        b = w1b[four * g : four * (g + 1)]
        b = jnp.concatenate([b[:, :, :128], b[:, :, 128:]], axis=1).reshape(four * IN_OWN, 128)
        part = dot_t(act[:, :256], a) + dot_t(act[:, 256:], b[:, :64])
        out_ref[:, four * IN_OWN * g : four * IN_OWN * (g + 1)] = part.astype(BF16)


def add_kernel(recv_ref, out_ref):
    total = recv_ref[0].astype(F32)
    for k in range(1, SIDE):
        total = total + recv_ref[k].astype(F32)
    out_ref[...] = total.astype(BF16)


def norm_kernel(recv_ref, patches_ref, gain_ref, out_ref):
    for m in range(MERGE):
        cols = slice(m * VIT, (m + 1) * VIT)
        upstream = recv_ref[0, :, cols].astype(F32)
        for k in range(1, SIDE):
            upstream = upstream + recv_ref[k, :, cols].astype(F32)
        inputs = patches_ref[:, cols].astype(F32)
        scaled = upstream * gain_ref[...]
        inverse = lax.rsqrt(jnp.mean(inputs * inputs, axis=-1, keepdims=True) + 1e-06)
        inner = jnp.mean(scaled * inputs, axis=-1, keepdims=True)
        result = inverse * scaled - inputs * inverse * inverse * inverse * inner
        out_ref[:, cols] = result.astype(BF16)


def call(kernel, out_shape, n_in, flops=0, bytes_accessed=0, **kw):
    vmem = pl.BlockSpec(memory_space=pltpu.VMEM)
    return pl.pallas_call(
        kernel,
        out_shape=jax.ShapeDtypeStruct(out_shape, BF16),
        in_specs=kw.pop("in_specs", [vmem] * n_in),
        out_specs=vmem,
        cost_estimate=pl.CostEstimate(flops=flops, bytes_accessed=bytes_accessed, transcendentals=0),
        compiler_params=pltpu.CompilerParams(vmem_limit_bytes=kw.pop("vmem", 16 << 20)),
        **kw,
    )


def per_device(row_grads, used_ids, used_count, pre_act, patches, ln_gain, w_fc2, w_fc1):
    core = lax.axis_index("prompt") % 2
    tail = jnp.pad(w_fc1[:, 256:], ((0, 0), (0, 64)))
    weights = jnp.concatenate(
        [w_fc2, w_fc1[:, :256], jnp.concatenate([tail[:TAIL], tail[TAIL:]], axis=1)], axis=0
    )
    weights = lax.all_gather(weights, "prompt", axis=0, tiled=False)

    ids = used_ids[0]
    owner = ids // OWN
    turned = (owner % SIDE) * SIDE + owner // SIDE
    place = jnp.where(core == 0, turned, owner) * OWN + ids % OWN + 1
    place = jnp.where(jnp.arange(SLOTS, dtype=jnp.int32)[None] < used_count, place, 0)
    place = jnp.pad(place, ((0, 0), (0, COLS - SLOTS)))
    codes = jnp.concatenate([place // 16, place % 16], axis=0).astype(F32)
    meta = jnp.pad(codes, ((2, 12), (0, 0)))
    grads = jnp.pad(row_grads[0, 0], ((0, PAD_SLOTS - SLOTS), (0, 0)))
    outgoing = call(pack_kernel, (ROLLOUTS, PAD_SLOTS, COLS), 2, bytes_accessed=2 << 20)(grads, meta)
    received = lax.all_to_all(outgoing, "rollout", split_axis=0, concat_axis=0, tiled=True)
    summed = call(sum_kernel, (SIDE, ROWS, COLS), 1, flops=1 << 28, bytes_accessed=3 << 20)(received)
    line = exchange(summed, 0)
    plane = exchange(jnp.broadcast_to(line[None], (SIDE, SIDE, ROWS, COLS)), 1)

    slope = gelu_slope(pre_act.astype(F32)).reshape(SIDE, SIDE, OWN, HID_OWN)
    slope = jnp.where(core == 0, slope.transpose(1, 0, 2, 3), slope).reshape(ROWS, HID_OWN)
    vmem = pl.BlockSpec(memory_space=pltpu.VMEM)
    partial = call(
        mlp_kernel,
        (ROWS, HID),
        4,
        flops=3 << 30,
        bytes_accessed=20 << 20,
        vmem=50 << 20,
        in_specs=[
            pl.BlockSpec(memory_space=pltpu.SMEM),
            pl.BlockSpec(memory_space=pl.ANY),
            vmem,
            vmem,
        ],
        scratch_shapes=[
            pltpu.VMEM((PROMPTS, HID_OWN, W2_COLS), BF16),
            pltpu.VMEM((PROMPTS, IN_OWN, 256), BF16),
            pltpu.VMEM((PROMPTS, TAIL, 256), BF16),
            pltpu.SemaphoreType.DMA((6,)),
        ],
    )(core.astype(jnp.int32)[None], weights, plane.reshape(ROLLOUTS, ROWS, COLS), slope)

    halfway = exchange(partial.reshape(SIDE, SIDE * OWN, HID), 0)
    halfway = call(add_kernel, (SIDE * OWN, HID), 1, bytes_accessed=5 << 20, vmem=24 << 20)(halfway)
    last = exchange(halfway.reshape(SIDE, OWN, HID), 1)
    return call(norm_kernel, (OWN, HID), 3, bytes_accessed=2 << 20)(
        last, patches, ln_gain.reshape(1, VIT)
    )


def solution(mesh):
    return jax.shard_map(
        per_device,
        mesh=mesh,
        in_specs=(
            P("prompt", "rollout", None, None),
            P("prompt", "rollout", None),
            P("prompt", "rollout"),
            P("prompt", "rollout"),
            P(("prompt", "rollout"), None),
            P(),
            P("rollout", "prompt"),
            P("prompt", "rollout"),
        ),
        out_specs=P(("prompt", "rollout"), None),
        check_vma=False,
    )
```

```python
import jax
import jax.numpy as jnp
from jax import lax
from jax.experimental import pallas as pl
from jax.experimental.pallas import tpu as pltpu
from jax.sharding import PartitionSpec as P

VIT = 1280
MERGE = 4
PROMPTS = 32
ROLLOUTS = 16
SIDE = 4
SLOTS = 50
PAD_SLOTS = 64
OWN = 24
ROWS = OWN * ROLLOUTS
D_LLM = 8192
COLS = D_LLM // ROLLOUTS
HID = 5120
HID_OWN = HID // ROLLOUTS
IN_OWN = HID // PROMPTS
W2_COLS = D_LLM // PROMPTS
TAIL = IN_OWN // 2
W_ROWS = HID_OWN + IN_OWN + TAIL
AXES = ("prompt", "rollout")
F32 = jnp.float32
BF16 = jnp.bfloat16


def gelu_slope(value):
    return (
        0.5 * (1.0 + jax.scipy.special.erf(value * 0.7071067811865476))
        + value * jnp.exp(-0.5 * value * value) * 0.3989422804014327
    )


def dot_t(left, right):
    return lax.dot_general(left, right, (((1,), (1,)), ((), ())), preferred_element_type=F32)


def line_groups(phase):
    groups = []
    for prompt in range(PROMPTS):
        for other in range(SIDE):
            along_x = (prompt % 2 == 0) == (phase == 0)
            line = [(other * SIDE + i) if along_x else (i * SIDE + other) for i in range(SIDE)]
            groups.append([prompt * ROLLOUTS + r for r in line])
    return groups


def exchange(blocks, phase):
    return lax.all_to_all(
        blocks, AXES, split_axis=0, concat_axis=0, axis_index_groups=line_groups(phase), tiled=True
    )


def shift(value, phase, by):
    pairs = []
    for line in line_groups(phase):
        pairs += [(line[i], line[(i + by) % SIDE]) for i in range(SIDE)]
    return lax.ppermute(value, AXES, pairs)


def place_in_plane():
    rollout = lax.axis_index("rollout")
    even = lax.axis_index("prompt") % 2 == 0
    y, x = rollout // SIDE, rollout % SIDE
    return even, jnp.where(even, x, y), jnp.where(even, y, x)


def weights_kernel(w2_ref, w1_ref, out_ref):
    out_ref[0:HID_OWN, :] = w2_ref[...]
    out_ref[HID_OWN : HID_OWN + IN_OWN, :] = w1_ref[:, 0:256]
    base = HID_OWN + IN_OWN
    out_ref[base:W_ROWS, :] = jnp.zeros((TAIL, 256), BF16)
    out_ref[base:W_ROWS, 0:64] = w1_ref[0:TAIL, 256:320]
    out_ref[base:W_ROWS, 128:192] = w1_ref[TAIL:IN_OWN, 256:320]


def pack_kernel(count_ref, ids_ref, grads_ref, out_ref, meta):
    even, _, _ = place_in_plane()
    ids = ids_ref[...]
    owner = (ids * 2731) >> 16
    turned = (owner & 3) * SIDE + (owner >> 2)
    place = jnp.where(even, turned, owner) * OWN + ids - owner * OWN + 1
    live = lax.broadcasted_iota(jnp.int32, (1, SLOTS), 1) < count_ref[0, 0]
    place = jnp.where(live, place, 0)
    meta[...] = jnp.zeros((8, COLS), F32)
    meta[2:3, 0:SLOTS] = (place >> 4).astype(F32)
    meta[3:4, 0:SLOTS] = (place & 15).astype(F32)
    codes = meta[...]
    zeros = jnp.zeros((8, COLS), F32)
    for k in range(ROLLOUTS):
        cols = pl.ds(k * COLS, COLS)
        out_ref[k, 0:48, :] = grads_ref[0:48, cols]
        two = jnp.concatenate([grads_ref[48:SLOTS, cols].astype(F32), zeros[0:6]], axis=0)
        out_ref[k, 48:64, :] = jnp.concatenate([two + codes, zeros], axis=0).astype(BF16)


def sum_kernel(recv_ref, out_ref):
    rows = (lax.broadcasted_iota(jnp.int32, (ROWS, 4 * PAD_SLOTS), 0) + 1).astype(F32)
    total = jnp.zeros((ROWS, COLS), F32)
    for g in range(ROLLOUTS // 4):
        codes = jnp.zeros((8, 4 * PAD_SLOTS), F32)
        for k in range(4):
            tile = recv_ref[4 * g + k, 48:64, 0 : 4 * PAD_SLOTS].astype(F32)[0:8]
            codes = codes + (pltpu.roll(tile, PAD_SLOTS * k, 1) if k else tile)
        row = codes[2:3] * 16.0 + codes[3:4]
        onehot = jnp.where(rows == row, 1.0, 0.0).astype(BF16)
        block = recv_ref[4 * g : 4 * g + 4].reshape(4 * PAD_SLOTS, COLS)
        total = total + jnp.dot(onehot, block, preferred_element_type=F32)
    value = total.astype(BF16)
    for k in range(SIDE):
        out_ref[k] = value


def start_w1(w_ref, w1, sems):
    base = HID_OWN + IN_OWN
    copies = [
        pltpu.make_async_copy(w_ref.at[:, HID_OWN:base], w1.at[:, :, 0:256], sems.at[0]),
        pltpu.make_async_copy(w_ref.at[:, base:W_ROWS, 0:128], w1.at[:, 0:TAIL, 256:384], sems.at[1]),
        pltpu.make_async_copy(w_ref.at[:, base:W_ROWS, 128:256], w1.at[:, TAIL:IN_OWN, 256:384], sems.at[2]),
    ]
    for copy in copies:
        copy.start()
    return copies


def w1_chunk(w1, g, prompts):
    return w1[prompts * g : prompts * (g + 1)].reshape(prompts * IN_OWN, 384)[:, :HID_OWN]


GATHERED = ((0, (0, 1, 2, 3), 0), (1, (0, 1), 3), (2, (2, 3), 3), (3, (2, 3), 1), (4, (0, 1), 1), (5, (0, 1), 2), (6, (2, 3), 2))


def act_kernel(w_ref, *refs):
    sums, (slope_ref, act_ref, low_ref, high_ref, w2, w1, sems2, sems1) = refs[:7], refs[7:]
    even, first, second = place_in_plane()
    slots, copies = [], []
    for operand, places, offset in GATHERED:
        for n, k in enumerate(places):
            s = lax.rem(second + offset, SIDE)
            block = jnp.where(even, s * SIDE + k, k * SIDE + s)
            i = len(slots)
            pair = [
                pltpu.make_async_copy(
                    w_ref.at[2 * block + h, 0:HID_OWN],
                    w2.at[:, pl.ds((2 * i + h) * W2_COLS, W2_COLS)],
                    sems2.at[i, h],
                )
                for h in range(2)
            ]
            for copy in pair:
                copy.start()
            copies.append(pair)
            slots.append((sums[operand], n))
    late = start_w1(w_ref, w1, sems1)
    hidden = None
    for i, (ref, n) in enumerate(slots):
        for copy in copies[i]:
            copy.wait()
        part = dot_t(ref[n], w2[:, i * COLS : (i + 1) * COLS])
        hidden = part if hidden is None else hidden + part
    act_ref[...] = (hidden * slope_ref[...]).astype(BF16)
    far = lax.rem(first + 2, SIDE)
    rows = act_ref[pl.ds(pl.multiple_of(far * 96, 96), 96), :]
    for copy in late:
        copy.wait()
    for g in range(8):
        part = dot_t(rows, w1_chunk(w1, g, 4)).astype(BF16)
        cols = slice(640 * g, 640 * (g + 1))
        low_ref[:, cols] = part[:48]
        high_ref[:, cols] = part[48:]


def rest_kernel(w_ref, act_ref, right_low, right_high, left_low, left_high, own_ref, w1, sems1):
    _, first, _ = place_in_plane()
    late = start_w1(w_ref, w1, sems1)
    blocks = [
        act_ref[pl.ds(pl.multiple_of(lax.rem(first + by, SIDE) * 96, 96), 96), :] for by in (1, 3, 0)
    ]
    rows = jnp.concatenate(blocks, axis=0)
    for copy in late:
        copy.wait()
    for g in range(8):
        part = dot_t(rows, w1_chunk(w1, g, 4)).astype(BF16)
        cols = slice(640 * g, 640 * (g + 1))
        right_low[:, cols] = part[0:48]
        right_high[:, cols] = part[48:96]
        left_low[:, cols] = part[96:144]
        left_high[:, cols] = part[144:192]
        own_ref[:, cols] = part[192:288]


def pair_kernel(a_ref, b_ref, out_ref):
    out_ref[...] = (a_ref[...].astype(F32) + b_ref[...].astype(F32)).astype(BF16)


def join_kernel(own_ref, low_a, low_b, high_a, high_b, out_ref):
    low = own_ref[0:48].astype(F32) + low_a[...].astype(F32) + low_b[...].astype(F32)
    high = own_ref[48:96].astype(F32) + high_a[...].astype(F32) + high_b[...].astype(F32)
    out_ref[0:48] = low.astype(BF16)
    out_ref[48:96] = high.astype(BF16)


def norm_kernel(recv_ref, patches_ref, gain_ref, out_ref):
    for m in range(MERGE):
        cols = slice(m * VIT, (m + 1) * VIT)
        upstream = recv_ref[0, :, cols].astype(F32)
        for k in range(1, SIDE):
            upstream = upstream + recv_ref[k, :, cols].astype(F32)
        inputs = patches_ref[:, cols].astype(F32)
        scaled = upstream * gain_ref[...]
        inverse = lax.rsqrt(jnp.mean(inputs * inputs, axis=-1, keepdims=True) + 1e-06)
        inner = jnp.mean(scaled * inputs, axis=-1, keepdims=True)
        result = inverse * scaled - inputs * inverse * inverse * inverse * inner
        out_ref[:, cols] = result.astype(BF16)


VMEM = pl.BlockSpec(memory_space=pltpu.VMEM)
SMEM = pl.BlockSpec(memory_space=pltpu.SMEM)
ANY = pl.BlockSpec(memory_space=pl.ANY)


def call(kernel, shapes, in_specs, flops=0, moved=0, vmem=16, scratch=()):
    one = not isinstance(shapes[0], tuple)
    shapes = (shapes,) if one else shapes
    run = pl.pallas_call(
        kernel,
        out_shape=[jax.ShapeDtypeStruct(shape, BF16) for shape in shapes],
        in_specs=in_specs,
        out_specs=[VMEM] * len(shapes),
        scratch_shapes=list(scratch),
        cost_estimate=pl.CostEstimate(flops=flops, bytes_accessed=moved, transcendentals=0),
        compiler_params=pltpu.CompilerParams(vmem_limit_bytes=vmem << 20),
    )
    return (lambda *args: run(*args)[0]) if one else run


def per_device(row_grads, used_ids, used_count, pre_act, patches, ln_gain, w_fc2, w_fc1):
    weights = call(weights_kernel, (W_ROWS, 256), [VMEM] * 2)(w_fc2, w_fc1)
    weights = lax.all_gather(weights, "prompt", axis=0, tiled=False)

    outgoing = call(
        pack_kernel, (ROLLOUTS, PAD_SLOTS, COLS), [SMEM, VMEM, VMEM], scratch=[pltpu.VMEM((8, COLS), F32)]
    )(used_count, used_ids[0], row_grads[0, 0])
    received = lax.all_to_all(outgoing, "rollout", split_axis=0, concat_axis=0, tiled=True)
    summed = call(sum_kernel, (SIDE, ROWS, COLS), [VMEM])(received)
    line = exchange(summed, 0)
    a1, b1 = shift(line[:2], 1, 1), shift(line[2:], 1, -1)
    a2, b2 = shift(line[2:], 1, 1), shift(line[:2], 1, -1)
    a3, b3 = shift(a1, 1, 1), shift(b1, 1, -1)

    even = lax.axis_index("prompt") % 2 == 0
    slope = gelu_slope(pre_act.astype(F32)).reshape(SIDE, SIDE, OWN, HID_OWN)
    slope = jnp.where(even, slope.transpose(1, 0, 2, 3), slope).reshape(ROWS, HID_OWN)
    w1_scratch = [pltpu.VMEM((PROMPTS, IN_OWN, 384), BF16), pltpu.SemaphoreType.DMA((3,))]
    act, far_low, far_high = call(
        act_kernel,
        ((ROWS, HID_OWN), (48, HID), (48, HID)),
        [ANY] + [VMEM] * 8,
        flops=5 << 29,
        moved=12 << 20,
        vmem=30,
        scratch=[
            pltpu.VMEM((HID_OWN, D_LLM), BF16),
            w1_scratch[0],
            pltpu.SemaphoreType.DMA((ROLLOUTS, 2)),
            w1_scratch[1],
        ],
    )(weights, line, a1, a2, b1, b2, a3, b3, slope)

    via_right, via_left = shift(far_low, 0, 1), shift(far_high, 0, -1)
    right_low, right_high, left_low, left_high, own = call(
        rest_kernel,
        ((48, HID),) * 4 + ((96, HID),),
        [ANY, VMEM],
        flops=1 << 30,
        moved=8 << 20,
        vmem=20,
        scratch=w1_scratch,
    )(weights, act)
    high_a, low_b = shift(right_high, 0, 1), shift(left_low, 0, -1)
    pair = call(pair_kernel, (48, HID), [VMEM] * 2)
    low_a, high_b = shift(pair(right_low, via_right), 0, 1), shift(pair(left_high, via_left), 0, -1)
    halfway = call(join_kernel, (96, HID), [VMEM] * 5)(own, low_a, low_b, high_a, high_b)
    last = exchange(halfway.reshape(SIDE, OWN, HID), 1)
    return call(norm_kernel, (OWN, HID), [VMEM] * 3)(last, patches, ln_gain.reshape(1, VIT))


def solution(mesh):
    return jax.shard_map(
        per_device,
        mesh=mesh,
        in_specs=(
            P("prompt", "rollout", None, None),
            P("prompt", "rollout", None),
            P("prompt", "rollout"),
            P("prompt", "rollout"),
            P(("prompt", "rollout"), None),
            P(),
            P("rollout", "prompt"),
            P("prompt", "rollout"),
        ),
        out_specs=P(("prompt", "rollout"), None),
        check_vma=False,
    )
```

```python
import jax
import jax.numpy as jnp
from jax import lax
from jax.experimental import pallas as pl
from jax.experimental.pallas import tpu as pltpu
from jax.sharding import PartitionSpec as P

VIT = 1280
MERGE = 4
PROMPTS = 32
ROLLOUTS = 16
SIDE = 4
SLOTS = 50
PAD_SLOTS = 64
OWN = 24
ROWS = OWN * ROLLOUTS
D_LLM = 8192
COLS = D_LLM // ROLLOUTS
HID = 5120
HID_OWN = HID // ROLLOUTS
IN_OWN = HID // PROMPTS
W2_COLS = D_LLM // PROMPTS
PART = IN_OWN // SIDE
PART_PAD = 48
W1_ROWS = SIDE * PART_PAD
W_ROWS = HID_OWN + W1_ROWS + PART_PAD
IN_PAD = PROMPTS * PART_PAD
HALF = IN_PAD // (2 * MERGE)
AXES = ("prompt", "rollout")
F32 = jnp.float32
BF16 = jnp.bfloat16
VMEM = pl.BlockSpec(memory_space=pltpu.VMEM)
SMEM = pl.BlockSpec(memory_space=pltpu.SMEM)
HBM = pl.BlockSpec(memory_space=pltpu.HBM)


def gelu_slope(value):
    return (
        0.5 * (1.0 + jax.scipy.special.erf(value * 0.7071067811865476))
        + value * jnp.exp(-0.5 * value * value) * 0.3989422804014327
    )


def dot_t(left, right):
    return lax.dot_general(left, right, (((1,), (1,)), ((), ())), preferred_element_type=F32)


def line_groups(phase):
    groups = []
    for prompt in range(PROMPTS):
        for other in range(SIDE):
            along_x = (prompt % 2 == 0) == (phase == 0)
            line = [(other * SIDE + i) if along_x else (i * SIDE + other) for i in range(SIDE)]
            groups.append([prompt * ROLLOUTS + r for r in line])
    return groups


def x_groups():
    return [[row * SIDE + i for i in range(SIDE)] for row in range(PROMPTS * SIDE)]


def exchange(blocks, groups):
    return lax.all_to_all(
        blocks, AXES, split_axis=0, concat_axis=0, axis_index_groups=groups, tiled=True
    )


def exchange_all(blocks):
    return lax.all_to_all(blocks, "rollout", split_axis=0, concat_axis=0, tiled=True)


def shift(value, phase, by):
    pairs = []
    for line in line_groups(phase):
        pairs += [(line[i], line[(i + by) % SIDE]) for i in range(SIDE)]
    return lax.ppermute(value, AXES, pairs)


def split_kernel(w1_ref, out_ref):
    rows = w1_ref[...].astype(F32)
    zeros = jnp.zeros((PART_PAD - PART, HID_OWN), F32)
    for i in range(SIDE):
        part = jnp.concatenate([rows[i * PART : (i + 1) * PART], zeros], axis=0)
        out_ref[i] = part.astype(BF16)


def weights_kernel(w2_ref, w1_ref, out_ref):
    out_ref[0:HID_OWN, :] = w2_ref[...]
    for k in range(SIDE):
        base = HID_OWN + k * PART_PAD
        out_ref[base : base + PART_PAD, :] = w1_ref[k, :, 0:256]
    rest = jnp.concatenate([w1_ref[k, :, 256:HID_OWN] for k in range(SIDE)], axis=1)
    out_ref[HID_OWN + W1_ROWS : W_ROWS, :] = rest


def pack_kernel(count_ref, ids_ref, grads_ref, out_ref, meta):
    live = lax.broadcasted_iota(jnp.int32, (1, SLOTS), 1) < count_ref[0, 0]
    place = jnp.where(live, ids_ref[...] + 1, 0)
    meta[...] = jnp.zeros((8, COLS), F32)
    meta[2:3, 0:SLOTS] = (place >> 4).astype(F32)
    meta[3:4, 0:SLOTS] = (place & 15).astype(F32)
    codes = meta[...]
    zeros = jnp.zeros((8, COLS), F32)
    for k in range(ROLLOUTS):
        cols = pl.ds(k * COLS, COLS)
        out_ref[k, 0:48, :] = grads_ref[0:48, cols]
        two = jnp.concatenate([grads_ref[48:SLOTS, cols].astype(F32), zeros[0:6]], axis=0)
        out_ref[k, 48:64, :] = jnp.concatenate([two + codes, zeros], axis=0).astype(BF16)


def sum_kernel(recv_ref, out_ref):
    rows = (lax.broadcasted_iota(jnp.int32, (ROWS, 4 * PAD_SLOTS), 0) + 1).astype(F32)
    total = jnp.zeros((ROWS, COLS), F32)
    for g in range(ROLLOUTS // 4):
        codes = jnp.zeros((8, 4 * PAD_SLOTS), F32)
        for k in range(4):
            tile = recv_ref[4 * g + k, 48:64, 0 : 4 * PAD_SLOTS].astype(F32)[0:8]
            codes = codes + (pltpu.roll(tile, PAD_SLOTS * k, 1) if k else tile)
        row = codes[2:3] * 16.0 + codes[3:4]
        onehot = jnp.where(rows == row, 1.0, 0.0).astype(BF16)
        block = recv_ref[4 * g : 4 * g + 4].reshape(4 * PAD_SLOTS, COLS)
        total = total + jnp.dot(onehot, block, preferred_element_type=F32)
    value = total.astype(BF16)
    for k in range(SIDE):
        out_ref[k] = value


GATHERED = (
    (0, (0, 1, 2, 3), 0),
    (1, (0, 1), 3),
    (2, (2, 3), 3),
    (3, (2, 3), 1),
    (4, (0, 1), 1),
    (5, (0, 1), 2),
    (6, (2, 3), 2),
)


def act_kernel(w_ref, *refs):
    sums, (slope_ref, act_ref, w2, sems) = refs[:7], refs[7:]
    even = lax.axis_index("prompt") % 2 == 0
    rollout = lax.axis_index("rollout")
    own = jnp.where(even, rollout // SIDE, rollout % SIDE)
    slots, copies = [], []
    for operand, places, offset in GATHERED:
        for n, k in enumerate(places):
            other = lax.rem(own + offset, SIDE)
            block = jnp.where(even, other * SIDE + k, k * SIDE + other)
            i = len(slots)
            pair = [
                pltpu.make_async_copy(
                    w_ref.at[2 * block + h, 0:HID_OWN],
                    w2.at[:, pl.ds((2 * i + h) * W2_COLS, W2_COLS)],
                    sems.at[i, h],
                )
                for h in range(2)
            ]
            for copy in pair:
                copy.start()
            copies.append(pair)
            slots.append((sums[operand], n))
    hidden = None
    for i, (ref, n) in enumerate(slots):
        for copy in copies[i]:
            copy.wait()
        part = dot_t(ref[n], w2[:, i * COLS : (i + 1) * COLS])
        hidden = part if hidden is None else hidden + part
    act = (hidden * slope_ref[...]).astype(BF16)
    for k in range(SIDE):
        act_ref[k] = act


def upstream_kernel(w_ref, act_ref, out_ref, w1, sems):
    copies = []
    for m in range(MERGE):
        prompts = pl.ds(m * 8, 8)
        copies.append(pltpu.make_async_copy(w_ref.at[prompts, HID_OWN:W_ROWS], w1.at[prompts], sems.at[m]))
        copies[m].start()
    rest = jnp.concatenate([act_ref[k, :, 256:HID_OWN] for k in range(SIDE)], axis=1)
    for m in range(MERGE):
        copies[m].wait()
        total = None
        for k in range(SIDE + 1):
            w = w1[8 * m : 8 * m + 8, k * PART_PAD : (k + 1) * PART_PAD].reshape(8 * PART_PAD, 256)
            part = dot_t(act_ref[k, :, 0:256] if k < SIDE else rest, w)
            total = part if total is None else total + part
        blocks = total.reshape(ROLLOUTS, OWN, 8 * PART_PAD).astype(BF16)
        out_ref[:, :, 8 * PART_PAD * m : 8 * PART_PAD * (m + 1)] = blocks


def norm_kernel(recv_ref, order_ref, patches_ref, gain_ref, out_ref):
    parts = []
    for i in range(SIDE):
        total = None
        for s in range(SIDE):
            part = recv_ref[s * SIDE + i].astype(F32)
            total = part if total is None else total + part
        parts.append(total)
    rows = []
    for g in range(2 * MERGE):
        whole = jnp.concatenate([part[:, g * HALF : (g + 1) * HALF] for part in parts], axis=1)
        high = whole.astype(BF16)
        rows += [high, (whole - high.astype(F32)).astype(BF16)]
    ordered = jnp.dot(
        jnp.concatenate([r.astype(F32) for r in rows], axis=0).astype(BF16),
        order_ref[...],
        preferred_element_type=F32,
    )
    for m in range(MERGE):
        halves = []
        for g in (2 * m, 2 * m + 1):
            at = 2 * g * OWN
            halves.append(ordered[at : at + OWN] + ordered[at + OWN : at + 2 * OWN])
        upstream = jnp.concatenate(halves, axis=1)
        cols = slice(m * VIT, (m + 1) * VIT)
        inputs = patches_ref[:, cols].astype(F32)
        scaled = upstream * gain_ref[...]
        inverse = lax.rsqrt(jnp.mean(inputs * inputs, axis=-1, keepdims=True) + 1e-06)
        inner = jnp.mean(scaled * inputs, axis=-1, keepdims=True)
        result = inverse * scaled - inputs * inverse * inverse * inverse * inner
        out_ref[:, cols] = result.astype(BF16)


def call(kernel, shape, in_specs, flops=0, moved=0, vmem=16, scratch=()):
    return pl.pallas_call(
        kernel,
        out_shape=jax.ShapeDtypeStruct(shape, BF16),
        in_specs=in_specs,
        out_specs=VMEM,
        scratch_shapes=list(scratch),
        cost_estimate=pl.CostEstimate(flops=flops, bytes_accessed=moved, transcendentals=0),
        compiler_params=pltpu.CompilerParams(vmem_limit_bytes=vmem << 20),
    )


def column_order():
    lane = lax.broadcasted_iota(jnp.int32, (SIDE * HALF, HALF // PART_PAD * IN_OWN), 0)
    col = lax.broadcasted_iota(jnp.int32, lane.shape, 1)
    place, prompt, row = lane // HALF, lane % HALF // PART_PAD, lane % PART_PAD
    return ((prompt * IN_OWN + place * PART + row == col) & (row < PART)).astype(BF16)


def per_device(row_grads, used_ids, used_count, pre_act, patches, ln_gain, w_fc2, w_fc1):
    w1_part = exchange(call(split_kernel, (SIDE, PART_PAD, HID_OWN), [VMEM])(w_fc1), x_groups())
    weights = call(weights_kernel, (W_ROWS, 256), [VMEM] * 2)(w_fc2, w1_part)
    weights = lax.all_gather(weights, "prompt", axis=0, tiled=False)

    outgoing = call(
        pack_kernel, (ROLLOUTS, PAD_SLOTS, COLS), [SMEM, VMEM, VMEM], scratch=[pltpu.VMEM((8, COLS), F32)]
    )(used_count, used_ids[0], row_grads[0, 0])
    summed = call(sum_kernel, (SIDE, ROWS, COLS), [VMEM])(exchange_all(outgoing))
    line = exchange(summed, line_groups(0))
    a1, b1 = shift(line[:2], 1, 1), shift(line[2:], 1, -1)
    a2, b2 = shift(line[2:], 1, 1), shift(line[:2], 1, -1)
    a3, b3 = shift(a1, 1, 1), shift(b1, 1, -1)

    act = call(
        act_kernel,
        (SIDE, ROWS, HID_OWN),
        [HBM] + [VMEM] * 8,
        flops=1 << 31,
        moved=12 << 20,
        vmem=24,
        scratch=[pltpu.VMEM((HID_OWN, D_LLM), BF16), pltpu.SemaphoreType.DMA((ROLLOUTS, 2))],
    )(weights, line, a1, a2, b1, b2, a3, b3, gelu_slope(pre_act.astype(F32)))
    act_line = exchange(act, x_groups())
    partial = call(
        upstream_kernel,
        (ROLLOUTS, OWN, IN_PAD),
        [HBM, VMEM],
        flops=5 << 28,
        moved=6 << 20,
        vmem=24,
        scratch=[
            pltpu.VMEM((PROMPTS, W_ROWS - HID_OWN, 256), BF16),
            pltpu.SemaphoreType.DMA((MERGE,)),
        ],
    )(weights, act_line)
    return call(norm_kernel, (OWN, HID), [VMEM] * 4)(
        exchange_all(partial), column_order(), patches, ln_gain.reshape(1, VIT)
    )


def solution(mesh):
    return jax.shard_map(
        per_device,
        mesh=mesh,
        in_specs=(
            P("prompt", "rollout", None, None),
            P("prompt", "rollout", None),
            P("prompt", "rollout"),
            P("prompt", "rollout"),
            P(("prompt", "rollout"), None),
            P(),
            P("rollout", "prompt"),
            P("prompt", "rollout"),
        ),
        out_specs=P(("prompt", "rollout"), None),
        check_vma=False,
    )
```

```python
import jax
import jax.numpy as jnp
from jax import lax
from jax.experimental import pallas as pl
from jax.experimental.pallas import tpu as pltpu
from jax.sharding import PartitionSpec as P

VIT = 1280
MERGE = 4
PROMPTS = 32
ROLLOUTS = 16
SIDE = 4
SLOTS = 50
PAD_SLOTS = 64
OWN = 24
ROWS = OWN * ROLLOUTS
D_LLM = 8192
COLS = D_LLM // ROLLOUTS
HID = 5120
HID_OWN = HID // ROLLOUTS
IN_OWN = HID // PROMPTS
W2_COLS = D_LLM // PROMPTS
TAIL = IN_OWN // 2
W_ROWS = HID_OWN + IN_OWN + TAIL
AXES = ("prompt", "rollout")
F32 = jnp.float32
BF16 = jnp.bfloat16


def gelu_slope(value):
    return (
        0.5 * (1.0 + jax.scipy.special.erf(value * 0.7071067811865476))
        + value * jnp.exp(-0.5 * value * value) * 0.3989422804014327
    )


def dot_t(left, right):
    return lax.dot_general(left, right, (((1,), (1,)), ((), ())), preferred_element_type=F32)


def line_groups(phase):
    groups = []
    for prompt in range(PROMPTS):
        for other in range(SIDE):
            along_x = (prompt % 2 == 0) == (phase == 0)
            line = [(other * SIDE + i) if along_x else (i * SIDE + other) for i in range(SIDE)]
            groups.append([prompt * ROLLOUTS + r for r in line])
    return groups


def exchange(blocks, phase):
    return lax.all_to_all(
        blocks, AXES, split_axis=0, concat_axis=0, axis_index_groups=line_groups(phase), tiled=True
    )


def shift(value, phase, by):
    pairs = []
    for line in line_groups(phase):
        pairs += [(line[i], line[(i + by) % SIDE]) for i in range(SIDE)]
    return lax.ppermute(value, AXES, pairs)


def place_in_plane():
    rollout = lax.axis_index("rollout")
    even = lax.axis_index("prompt") % 2 == 0
    return even, jnp.where(even, rollout // SIDE, rollout % SIDE)


def weights_kernel(w2_ref, w1_ref, out_ref):
    out_ref[0:HID_OWN, :] = w2_ref[...]
    out_ref[HID_OWN : HID_OWN + IN_OWN, :] = w1_ref[:, 0:256]
    base = HID_OWN + IN_OWN
    out_ref[base:W_ROWS, :] = jnp.zeros((TAIL, 256), BF16)
    out_ref[base:W_ROWS, 0:64] = w1_ref[0:TAIL, 256:320]
    out_ref[base:W_ROWS, 128:192] = w1_ref[TAIL:IN_OWN, 256:320]


def pack_kernel(count_ref, ids_ref, grads_ref, out_ref, meta):
    even, _ = place_in_plane()
    ids = ids_ref[...]
    owner = (ids * 2731) >> 16
    turned = (owner & 3) * SIDE + (owner >> 2)
    place = jnp.where(even, turned, owner) * OWN + ids - owner * OWN + 1
    live = lax.broadcasted_iota(jnp.int32, (1, SLOTS), 1) < count_ref[0, 0]
    place = jnp.where(live, place, 0)
    meta[...] = jnp.zeros((8, COLS), F32)
    meta[2:3, 0:SLOTS] = (place >> 4).astype(F32)
    meta[3:4, 0:SLOTS] = (place & 15).astype(F32)
    codes = meta[...]
    zeros = jnp.zeros((8, COLS), F32)
    for k in range(ROLLOUTS):
        cols = pl.ds(k * COLS, COLS)
        out_ref[k, 0:48, :] = grads_ref[0:48, cols]
        two = jnp.concatenate([grads_ref[48:SLOTS, cols].astype(F32), zeros[0:6]], axis=0)
        out_ref[k, 48:64, :] = jnp.concatenate([two + codes, zeros], axis=0).astype(BF16)


def sum_kernel(recv_ref, out_ref):
    rows = (lax.broadcasted_iota(jnp.int32, (ROWS, 4 * PAD_SLOTS), 0) + 1).astype(F32)
    total = jnp.zeros((ROWS, COLS), F32)
    for g in range(ROLLOUTS // 4):
        codes = jnp.zeros((8, 4 * PAD_SLOTS), F32)
        for k in range(4):
            tile = recv_ref[4 * g + k, 48:64, 0 : 4 * PAD_SLOTS].astype(F32)[0:8]
            codes = codes + (pltpu.roll(tile, PAD_SLOTS * k, 1) if k else tile)
        row = codes[2:3] * 16.0 + codes[3:4]
        onehot = jnp.where(rows == row, 1.0, 0.0).astype(BF16)
        block = recv_ref[4 * g : 4 * g + 4].reshape(4 * PAD_SLOTS, COLS)
        total = total + jnp.dot(onehot, block, preferred_element_type=F32)
    value = total.astype(BF16)
    for k in range(SIDE):
        out_ref[k] = value


def start_w1(w_ref, w1, sems):
    base = HID_OWN + IN_OWN
    copies = [
        pltpu.make_async_copy(w_ref.at[:, HID_OWN:base], w1.at[:, :, 0:256], sems.at[0]),
        pltpu.make_async_copy(w_ref.at[:, base:W_ROWS, 0:128], w1.at[:, 0:TAIL, 256:384], sems.at[1]),
        pltpu.make_async_copy(w_ref.at[:, base:W_ROWS, 128:256], w1.at[:, TAIL:IN_OWN, 256:384], sems.at[2]),
    ]
    for copy in copies:
        copy.start()
    return copies


def w1_chunk(w1, g, prompts):
    return w1[prompts * g : prompts * (g + 1)].reshape(prompts * IN_OWN, 384)[:, :HID_OWN]


GATHERED = ((0, (0, 1, 2, 3), 0), (1, (0, 1), 3), (2, (2, 3), 3), (3, (2, 3), 1), (4, (0, 1), 1), (5, (0, 1), 2), (6, (2, 3), 2))


def mlp_kernel(w_ref, *refs):
    sums, (slope_ref, out_ref, w2, w1, sems2, sems1) = refs[:7], refs[7:]
    even, second = place_in_plane()
    slots, copies = [], []
    for operand, places, offset in GATHERED:
        for n, k in enumerate(places):
            s = lax.rem(second + offset, SIDE)
            block = jnp.where(even, s * SIDE + k, k * SIDE + s)
            i = len(slots)
            pair = [
                pltpu.make_async_copy(
                    w_ref.at[2 * block + h, 0:HID_OWN],
                    w2.at[:, pl.ds((2 * i + h) * W2_COLS, W2_COLS)],
                    sems2.at[i, h],
                )
                for h in range(2)
            ]
            for copy in pair:
                copy.start()
            copies.append(pair)
            slots.append((sums[operand], n))
    late = start_w1(w_ref, w1, sems1)
    hidden = None
    for i, (ref, n) in enumerate(slots):
        for copy in copies[i]:
            copy.wait()
        part = dot_t(ref[n], w2[:, i * COLS : (i + 1) * COLS])
        hidden = part if hidden is None else hidden + part
    act = (hidden * slope_ref[...]).astype(BF16)
    for copy in late:
        copy.wait()
    for g in range(8):
        out_ref[:, 640 * g : 640 * (g + 1)] = dot_t(act, w1_chunk(w1, g, 4)).astype(BF16)


def add_kernel(recv_ref, out_ref):
    total = recv_ref[0].astype(F32)
    for k in range(1, SIDE):
        total = total + recv_ref[k].astype(F32)
    out_ref[...] = total.astype(BF16)


def norm_kernel(recv_ref, patches_ref, gain_ref, out_ref):
    for m in range(MERGE):
        cols = slice(m * VIT, (m + 1) * VIT)
        upstream = recv_ref[0, :, cols].astype(F32)
        for k in range(1, SIDE):
            upstream = upstream + recv_ref[k, :, cols].astype(F32)
        inputs = patches_ref[:, cols].astype(F32)
        scaled = upstream * gain_ref[...]
        inverse = lax.rsqrt(jnp.mean(inputs * inputs, axis=-1, keepdims=True) + 1e-06)
        inner = jnp.mean(scaled * inputs, axis=-1, keepdims=True)
        result = inverse * scaled - inputs * inverse * inverse * inverse * inner
        out_ref[:, cols] = result.astype(BF16)


VMEM = pl.BlockSpec(memory_space=pltpu.VMEM)
SMEM = pl.BlockSpec(memory_space=pltpu.SMEM)
ANY = pl.BlockSpec(memory_space=pl.ANY)


def call(kernel, shape, in_specs, flops=0, moved=0, vmem=16, scratch=()):
    return pl.pallas_call(
        kernel,
        out_shape=jax.ShapeDtypeStruct(shape, BF16),
        in_specs=in_specs,
        out_specs=VMEM,
        scratch_shapes=list(scratch),
        cost_estimate=pl.CostEstimate(flops=flops, bytes_accessed=moved, transcendentals=0),
        compiler_params=pltpu.CompilerParams(vmem_limit_bytes=vmem << 20),
    )


def per_device(row_grads, used_ids, used_count, pre_act, patches, ln_gain, w_fc2, w_fc1):
    weights = call(weights_kernel, (W_ROWS, 256), [VMEM] * 2)(w_fc2, w_fc1)
    weights = lax.all_gather(weights, "prompt", axis=0, tiled=False)

    outgoing = call(
        pack_kernel, (ROLLOUTS, PAD_SLOTS, COLS), [SMEM, VMEM, VMEM], scratch=[pltpu.VMEM((8, COLS), F32)]
    )(used_count, used_ids[0], row_grads[0, 0])
    received = lax.all_to_all(outgoing, "rollout", split_axis=0, concat_axis=0, tiled=True)
    summed = call(sum_kernel, (SIDE, ROWS, COLS), [VMEM])(received)
    line = exchange(summed, 0)
    a1, b1 = shift(line[:2], 1, 1), shift(line[2:], 1, -1)
    a2, b2 = shift(line[2:], 1, 1), shift(line[:2], 1, -1)
    a3, b3 = shift(a1, 1, 1), shift(b1, 1, -1)

    even = lax.axis_index("prompt") % 2 == 0
    slope = gelu_slope(pre_act.astype(F32)).reshape(SIDE, SIDE, OWN, HID_OWN)
    slope = jnp.where(even, slope.transpose(1, 0, 2, 3), slope).reshape(ROWS, HID_OWN)
    partial = call(
        mlp_kernel,
        (ROWS, HID),
        [ANY] + [VMEM] * 8,
        flops=3 << 30,
        moved=16 << 20,
        vmem=50,
        scratch=[
            pltpu.VMEM((HID_OWN, D_LLM), BF16),
            pltpu.VMEM((PROMPTS, IN_OWN, 384), BF16),
            pltpu.SemaphoreType.DMA((ROLLOUTS, 2)),
            pltpu.SemaphoreType.DMA((3,)),
        ],
    )(weights, line, a1, a2, b1, b2, a3, b3, slope)

    halfway = exchange(partial.reshape(SIDE, SIDE * OWN, HID), 0)
    halfway = call(add_kernel, (SIDE * OWN, HID), [VMEM], moved=5 << 20)(halfway)
    last = exchange(halfway.reshape(SIDE, OWN, HID), 1)
    return call(norm_kernel, (OWN, HID), [VMEM] * 3)(last, patches, ln_gain.reshape(1, VIT))


def solution(mesh):
    return jax.shard_map(
        per_device,
        mesh=mesh,
        in_specs=(
            P("prompt", "rollout", None, None),
            P("prompt", "rollout", None),
            P("prompt", "rollout"),
            P("prompt", "rollout"),
            P(("prompt", "rollout"), None),
            P(),
            P("rollout", "prompt"),
            P("prompt", "rollout"),
        ),
        out_specs=P(("prompt", "rollout"), None),
        check_vma=False,
    )
```

```python
import jax
import jax.numpy as jnp
from jax import lax
from jax.experimental import pallas as pl
from jax.experimental.pallas import tpu as pltpu
from jax.sharding import PartitionSpec as P

VIT = 1280
MERGE = 4
PROMPTS = 32
ROLLOUTS = 16
SIDE = 4
SLOTS = 50
PAD_SLOTS = 64
OWN = 24
ROWS = OWN * ROLLOUTS
D_LLM = 8192
COLS = D_LLM // ROLLOUTS
HID = 5120
HID_OWN = HID // ROLLOUTS
IN_OWN = HID // PROMPTS
W2_COLS = D_LLM // PROMPTS
PART = IN_OWN // 2
TAIL = 48
W_ROWS = HID_OWN + 2 * PART + TAIL
IN_PART = HID // 2
RUN = 4 * PART
AXES = ("prompt", "rollout")
F32 = jnp.float32
BF16 = jnp.bfloat16
VMEM = pl.BlockSpec(memory_space=pltpu.VMEM)
SMEM = pl.BlockSpec(memory_space=pltpu.SMEM)
ANY = pl.BlockSpec(memory_space=pl.ANY)


def gelu_slope(value):
    return (
        0.5 * (1.0 + jax.scipy.special.erf(value * 0.7071067811865476))
        + value * jnp.exp(-0.5 * value * value) * 0.3989422804014327
    )


def dot_t(left, right):
    return lax.dot_general(left, right, (((1,), (1,)), ((), ())), preferred_element_type=F32)


def line_groups(phase):
    groups = []
    for prompt in range(PROMPTS):
        for other in range(SIDE):
            along_x = (prompt % 2 == 0) == (phase == 0)
            line = [(other * SIDE + i) if along_x else (i * SIDE + other) for i in range(SIDE)]
            groups.append([prompt * ROLLOUTS + r for r in line])
    return groups


def exchange(blocks, groups):
    return lax.all_to_all(
        blocks, AXES, split_axis=0, concat_axis=0, axis_index_groups=groups, tiled=True
    )


def exchange_all(blocks):
    return lax.all_to_all(blocks, "rollout", split_axis=0, concat_axis=0, tiled=True)


def shift(value, phase, by):
    pairs = []
    for line in line_groups(phase):
        pairs += [(line[i], line[(i + by) % SIDE]) for i in range(SIDE)]
    return lax.ppermute(value, AXES, pairs)


def swap(value):
    return lax.ppermute(value, "rollout", [(r, r ^ 1) for r in range(ROLLOUTS)])


def weights_kernel(w2_ref, mine_ref, theirs_ref, out_ref):
    odd = lax.axis_index("rollout") % 2 == 1
    out_ref[0:HID_OWN, :] = w2_ref[...]
    mine = jnp.where(odd, mine_ref[PART:IN_OWN].astype(F32), mine_ref[0:PART].astype(F32))
    theirs = theirs_ref[...].astype(F32)
    left = jnp.where(odd, theirs, mine).astype(BF16)
    right = jnp.where(odd, mine, theirs).astype(BF16)
    base = HID_OWN + PART
    out_ref[HID_OWN:base, :] = left[:, 0:256]
    out_ref[base : base + PART, :] = right[:, 0:256]
    rest = jnp.concatenate([left[:, 256:HID_OWN], right[:, 256:HID_OWN]], axis=1)
    out_ref[base + PART : W_ROWS, 0:128] = rest[0:TAIL]
    low = jnp.concatenate([rest[TAIL:PART], jnp.zeros((2 * TAIL - PART, 128), BF16)], axis=0)
    out_ref[base + PART : W_ROWS, 128:256] = low


def pack_kernel(count_ref, ids_ref, grads_ref, out_ref, meta):
    live = lax.broadcasted_iota(jnp.int32, (1, SLOTS), 1) < count_ref[0, 0]
    place = jnp.where(live, ids_ref[...] + 1, 0)
    meta[...] = jnp.zeros((8, COLS), F32)
    meta[2:3, 0:SLOTS] = (place >> 4).astype(F32)
    meta[3:4, 0:SLOTS] = (place & 15).astype(F32)
    codes = meta[...]
    zeros = jnp.zeros((8, COLS), F32)
    for k in range(ROLLOUTS):
        cols = pl.ds(k * COLS, COLS)
        out_ref[k, 0:48, :] = grads_ref[0:48, cols]
        two = jnp.concatenate([grads_ref[48:SLOTS, cols].astype(F32), zeros[0:6]], axis=0)
        out_ref[k, 48:64, :] = jnp.concatenate([two + codes, zeros], axis=0).astype(BF16)


def sum_kernel(recv_ref, out_ref):
    rows = (lax.broadcasted_iota(jnp.int32, (ROWS, 4 * PAD_SLOTS), 0) + 1).astype(F32)
    total = jnp.zeros((ROWS, COLS), F32)
    for g in range(ROLLOUTS // 4):
        codes = jnp.zeros((8, 4 * PAD_SLOTS), F32)
        for k in range(4):
            tile = recv_ref[4 * g + k, 48:64, 0 : 4 * PAD_SLOTS].astype(F32)[0:8]
            codes = codes + (pltpu.roll(tile, PAD_SLOTS * k, 1) if k else tile)
        row = codes[2:3] * 16.0 + codes[3:4]
        onehot = jnp.where(rows == row, 1.0, 0.0).astype(BF16)
        block = recv_ref[4 * g : 4 * g + 4].reshape(4 * PAD_SLOTS, COLS)
        total = total + jnp.dot(onehot, block, preferred_element_type=F32)
    value = total.astype(BF16)
    for k in range(SIDE):
        out_ref[k] = value


GATHERED = (
    (0, (0, 1, 2, 3), 0),
    (1, (0, 1), 3),
    (2, (2, 3), 3),
    (3, (2, 3), 1),
    (4, (0, 1), 1),
    (5, (0, 1), 2),
    (6, (2, 3), 2),
)


def act_kernel(w_ref, *refs):
    sums, (slope_ref, act_ref, w2, sems) = refs[:7], refs[7:]
    even = lax.axis_index("prompt") % 2 == 0
    rollout = lax.axis_index("rollout")
    own = jnp.where(even, rollout // SIDE, rollout % SIDE)
    slots, copies = [], []
    for operand, places, offset in GATHERED:
        for n, k in enumerate(places):
            other = lax.rem(own + offset, SIDE)
            block = jnp.where(even, other * SIDE + k, k * SIDE + other)
            i = len(slots)
            pair = [
                pltpu.make_async_copy(
                    w_ref.at[2 * block + h, 0:HID_OWN],
                    w2.at[:, pl.ds((2 * i + h) * W2_COLS, W2_COLS)],
                    sems.at[i, h],
                )
                for h in range(2)
            ]
            for copy in pair:
                copy.start()
            copies.append(pair)
            slots.append((sums[operand], n))
    hidden = None
    for i, (ref, n) in enumerate(slots):
        for copy in copies[i]:
            copy.wait()
        part = dot_t(ref[n], w2[:, i * COLS : (i + 1) * COLS])
        hidden = part if hidden is None else hidden + part
    act_ref[...] = (hidden * slope_ref[...]).astype(BF16)


def upstream_kernel(w_ref, mine_ref, theirs_ref, out_ref, w1, sems):
    copies = []
    for m in range(MERGE):
        prompts = pl.ds(m * 8, 8)
        copies.append(pltpu.make_async_copy(w_ref.at[prompts, HID_OWN:W_ROWS], w1.at[prompts], sems.at[m]))
        copies[m].start()
    odd = lax.axis_index("rollout") % 2 == 1
    mine, theirs = mine_ref[...], theirs_ref[...]
    left, right = jnp.where(odd, theirs, mine), jnp.where(odd, mine, theirs)
    rest = jnp.concatenate([left[:, 256:HID_OWN], right[:, 256:HID_OWN]], axis=1)
    for m in range(MERGE):
        copies[m].wait()
        w = w1[8 * m : 8 * m + 8]
        fold = w[:, 2 * PART :]
        tail = jnp.concatenate([fold[:, :, 0:128], fold[:, 0 : PART - TAIL, 128:256]], axis=1)
        total = dot_t(left[:, 0:256], w[:, 0:PART].reshape(8 * PART, 256))
        total = total + dot_t(right[:, 0:256], w[:, PART : 2 * PART].reshape(8 * PART, 256))
        total = total + dot_t(rest, tail.reshape(8 * PART, 128))
        blocks = total.reshape(ROLLOUTS, OWN, 8 * PART).astype(BF16)
        out_ref[:, :, 8 * PART * m : 8 * PART * (m + 1)] = blocks


def norm_kernel(recv_ref, order_ref, patches_ref, gain_ref, out_ref):
    parts = []
    for i in range(2):
        total = None
        for s in range(ROLLOUTS // 2):
            part = recv_ref[2 * s + i].astype(F32)
            total = part if total is None else total + part
        parts.append(total)
    rows = []
    for g in range(2 * MERGE):
        whole = jnp.concatenate([part[:, g * RUN : (g + 1) * RUN] for part in parts], axis=1)
        high = whole.astype(BF16)
        rows += [high, (whole - high.astype(F32)).astype(BF16)]
    ordered = jnp.dot(
        jnp.concatenate([r.astype(F32) for r in rows], axis=0).astype(BF16),
        order_ref[...],
        preferred_element_type=F32,
    )
    for m in range(MERGE):
        halves = []
        for g in (2 * m, 2 * m + 1):
            at = 2 * g * OWN
            halves.append(ordered[at : at + OWN] + ordered[at + OWN : at + 2 * OWN])
        upstream = jnp.concatenate(halves, axis=1)
        cols = slice(m * VIT, (m + 1) * VIT)
        inputs = patches_ref[:, cols].astype(F32)
        scaled = upstream * gain_ref[...]
        inverse = lax.rsqrt(jnp.mean(inputs * inputs, axis=-1, keepdims=True) + 1e-06)
        inner = jnp.mean(scaled * inputs, axis=-1, keepdims=True)
        result = inverse * scaled - inputs * inverse * inverse * inverse * inner
        out_ref[:, cols] = result.astype(BF16)


def call(kernel, shape, in_specs, flops=0, moved=0, vmem=16, scratch=()):
    return pl.pallas_call(
        kernel,
        out_shape=jax.ShapeDtypeStruct(shape, BF16),
        in_specs=in_specs,
        out_specs=VMEM,
        scratch_shapes=list(scratch),
        cost_estimate=pl.CostEstimate(flops=flops, bytes_accessed=moved, transcendentals=0),
        compiler_params=pltpu.CompilerParams(vmem_limit_bytes=vmem << 20),
    )


def column_order():
    lane = lax.broadcasted_iota(jnp.int32, (2 * RUN, 2 * RUN), 0)
    col = lax.broadcasted_iota(jnp.int32, lane.shape, 1)
    side, prompt, row = lane // RUN, lane % RUN // PART, lane % PART
    return (prompt * IN_OWN + side * PART + row == col).astype(BF16)


def per_device(row_grads, used_ids, used_count, pre_act, patches, ln_gain, w_fc2, w_fc1):
    odd = lax.axis_index("rollout") % 2 == 1
    theirs = swap(jnp.where(odd, w_fc1[:PART], w_fc1[PART:]))
    weights = call(weights_kernel, (W_ROWS, 256), [VMEM] * 3)(w_fc2, w_fc1, theirs)
    weights = lax.all_gather(weights, "prompt", axis=0, tiled=False)

    outgoing = call(
        pack_kernel, (ROLLOUTS, PAD_SLOTS, COLS), [SMEM, VMEM, VMEM], scratch=[pltpu.VMEM((8, COLS), F32)]
    )(used_count, used_ids[0], row_grads[0, 0])
    summed = call(sum_kernel, (SIDE, ROWS, COLS), [VMEM])(exchange_all(outgoing))
    line = exchange(summed, line_groups(0))
    a1, b1 = shift(line[:2], 1, 1), shift(line[2:], 1, -1)
    a2, b2 = shift(line[2:], 1, 1), shift(line[:2], 1, -1)
    a3, b3 = shift(a1, 1, 1), shift(b1, 1, -1)

    act = call(
        act_kernel,
        (ROWS, HID_OWN),
        [ANY] + [VMEM] * 8,
        flops=1 << 31,
        moved=12 << 20,
        vmem=50,
        scratch=[pltpu.VMEM((HID_OWN, D_LLM), BF16), pltpu.SemaphoreType.DMA((ROLLOUTS, 2))],
    )(weights, line, a1, a2, b1, b2, a3, b3, gelu_slope(pre_act.astype(F32)))
    partial = call(
        upstream_kernel,
        (ROLLOUTS, OWN, IN_PART),
        [ANY, VMEM, VMEM],
        flops=5 << 28,
        moved=6 << 20,
        vmem=56,
        scratch=[
            pltpu.VMEM((PROMPTS, W_ROWS - HID_OWN, 256), BF16),
            pltpu.SemaphoreType.DMA((MERGE,)),
        ],
    )(weights, act, swap(act))
    return call(norm_kernel, (OWN, HID), [VMEM] * 4)(
        exchange_all(partial), column_order(), patches, ln_gain.reshape(1, VIT)
    )


def solution(mesh):
    return jax.shard_map(
        per_device,
        mesh=mesh,
        in_specs=(
            P("prompt", "rollout", None, None),
            P("prompt", "rollout", None),
            P("prompt", "rollout"),
            P("prompt", "rollout"),
            P(("prompt", "rollout"), None),
            P(),
            P("rollout", "prompt"),
            P("prompt", "rollout"),
        ),
        out_specs=P(("prompt", "rollout"), None),
        check_vma=False,
    )
```

```python
import jax
import jax.numpy as jnp
from jax import lax
from jax.experimental import pallas as pl
from jax.experimental.pallas import tpu as pltpu
from jax.sharding import PartitionSpec as P

VIT = 1280
MERGE = 4
PROMPTS = 32
ROLLOUTS = 16
SIDE = 4
SLOTS = 50
PAD_SLOTS = 64
OWN = 24
ROWS = OWN * ROLLOUTS
D_LLM = 8192
COLS = D_LLM // ROLLOUTS
HID = 5120
HID_OWN = HID // ROLLOUTS
IN_OWN = HID // PROMPTS
W2_COLS = D_LLM // PROMPTS
TAIL = IN_OWN // 2
W_ROWS = HID_OWN + IN_OWN + TAIL
AXES = ("prompt", "rollout")
F32 = jnp.float32
BF16 = jnp.bfloat16


def gelu_slope(value):
    return (
        0.5 * (1.0 + jax.scipy.special.erf(value * 0.7071067811865476))
        + value * jnp.exp(-0.5 * value * value) * 0.3989422804014327
    )


def dot_t(left, right):
    return lax.dot_general(left, right, (((1,), (1,)), ((), ())), preferred_element_type=F32)


def line_groups(phase):
    groups = []
    for prompt in range(PROMPTS):
        for other in range(SIDE):
            along_x = (prompt % 2 == 0) == (phase == 0)
            line = [(other * SIDE + i) if along_x else (i * SIDE + other) for i in range(SIDE)]
            groups.append([prompt * ROLLOUTS + r for r in line])
    return groups


def exchange(blocks, phase):
    return lax.all_to_all(
        blocks, AXES, split_axis=0, concat_axis=0, axis_index_groups=line_groups(phase), tiled=True
    )


def shift(value, phase, by):
    pairs = []
    for line in line_groups(phase):
        pairs += [(line[i], line[(i + by) % SIDE]) for i in range(SIDE)]
    return lax.ppermute(value, AXES, pairs)


def place_in_plane():
    rollout = lax.axis_index("rollout")
    even = lax.axis_index("prompt") % 2 == 0
    y, x = rollout // SIDE, rollout % SIDE
    return even, jnp.where(even, x, y), jnp.where(even, y, x)


def weights_kernel(w2_ref, w1_ref, out_ref):
    out_ref[0:HID_OWN, :] = w2_ref[...]
    out_ref[HID_OWN : HID_OWN + IN_OWN, :] = w1_ref[:, 0:256]
    base = HID_OWN + IN_OWN
    out_ref[base:W_ROWS, :] = jnp.zeros((TAIL, 256), BF16)
    out_ref[base:W_ROWS, 0:64] = w1_ref[0:TAIL, 256:320]
    out_ref[base:W_ROWS, 128:192] = w1_ref[TAIL:IN_OWN, 256:320]


def pack_kernel(count_ref, ids_ref, grads_ref, out_ref, meta):
    even, _, _ = place_in_plane()
    ids = ids_ref[...]
    owner = (ids * 2731) >> 16
    turned = (owner & 3) * SIDE + (owner >> 2)
    place = jnp.where(even, turned, owner) * OWN + ids - owner * OWN + 1
    live = lax.broadcasted_iota(jnp.int32, (1, SLOTS), 1) < count_ref[0, 0]
    place = jnp.where(live, place, 0)
    meta[...] = jnp.zeros((8, COLS), F32)
    meta[2:3, 0:SLOTS] = (place >> 4).astype(F32)
    meta[3:4, 0:SLOTS] = (place & 15).astype(F32)
    codes = meta[...]
    zeros = jnp.zeros((8, COLS), F32)
    for k in range(ROLLOUTS):
        cols = pl.ds(k * COLS, COLS)
        out_ref[k, 0:48, :] = grads_ref[0:48, cols]
        two = jnp.concatenate([grads_ref[48:SLOTS, cols].astype(F32), zeros[0:6]], axis=0)
        out_ref[k, 48:64, :] = jnp.concatenate([two + codes, zeros], axis=0).astype(BF16)


def sum_kernel(recv_ref, out_ref):
    rows = (lax.broadcasted_iota(jnp.int32, (ROWS, 4 * PAD_SLOTS), 0) + 1).astype(F32)
    total = jnp.zeros((ROWS, COLS), F32)
    for g in range(ROLLOUTS // 4):
        codes = jnp.zeros((8, 4 * PAD_SLOTS), F32)
        for k in range(4):
            tile = recv_ref[4 * g + k, 48:64, 0 : 4 * PAD_SLOTS].astype(F32)[0:8]
            codes = codes + (pltpu.roll(tile, PAD_SLOTS * k, 1) if k else tile)
        row = codes[2:3] * 16.0 + codes[3:4]
        onehot = jnp.where(rows == row, 1.0, 0.0).astype(BF16)
        block = recv_ref[4 * g : 4 * g + 4].reshape(4 * PAD_SLOTS, COLS)
        total = total + jnp.dot(onehot, block, preferred_element_type=F32)
    value = total.astype(BF16)
    for k in range(SIDE):
        out_ref[k] = value


def start_w1(w_ref, w1, sems):
    base = HID_OWN + IN_OWN
    quarters = []
    for q in range(SIDE):
        copies = [
            pltpu.make_async_copy(w_ref.at[q, :, :, HID_OWN:base], w1.at[q, :, :, :, 0:256], sems.at[q, 0]),
            pltpu.make_async_copy(
                w_ref.at[q, :, :, base:W_ROWS, 0:128], w1.at[q, :, :, 0:TAIL, 256:384], sems.at[q, 1]
            ),
            pltpu.make_async_copy(
                w_ref.at[q, :, :, base:W_ROWS, 128:256], w1.at[q, :, :, TAIL:IN_OWN, 256:384], sems.at[q, 2]
            ),
        ]
        for copy in copies:
            copy.start()
        quarters.append(copies)
    return quarters


def w1_chunks(w1, quarters):
    for q in range(SIDE):
        for copy in quarters[q]:
            copy.wait()
        for h in range(2):
            rows = w1[q, 2 * h : 2 * h + 2].reshape(4 * IN_OWN, 384)[:, :HID_OWN]
            at = (2 * q + h) * 4 * IN_OWN
            yield slice(at, at + 4 * IN_OWN), rows


GATHERED = (
    (0, ((0, 0), (0, 1), (0, 2), (0, 3))),
    (3, ((1, 0), (1, 1), (2, 0), (2, 1))),
    (1, ((4, 0), (4, 1), (3, 0), (3, 1))),
    (2, ((5, 0), (5, 1), (6, 0), (6, 1))),
)


def act_kernel(w_ref, *refs):
    sums, (slope_ref, act_ref, far_ref, w2, w1, sems2, sems1) = refs[:7], refs[7:]
    even, first, second = place_in_plane()
    copies = []
    for n, (offset, _) in enumerate(GATHERED):
        other = lax.rem(second + offset, SIDE)
        by_row = pltpu.make_async_copy(w_ref.at[other, :, :, 0:HID_OWN], w2.at[n], sems2.at[n])
        by_col = pltpu.make_async_copy(w_ref.at[:, other, :, 0:HID_OWN], w2.at[n], sems2.at[n])
        pl.when(even)(by_row.start)
        pl.when(jnp.logical_not(even))(by_col.start)
        copies.append(by_row)
    quarters = start_w1(w_ref, w1, sems1)
    hidden = None
    for n, (_, blocks) in enumerate(GATHERED):
        copies[n].wait()
        for k, (operand, index) in enumerate(blocks):
            block = sums[operand][index]
            part = dot_t(block[:, :W2_COLS], w2[n, k, 0]) + dot_t(block[:, W2_COLS:], w2[n, k, 1])
            hidden = part if hidden is None else hidden + part
    act_ref[...] = (hidden * slope_ref[...]).astype(BF16)
    far = lax.rem(first + 2, SIDE)
    rows = act_ref[pl.ds(pl.multiple_of(far * 96, 96), 96), :]
    for cols, w in w1_chunks(w1, quarters):
        far_ref[:, cols] = dot_t(rows, w).astype(BF16)


def rest_kernel(w_ref, act_ref, right_ref, left_ref, own_ref, w1, sems1):
    _, first, _ = place_in_plane()
    quarters = start_w1(w_ref, w1, sems1)
    blocks = [
        act_ref[pl.ds(pl.multiple_of(lax.rem(first + by, SIDE) * 96, 96), 96), :] for by in (1, 3, 0)
    ]
    rows = jnp.concatenate(blocks, axis=0)
    for cols, w in w1_chunks(w1, quarters):
        part = dot_t(rows, w).astype(BF16)
        right_ref[:, cols] = part[0:96]
        left_ref[:, cols] = part[96:192]
        own_ref[:, cols] = part[192:288]


def join_kernel(own_ref, a_ref, b_ref, c_ref, out_ref):
    total = own_ref[...].astype(F32) + a_ref[...].astype(F32)
    total = total + b_ref[...].astype(F32) + c_ref[...].astype(F32)
    out_ref[...] = total.astype(BF16)


def norm_kernel(recv_ref, patches_ref, gain_ref, out_ref):
    for m in range(MERGE):
        cols = slice(m * VIT, (m + 1) * VIT)
        upstream = recv_ref[0, :, cols].astype(F32)
        for k in range(1, SIDE):
            upstream = upstream + recv_ref[k, :, cols].astype(F32)
        inputs = patches_ref[:, cols].astype(F32)
        scaled = upstream * gain_ref[...]
        inverse = lax.rsqrt(jnp.mean(inputs * inputs, axis=-1, keepdims=True) + 1e-06)
        inner = jnp.mean(scaled * inputs, axis=-1, keepdims=True)
        result = inverse * scaled - inputs * inverse * inverse * inverse * inner
        out_ref[:, cols] = result.astype(BF16)


VMEM = pl.BlockSpec(memory_space=pltpu.VMEM)
SMEM = pl.BlockSpec(memory_space=pltpu.SMEM)
ANY = pl.BlockSpec(memory_space=pl.ANY)


def call(kernel, shapes, in_specs, flops=0, moved=0, vmem=16, scratch=()):
    one = not isinstance(shapes[0], tuple)
    shapes = (shapes,) if one else shapes
    run = pl.pallas_call(
        kernel,
        out_shape=[jax.ShapeDtypeStruct(shape, BF16) for shape in shapes],
        in_specs=in_specs,
        out_specs=[VMEM] * len(shapes),
        scratch_shapes=list(scratch),
        cost_estimate=pl.CostEstimate(flops=flops, bytes_accessed=moved, transcendentals=0),
        compiler_params=pltpu.CompilerParams(vmem_limit_bytes=vmem << 20),
    )
    return (lambda *args: run(*args)[0]) if one else run


def per_device(row_grads, used_ids, used_count, pre_act, patches, ln_gain, w_fc2, w_fc1):
    weights = call(weights_kernel, (W_ROWS, 256), [VMEM] * 2)(w_fc2, w_fc1)
    weights = lax.all_gather(weights, "prompt", axis=0, tiled=False)

    outgoing = call(
        pack_kernel, (ROLLOUTS, PAD_SLOTS, COLS), [SMEM, VMEM, VMEM], scratch=[pltpu.VMEM((8, COLS), F32)]
    )(used_count, used_ids[0], row_grads[0, 0])
    received = lax.all_to_all(outgoing, "rollout", split_axis=0, concat_axis=0, tiled=True)
    summed = call(sum_kernel, (SIDE, ROWS, COLS), [VMEM])(received)
    line = exchange(summed, 0)
    a1, b1 = shift(line[:2], 1, 1), shift(line[2:], 1, -1)
    a2, b2 = shift(line[2:], 1, 1), shift(line[:2], 1, -1)
    a3, b3 = shift(a1, 1, 1), shift(b1, 1, -1)

    even = lax.axis_index("prompt") % 2 == 0
    slope = gelu_slope(pre_act.astype(F32)).reshape(SIDE, SIDE, OWN, HID_OWN)
    slope = jnp.where(even, slope.transpose(1, 0, 2, 3), slope).reshape(ROWS, HID_OWN)
    weights = weights.reshape(SIDE, SIDE, 2, W_ROWS, 256)
    w1_scratch = [pltpu.VMEM((SIDE, SIDE, 2, IN_OWN, 384), BF16), pltpu.SemaphoreType.DMA((SIDE, 3))]
    act, far = call(
        act_kernel,
        ((ROWS, HID_OWN), (96, HID)),
        [ANY] + [VMEM] * 8,
        flops=5 << 29,
        moved=12 << 20,
        vmem=50,
        scratch=[
            pltpu.VMEM((SIDE, SIDE, 2, HID_OWN, W2_COLS), BF16),
            w1_scratch[0],
            pltpu.SemaphoreType.DMA((SIDE,)),
            w1_scratch[1],
        ],
    )(weights, line, a1, a2, b1, b2, a3, b3, slope)

    from_far = shift(far, 0, 2)
    right, left, own = call(
        rest_kernel, ((96, HID),) * 3, [ANY, VMEM], flops=1 << 30, moved=8 << 20, vmem=54, scratch=w1_scratch
    )(weights, act)
    right, left, from_far = lax.optimization_barrier((right, left, from_far))
    from_left, from_right = shift(right, 0, 1), shift(left, 0, -1)
    halfway = call(join_kernel, (96, HID), [VMEM] * 4)(own, from_far, from_left, from_right)
    last = exchange(halfway.reshape(SIDE, OWN, HID), 1)
    return call(norm_kernel, (OWN, HID), [VMEM] * 3)(last, patches, ln_gain.reshape(1, VIT))


def solution(mesh):
    return jax.shard_map(
        per_device,
        mesh=mesh,
        in_specs=(
            P("prompt", "rollout", None, None),
            P("prompt", "rollout", None),
            P("prompt", "rollout"),
            P("prompt", "rollout"),
            P(("prompt", "rollout"), None),
            P(),
            P("rollout", "prompt"),
            P("prompt", "rollout"),
        ),
        out_specs=P(("prompt", "rollout"), None),
        check_vma=False,
    )
```

```python
import jax
import jax.numpy as jnp
from jax import lax
from jax.experimental import pallas as pl
from jax.experimental.pallas import tpu as pltpu
from jax.sharding import PartitionSpec as P

VIT = 1280
MERGE = 4
PROMPTS = 32
ROLLOUTS = 16
SIDE = 4
SLOTS = 50
PAD_SLOTS = 64
OWN = 24
ROWS = OWN * ROLLOUTS
D_LLM = 8192
COLS = D_LLM // ROLLOUTS
HID = 5120
HID_OWN = HID // ROLLOUTS
IN_OWN = HID // PROMPTS
W2_COLS = D_LLM // PROMPTS
TAIL = IN_OWN // 2
W_ROWS = HID_OWN + IN_OWN + TAIL
AXES = ("prompt", "rollout")
F32 = jnp.float32
BF16 = jnp.bfloat16


def gelu_slope(value):
    return (
        0.5 * (1.0 + jax.scipy.special.erf(value * 0.7071067811865476))
        + value * jnp.exp(-0.5 * value * value) * 0.3989422804014327
    )


def dot_t(left, right):
    return lax.dot_general(left, right, (((1,), (1,)), ((), ())), preferred_element_type=F32)


def line_groups(phase):
    groups = []
    for prompt in range(PROMPTS):
        for other in range(SIDE):
            along_x = (prompt % 2 == 0) == (phase == 0)
            line = [(other * SIDE + i) if along_x else (i * SIDE + other) for i in range(SIDE)]
            groups.append([prompt * ROLLOUTS + r for r in line])
    return groups


def exchange(blocks, phase):
    return lax.all_to_all(
        blocks, AXES, split_axis=0, concat_axis=0, axis_index_groups=line_groups(phase), tiled=True
    )


def shift(value, phase, by):
    pairs = []
    for line in line_groups(phase):
        pairs += [(line[i], line[(i + by) % SIDE]) for i in range(SIDE)]
    return lax.ppermute(value, AXES, pairs)


def place_in_plane():
    rollout = lax.axis_index("rollout")
    even = lax.axis_index("prompt") % 2 == 0
    return even, jnp.where(even, rollout // SIDE, rollout % SIDE)


def weights_kernel(w2_ref, w1_ref, out_ref):
    out_ref[0:HID_OWN, :] = w2_ref[...]
    out_ref[HID_OWN : HID_OWN + IN_OWN, :] = w1_ref[:, 0:256]
    base = HID_OWN + IN_OWN
    out_ref[base:W_ROWS, :] = jnp.zeros((TAIL, 256), BF16)
    out_ref[base:W_ROWS, 0:64] = w1_ref[0:TAIL, 256:320]
    out_ref[base:W_ROWS, 128:192] = w1_ref[TAIL:IN_OWN, 256:320]


def pack_kernel(count_ref, ids_ref, grads_ref, out_ref, meta):
    even, _ = place_in_plane()
    ids = ids_ref[...]
    owner = (ids * 2731) >> 16
    turned = (owner & 3) * SIDE + (owner >> 2)
    place = jnp.where(even, turned, owner) * OWN + ids - owner * OWN + 1
    live = lax.broadcasted_iota(jnp.int32, (1, SLOTS), 1) < count_ref[0, 0]
    place = jnp.where(live, place, 0)
    meta[...] = jnp.zeros((8, COLS), F32)
    meta[2:3, 0:SLOTS] = (place >> 4).astype(F32)
    meta[3:4, 0:SLOTS] = (place & 15).astype(F32)
    codes = meta[...]
    zeros = jnp.zeros((8, COLS), F32)
    for k in range(ROLLOUTS):
        cols = pl.ds(k * COLS, COLS)
        out_ref[k, 0:48, :] = grads_ref[0:48, cols]
        two = jnp.concatenate([grads_ref[48:SLOTS, cols].astype(F32), zeros[0:6]], axis=0)
        out_ref[k, 48:64, :] = jnp.concatenate([two + codes, zeros], axis=0).astype(BF16)


def sum_kernel(recv_ref, out_ref):
    rows = (lax.broadcasted_iota(jnp.int32, (ROWS, 4 * PAD_SLOTS), 0) + 1).astype(F32)
    total = jnp.zeros((ROWS, COLS), F32)
    for g in range(ROLLOUTS // 4):
        codes = jnp.zeros((8, 4 * PAD_SLOTS), F32)
        for k in range(4):
            tile = recv_ref[4 * g + k, 48:64, 0 : 4 * PAD_SLOTS].astype(F32)[0:8]
            codes = codes + (pltpu.roll(tile, PAD_SLOTS * k, 1) if k else tile)
        row = codes[2:3] * 16.0 + codes[3:4]
        onehot = jnp.where(rows == row, 1.0, 0.0).astype(BF16)
        block = recv_ref[4 * g : 4 * g + 4].reshape(4 * PAD_SLOTS, COLS)
        total = total + jnp.dot(onehot, block, preferred_element_type=F32)
    value = total.astype(BF16)
    for k in range(SIDE):
        out_ref[k] = value


GATHERED = (
    (0, ((0, 0),)),
    (3, ((1, 0), (2, 2))),
    (1, ((4, 0), (3, 2))),
    (2, ((5, 0), (6, 2))),
)


def mlp_kernel(w_ref, *refs):
    sums, (slope_ref, out_ref, s, w2, w1, w1_tail, out, sems2, sems1, out_sems) = refs[:7], refs[7:]
    even, second = place_in_plane()
    base = HID_OWN + IN_OWN
    copies, late = [], []
    for n, (offset, parts) in enumerate(GATHERED):
        other = lax.rem(second + offset, SIDE)
        by_row = pltpu.make_async_copy(w_ref.at[other, :, :, 0:HID_OWN], w2.at[n], sems2.at[n, 0])
        by_col = pltpu.make_async_copy(w_ref.at[:, other, :, 0:HID_OWN], w2.at[n], sems2.at[n, 0])
        pl.when(even)(by_row.start)
        pl.when(jnp.logical_not(even))(by_col.start)
        group = [by_row]
        for h, (operand, k) in enumerate(parts):
            count = SIDE // len(parts)
            copy = pltpu.make_async_copy(sums[operand], s.at[n, k : k + count], sems2.at[n, h + 1])
            copy.start()
            group.append(copy)
        copies.append(group)
    for q in range(SIDE):
        pair = [
            pltpu.make_async_copy(w_ref.at[q, :, :, HID_OWN:base], w1.at[q], sems1.at[q, 0]),
            pltpu.make_async_copy(w_ref.at[q, :, :, base:W_ROWS], w1_tail.at[q], sems1.at[q, 1]),
        ]
        for copy in pair:
            copy.start()
        late.append(pair)
    hidden = None
    for n in range(SIDE):
        for copy in copies[n]:
            copy.wait()
        for k in range(SIDE):
            block = s[n, k]
            part = dot_t(block[:, :W2_COLS], w2[n, k, 0]) + dot_t(block[:, W2_COLS:], w2[n, k, 1])
            hidden = part if hidden is None else hidden + part
    act = (hidden * slope_ref[...]).astype(BF16)
    width, done = HID // SIDE, []
    for q in range(SIDE):
        for copy in late[q]:
            copy.wait()
        fold = w1_tail[q]
        tail = jnp.concatenate([fold[..., 0:128], fold[..., 128:256]], axis=2).reshape(width, 128)
        part = dot_t(act[:, 0:256], w1[q].reshape(width, 256)) + dot_t(act[:, 256:], tail[:, 0:64])
        cols = pl.ds(width * q, width)
        out[:, cols] = part.astype(BF16)
        done.append(pltpu.make_async_copy(out.at[:, cols], out_ref.at[:, cols], out_sems.at[q]))
        done[q].start()
    for copy in done:
        copy.wait()


def add_kernel(recv_ref, out_ref):
    total = recv_ref[0].astype(F32)
    for k in range(1, SIDE):
        total = total + recv_ref[k].astype(F32)
    out_ref[...] = total.astype(BF16)


def norm_kernel(recv_ref, patches_ref, gain_ref, out_ref):
    for m in range(MERGE):
        cols = slice(m * VIT, (m + 1) * VIT)
        upstream = recv_ref[0, :, cols].astype(F32)
        for k in range(1, SIDE):
            upstream = upstream + recv_ref[k, :, cols].astype(F32)
        inputs = patches_ref[:, cols].astype(F32)
        scaled = upstream * gain_ref[...]
        inverse = lax.rsqrt(jnp.mean(inputs * inputs, axis=-1, keepdims=True) + 1e-06)
        inner = jnp.mean(scaled * inputs, axis=-1, keepdims=True)
        result = inverse * scaled - inputs * inverse * inverse * inverse * inner
        out_ref[:, cols] = result.astype(BF16)


VMEM = pl.BlockSpec(memory_space=pltpu.VMEM)
SMEM = pl.BlockSpec(memory_space=pltpu.SMEM)
ANY = pl.BlockSpec(memory_space=pl.ANY)


def call(kernel, shape, in_specs, flops=0, moved=0, vmem=16, scratch=()):
    return pl.pallas_call(
        kernel,
        out_shape=jax.ShapeDtypeStruct(shape, BF16),
        in_specs=in_specs,
        out_specs=VMEM,
        scratch_shapes=list(scratch),
        cost_estimate=pl.CostEstimate(flops=flops, bytes_accessed=moved, transcendentals=0),
        compiler_params=pltpu.CompilerParams(vmem_limit_bytes=vmem << 20),
    )


def per_device(row_grads, used_ids, used_count, pre_act, patches, ln_gain, w_fc2, w_fc1):
    weights = call(weights_kernel, (W_ROWS, 256), [VMEM] * 2)(w_fc2, w_fc1)
    weights = lax.all_gather(weights, "prompt", axis=0, tiled=False)

    outgoing = call(
        pack_kernel, (ROLLOUTS, PAD_SLOTS, COLS), [SMEM, VMEM, VMEM], scratch=[pltpu.VMEM((8, COLS), F32)]
    )(used_count, used_ids[0], row_grads[0, 0])
    received = lax.all_to_all(outgoing, "rollout", split_axis=0, concat_axis=0, tiled=True)
    summed = call(sum_kernel, (SIDE, ROWS, COLS), [VMEM])(received)
    line = exchange(summed, 0)
    a1, b1 = shift(line[:2], 1, 1), shift(line[2:], 1, -1)
    a2, b2 = shift(line[2:], 1, 1), shift(line[:2], 1, -1)
    a3, b3 = shift(a1, 1, 1), shift(b1, 1, -1)

    even = lax.axis_index("prompt") % 2 == 0
    slope = gelu_slope(pre_act.astype(F32)).reshape(SIDE, SIDE, OWN, HID_OWN)
    slope = jnp.where(even, slope.transpose(1, 0, 2, 3), slope).reshape(ROWS, HID_OWN)
    weights = weights.reshape(SIDE, SIDE, 2, W_ROWS, 256)
    partial = pl.pallas_call(
        mlp_kernel,
        out_shape=jax.ShapeDtypeStruct((ROWS, HID), BF16),
        in_specs=[ANY] * 8 + [VMEM],
        out_specs=ANY,
        scratch_shapes=[
            pltpu.VMEM((SIDE, SIDE, ROWS, COLS), BF16),
            pltpu.VMEM((SIDE, SIDE, 2, HID_OWN, W2_COLS), BF16),
            pltpu.VMEM((SIDE, SIDE, 2, IN_OWN, 256), BF16),
            pltpu.VMEM((SIDE, SIDE, 2, TAIL, 256), BF16),
            pltpu.VMEM((ROWS, HID), BF16),
            pltpu.SemaphoreType.DMA((SIDE, 3)),
            pltpu.SemaphoreType.DMA((SIDE, 2)),
            pltpu.SemaphoreType.DMA((SIDE,)),
        ],
        cost_estimate=pl.CostEstimate(flops=3 << 30, bytes_accessed=16 << 20, transcendentals=0),
        compiler_params=pltpu.CompilerParams(vmem_limit_bytes=50 << 20),
    )(weights, line, a1, a2, b1, b2, a3, b3, slope)

    halfway = exchange(partial.reshape(SIDE, SIDE * OWN, HID), 0)
    halfway = call(add_kernel, (SIDE * OWN, HID), [VMEM], moved=5 << 20)(halfway)
    last = exchange(halfway.reshape(SIDE, OWN, HID), 1)
    return call(norm_kernel, (OWN, HID), [VMEM] * 3)(last, patches, ln_gain.reshape(1, VIT))


def solution(mesh):
    return jax.shard_map(
        per_device,
        mesh=mesh,
        in_specs=(
            P("prompt", "rollout", None, None),
            P("prompt", "rollout", None),
            P("prompt", "rollout"),
            P("prompt", "rollout"),
            P(("prompt", "rollout"), None),
            P(),
            P("rollout", "prompt"),
            P("prompt", "rollout"),
        ),
        out_specs=P(("prompt", "rollout"), None),
        check_vma=False,
    )
```

```python
import jax
import jax.numpy as jnp
from jax import lax
from jax.experimental import pallas as pl
from jax.experimental.pallas import tpu as pltpu
from jax.sharding import PartitionSpec as P

VIT = 1280
MERGE = 4
PROMPTS = 32
ROLLOUTS = 16
SIDE = 4
SLOTS = 50
PAD_SLOTS = 64
OWN = 24
ROWS = OWN * ROLLOUTS
D_LLM = 8192
COLS = D_LLM // ROLLOUTS
HID = 5120
HID_OWN = HID // ROLLOUTS
IN_OWN = HID // PROMPTS
W2_COLS = D_LLM // PROMPTS
TAIL = IN_OWN // 2
W_ROWS = HID_OWN + IN_OWN + TAIL
AXES = ("prompt", "rollout")
F32 = jnp.float32
BF16 = jnp.bfloat16


def gelu_slope(value):
    return (
        0.5 * (1.0 + jax.scipy.special.erf(value * 0.7071067811865476))
        + value * jnp.exp(-0.5 * value * value) * 0.3989422804014327
    )


def dot_t(left, right):
    return lax.dot_general(left, right, (((1,), (1,)), ((), ())), preferred_element_type=F32)


def line_groups(phase):
    groups = []
    for prompt in range(PROMPTS):
        for other in range(SIDE):
            along_x = (prompt % 2 == 0) == (phase == 0)
            line = [(other * SIDE + i) if along_x else (i * SIDE + other) for i in range(SIDE)]
            groups.append([prompt * ROLLOUTS + r for r in line])
    return groups


def exchange(blocks, phase):
    return lax.all_to_all(
        blocks, AXES, split_axis=0, concat_axis=0, axis_index_groups=line_groups(phase), tiled=True
    )


def shift(value, phase, by):
    pairs = []
    for line in line_groups(phase):
        pairs += [(line[i], line[(i + by) % SIDE]) for i in range(SIDE)]
    return lax.ppermute(value, AXES, pairs)


def place_in_plane():
    rollout = lax.axis_index("rollout")
    even = lax.axis_index("prompt") % 2 == 0
    return even, jnp.where(even, rollout // SIDE, rollout % SIDE)


def weights_kernel(w2_ref, w1_ref, out_ref):
    out_ref[0:HID_OWN, :] = w2_ref[...]
    out_ref[HID_OWN : HID_OWN + IN_OWN, :] = w1_ref[:, 0:256]
    base = HID_OWN + IN_OWN
    out_ref[base:W_ROWS, :] = jnp.zeros((TAIL, 256), BF16)
    out_ref[base:W_ROWS, 0:64] = w1_ref[0:TAIL, 256:320]
    out_ref[base:W_ROWS, 128:192] = w1_ref[TAIL:IN_OWN, 256:320]


def pack_kernel(count_ref, ids_ref, grads_ref, out_ref, meta):
    even, _ = place_in_plane()
    ids = ids_ref[...]
    owner = (ids * 2731) >> 16
    turned = (owner & 3) * SIDE + (owner >> 2)
    place = jnp.where(even, turned, owner) * OWN + ids - owner * OWN + 1
    live = lax.broadcasted_iota(jnp.int32, (1, SLOTS), 1) < count_ref[0, 0]
    place = jnp.where(live, place, 0)
    meta[...] = jnp.zeros((8, COLS), F32)
    meta[2:3, 0:SLOTS] = (place >> 4).astype(F32)
    meta[3:4, 0:SLOTS] = (place & 15).astype(F32)
    codes = meta[...]
    zeros = jnp.zeros((8, COLS), F32)
    for k in range(ROLLOUTS):
        cols = pl.ds(k * COLS, COLS)
        out_ref[k, 0:48, :] = grads_ref[0:48, cols]
        two = jnp.concatenate([grads_ref[48:SLOTS, cols].astype(F32), zeros[0:6]], axis=0)
        out_ref[k, 48:64, :] = jnp.concatenate([two + codes, zeros], axis=0).astype(BF16)


def sum_kernel(recv_ref, out_ref):
    rows = (lax.broadcasted_iota(jnp.int32, (ROWS, 4 * PAD_SLOTS), 0) + 1).astype(F32)
    total = jnp.zeros((ROWS, COLS), F32)
    for g in range(ROLLOUTS // 4):
        codes = jnp.zeros((8, 4 * PAD_SLOTS), F32)
        for k in range(4):
            tile = recv_ref[4 * g + k, 48:64, 0 : 4 * PAD_SLOTS].astype(F32)[0:8]
            codes = codes + (pltpu.roll(tile, PAD_SLOTS * k, 1) if k else tile)
        row = codes[2:3] * 16.0 + codes[3:4]
        onehot = jnp.where(rows == row, 1.0, 0.0).astype(BF16)
        block = recv_ref[4 * g : 4 * g + 4].reshape(4 * PAD_SLOTS, COLS)
        total = total + jnp.dot(onehot, block, preferred_element_type=F32)
    value = total.astype(BF16)
    for k in range(SIDE):
        out_ref[k] = value


GATHERED = (
    (0, ((0, 0),)),
    (3, ((1, 0), (2, 2))),
    (1, ((4, 0), (3, 2))),
    (2, ((5, 0), (6, 2))),
)


def mlp_kernel(w_ref, *refs):
    sums, (slope_ref, out_ref, s, w2, w1, w1_tail, sems2, sems1) = refs[:7], refs[7:]
    even, second = place_in_plane()
    base = HID_OWN + IN_OWN
    copies, late = [], []
    for n, (offset, parts) in enumerate(GATHERED):
        other = lax.rem(second + offset, SIDE)
        by_row = pltpu.make_async_copy(w_ref.at[other, :, :, 0:HID_OWN], w2.at[n], sems2.at[n, 0])
        by_col = pltpu.make_async_copy(w_ref.at[:, other, :, 0:HID_OWN], w2.at[n], sems2.at[n, 0])
        pl.when(even)(by_row.start)
        pl.when(jnp.logical_not(even))(by_col.start)
        group = [by_row]
        for h, (operand, k) in enumerate(parts):
            count = SIDE // len(parts)
            copy = pltpu.make_async_copy(sums[operand], s.at[n, k : k + count], sems2.at[n, h + 1])
            copy.start()
            group.append(copy)
        copies.append(group)
    for q in range(SIDE):
        pair = [
            pltpu.make_async_copy(w_ref.at[q, :, :, HID_OWN:base], w1.at[q], sems1.at[q, 0]),
            pltpu.make_async_copy(w_ref.at[q, :, :, base:W_ROWS], w1_tail.at[q], sems1.at[q, 1]),
        ]
        for copy in pair:
            copy.start()
        late.append(pair)
    hidden = None
    for n in range(SIDE):
        for copy in copies[n]:
            copy.wait()
        for k in range(SIDE):
            block = s[n, k]
            part = dot_t(block[:, :W2_COLS], w2[n, k, 0]) + dot_t(block[:, W2_COLS:], w2[n, k, 1])
            hidden = part if hidden is None else hidden + part
    act = (hidden * slope_ref[...]).astype(BF16)
    width = HID // SIDE
    for q in range(SIDE):
        for copy in late[q]:
            copy.wait()
        fold = w1_tail[q]
        tail = jnp.concatenate([fold[..., 0:128], fold[..., 128:256]], axis=2).reshape(width, 128)
        part = dot_t(act[:, 0:256], w1[q].reshape(width, 256)) + dot_t(act[:, 256:], tail[:, 0:64])
        out_ref[:, width * q : width * (q + 1)] = part.astype(BF16)


def add_kernel(recv_ref, out_ref):
    total = recv_ref[0].astype(F32)
    for k in range(1, SIDE):
        total = total + recv_ref[k].astype(F32)
    out_ref[...] = total.astype(BF16)


def norm_kernel(recv_ref, patches_ref, gain_ref, out_ref):
    for m in range(MERGE):
        cols = slice(m * VIT, (m + 1) * VIT)
        upstream = recv_ref[0, :, cols].astype(F32)
        for k in range(1, SIDE):
            upstream = upstream + recv_ref[k, :, cols].astype(F32)
        inputs = patches_ref[:, cols].astype(F32)
        scaled = upstream * gain_ref[...]
        inverse = lax.rsqrt(jnp.mean(inputs * inputs, axis=-1, keepdims=True) + 1e-06)
        inner = jnp.mean(scaled * inputs, axis=-1, keepdims=True)
        result = inverse * scaled - inputs * inverse * inverse * inverse * inner
        out_ref[:, cols] = result.astype(BF16)


VMEM = pl.BlockSpec(memory_space=pltpu.VMEM)
SMEM = pl.BlockSpec(memory_space=pltpu.SMEM)
ANY = pl.BlockSpec(memory_space=pl.ANY)


def call(kernel, shape, in_specs, flops=0, moved=0, vmem=16, scratch=(), fast=False):
    return pl.pallas_call(
        kernel,
        out_shape=pltpu.VMEM(shape, BF16) if fast else jax.ShapeDtypeStruct(shape, BF16),
        in_specs=in_specs,
        out_specs=VMEM,
        scratch_shapes=list(scratch),
        cost_estimate=pl.CostEstimate(flops=flops, bytes_accessed=moved, transcendentals=0),
        compiler_params=pltpu.CompilerParams(vmem_limit_bytes=vmem << 20),
    )


def per_device(row_grads, used_ids, used_count, pre_act, patches, ln_gain, w_fc2, w_fc1):
    weights = call(weights_kernel, (W_ROWS, 256), [VMEM] * 2)(w_fc2, w_fc1)
    weights = lax.all_gather(weights, "prompt", axis=0, tiled=False)

    outgoing = call(
        pack_kernel, (ROLLOUTS, PAD_SLOTS, COLS), [SMEM, VMEM, VMEM], scratch=[pltpu.VMEM((8, COLS), F32)]
    )(used_count, used_ids[0], row_grads[0, 0])
    received = lax.all_to_all(outgoing, "rollout", split_axis=0, concat_axis=0, tiled=True)
    summed = call(sum_kernel, (SIDE, ROWS, COLS), [VMEM])(received)
    line = exchange(summed, 0)
    a1, b1 = shift(line[:2], 1, 1), shift(line[2:], 1, -1)
    a2, b2 = shift(line[2:], 1, 1), shift(line[:2], 1, -1)
    a3, b3 = shift(a1, 1, 1), shift(b1, 1, -1)

    even = lax.axis_index("prompt") % 2 == 0
    slope = gelu_slope(pre_act.astype(F32)).reshape(SIDE, SIDE, OWN, HID_OWN)
    slope = jnp.where(even, slope.transpose(1, 0, 2, 3), slope).reshape(ROWS, HID_OWN)
    weights = weights.reshape(SIDE, SIDE, 2, W_ROWS, 256)
    partial = pl.pallas_call(
        mlp_kernel,
        out_shape=pltpu.VMEM((ROWS, HID), BF16),
        in_specs=[ANY] * 8 + [VMEM],
        out_specs=VMEM,
        scratch_shapes=[
            pltpu.VMEM((SIDE, SIDE, ROWS, COLS), BF16),
            pltpu.VMEM((SIDE, SIDE, 2, HID_OWN, W2_COLS), BF16),
            pltpu.VMEM((SIDE, SIDE, 2, IN_OWN, 256), BF16),
            pltpu.VMEM((SIDE, SIDE, 2, TAIL, 256), BF16),
            pltpu.SemaphoreType.DMA((SIDE, 3)),
            pltpu.SemaphoreType.DMA((SIDE, 2)),
        ],
        cost_estimate=pl.CostEstimate(flops=3 << 30, bytes_accessed=16 << 20, transcendentals=0),
        compiler_params=pltpu.CompilerParams(vmem_limit_bytes=24 << 20),
    )(pltpu.with_memory_space_constraint(weights, pltpu.HBM), line, a1, a2, b1, b2, a3, b3, slope)

    halfway = exchange(partial.reshape(SIDE, SIDE * OWN, HID), 0)
    halfway = call(add_kernel, (SIDE * OWN, HID), [VMEM], moved=5 << 20, fast=True)(halfway)
    last = exchange(halfway.reshape(SIDE, OWN, HID), 1)
    return call(norm_kernel, (OWN, HID), [VMEM] * 3)(last, patches, ln_gain.reshape(1, VIT))


def solution(mesh):
    return jax.shard_map(
        per_device,
        mesh=mesh,
        in_specs=(
            P("prompt", "rollout", None, None),
            P("prompt", "rollout", None),
            P("prompt", "rollout"),
            P("prompt", "rollout"),
            P(("prompt", "rollout"), None),
            P(),
            P("rollout", "prompt"),
            P("prompt", "rollout"),
        ),
        out_specs=P(("prompt", "rollout"), None),
        check_vma=False,
    )
```

```python
import jax
import jax.numpy as jnp
from jax import lax
from jax.experimental import pallas as pl
from jax.experimental.pallas import tpu as pltpu
from jax.sharding import PartitionSpec as P

VIT = 1280
MERGE = 4
PROMPTS = 32
ROLLOUTS = 16
SIDE = 4
SLOTS = 50
PAD_SLOTS = 64
OWN = 24
ROWS = OWN * ROLLOUTS
D_LLM = 8192
COLS = D_LLM // ROLLOUTS
HID = 5120
HID_OWN = HID // ROLLOUTS
IN_OWN = HID // PROMPTS
W2_COLS = D_LLM // PROMPTS
TAIL = IN_OWN // 2
W_ROWS = HID_OWN + IN_OWN + TAIL
AXES = ("prompt", "rollout")
F32 = jnp.float32
BF16 = jnp.bfloat16


def gelu_slope(value):
    return (
        0.5 * (1.0 + jax.scipy.special.erf(value * 0.7071067811865476))
        + value * jnp.exp(-0.5 * value * value) * 0.3989422804014327
    )


def dot_t(left, right):
    return lax.dot_general(left, right, (((1,), (1,)), ((), ())), preferred_element_type=F32)


def line_groups(phase):
    groups = []
    for prompt in range(PROMPTS):
        for other in range(SIDE):
            along_x = (prompt % 2 == 0) == (phase == 0)
            line = [(other * SIDE + i) if along_x else (i * SIDE + other) for i in range(SIDE)]
            groups.append([prompt * ROLLOUTS + r for r in line])
    return groups


def exchange(blocks, phase):
    return lax.all_to_all(
        blocks, AXES, split_axis=0, concat_axis=0, axis_index_groups=line_groups(phase), tiled=True
    )


def shift(value, phase, by):
    pairs = []
    for line in line_groups(phase):
        pairs += [(line[i], line[(i + by) % SIDE]) for i in range(SIDE)]
    return lax.ppermute(value, AXES, pairs)


def place_in_plane():
    rollout = lax.axis_index("rollout")
    even = lax.axis_index("prompt") % 2 == 0
    return even, jnp.where(even, rollout // SIDE, rollout % SIDE)


def weights_kernel(w2_ref, w1_ref, out_ref):
    out_ref[0:HID_OWN, :] = w2_ref[...]
    out_ref[HID_OWN : HID_OWN + IN_OWN, :] = w1_ref[:, 0:256]
    base = HID_OWN + IN_OWN
    out_ref[base:W_ROWS, :] = jnp.zeros((TAIL, 256), BF16)
    out_ref[base:W_ROWS, 0:64] = w1_ref[0:TAIL, 256:320]
    out_ref[base:W_ROWS, 128:192] = w1_ref[TAIL:IN_OWN, 256:320]


def pack_kernel(count_ref, ids_ref, grads_ref, out_ref, meta):
    even, _ = place_in_plane()
    ids = ids_ref[...]
    owner = (ids * 2731) >> 16
    turned = (owner & 3) * SIDE + (owner >> 2)
    place = jnp.where(even, turned, owner) * OWN + ids - owner * OWN + 1
    live = lax.broadcasted_iota(jnp.int32, (1, SLOTS), 1) < count_ref[0, 0]
    place = jnp.where(live, place, 0)
    meta[...] = jnp.zeros((8, COLS), F32)
    meta[2:3, 0:SLOTS] = (place >> 4).astype(F32)
    meta[3:4, 0:SLOTS] = (place & 15).astype(F32)
    codes = meta[...]
    zeros = jnp.zeros((8, COLS), F32)
    for k in range(ROLLOUTS):
        cols = pl.ds(k * COLS, COLS)
        out_ref[k, 0:48, :] = grads_ref[0:48, cols]
        two = jnp.concatenate([grads_ref[48:SLOTS, cols].astype(F32), zeros[0:6]], axis=0)
        out_ref[k, 48:64, :] = jnp.concatenate([two + codes, zeros], axis=0).astype(BF16)


def sum_kernel(recv_ref, out_ref):
    rows = (lax.broadcasted_iota(jnp.int32, (ROWS, 4 * PAD_SLOTS), 0) + 1).astype(F32)
    total = jnp.zeros((ROWS, COLS), F32)
    for g in range(ROLLOUTS // 4):
        codes = jnp.zeros((8, 4 * PAD_SLOTS), F32)
        for k in range(4):
            tile = recv_ref[4 * g + k, 48:64, 0 : 4 * PAD_SLOTS].astype(F32)[0:8]
            codes = codes + (pltpu.roll(tile, PAD_SLOTS * k, 1) if k else tile)
        row = codes[2:3] * 16.0 + codes[3:4]
        onehot = jnp.where(rows == row, 1.0, 0.0).astype(BF16)
        block = recv_ref[4 * g : 4 * g + 4].reshape(4 * PAD_SLOTS, COLS)
        total = total + jnp.dot(onehot, block, preferred_element_type=F32)
    value = total.astype(BF16)
    for k in range(SIDE):
        out_ref[k] = value


GATHERED = (
    (0, ((0, 0),)),
    (3, ((1, 0), (2, 2))),
    (1, ((4, 0), (3, 2))),
    (2, ((5, 0), (6, 2))),
)


def mlp_kernel(w_ref, *refs):
    sums, (slope_ref, out_ref, s, w2, w1, w1_tail, sems2, sems1) = refs[:7], refs[7:]
    even, second = place_in_plane()
    base = HID_OWN + IN_OWN
    copies, late = [], []
    for n, (offset, parts) in enumerate(GATHERED):
        other = lax.rem(second + offset, SIDE)
        by_row = pltpu.make_async_copy(w_ref.at[other, :, :, 0:HID_OWN], w2.at[n], sems2.at[n, 0])
        by_col = pltpu.make_async_copy(w_ref.at[:, other, :, 0:HID_OWN], w2.at[n], sems2.at[n, 0])
        pl.when(even)(by_row.start)
        pl.when(jnp.logical_not(even))(by_col.start)
        group = [by_row]
        for h, (operand, k) in enumerate(parts):
            count = SIDE // len(parts)
            copy = pltpu.make_async_copy(sums[operand], s.at[n, k : k + count], sems2.at[n, h + 1])
            copy.start()
            group.append(copy)
        copies.append(group)
    for q in range(SIDE):
        pair = [
            pltpu.make_async_copy(w_ref.at[q, :, :, HID_OWN:base], w1.at[q], sems1.at[q, 0]),
            pltpu.make_async_copy(w_ref.at[q, :, :, base:W_ROWS], w1_tail.at[q], sems1.at[q, 1]),
        ]
        for copy in pair:
            copy.start()
        late.append(pair)
    hidden = None
    for n in range(SIDE):
        for copy in copies[n]:
            copy.wait()
        for k in range(SIDE):
            block = s[n, k]
            part = dot_t(w2[n, k, 0], block[:, :W2_COLS]) + dot_t(w2[n, k, 1], block[:, W2_COLS:])
            hidden = part if hidden is None else hidden + part
    act = (hidden.T * slope_ref[...]).astype(BF16)
    width = HID // SIDE
    for q in range(SIDE):
        for copy in late[q]:
            copy.wait()
        fold = w1_tail[q]
        tail = jnp.concatenate([fold[..., 0:128], fold[..., 128:256]], axis=2).reshape(width, 128)
        part = dot_t(act[:, 0:256], w1[q].reshape(width, 256)) + dot_t(act[:, 256:], tail[:, 0:64])
        out_ref[:, width * q : width * (q + 1)] = part.astype(BF16)


def add_kernel(recv_ref, out_ref):
    total = recv_ref[0].astype(F32)
    for k in range(1, SIDE):
        total = total + recv_ref[k].astype(F32)
    out_ref[...] = total.astype(BF16)


def norm_kernel(recv_ref, patches_hbm, gain_hbm, out_ref, patches_ref, gain_ref, sems):
    copies = [
        pltpu.make_async_copy(patches_hbm, patches_ref, sems.at[0]),
        pltpu.make_async_copy(gain_hbm, gain_ref, sems.at[1]),
    ]
    for copy in copies:
        copy.start()
    for copy in copies:
        copy.wait()
    for m in range(MERGE):
        cols = slice(m * VIT, (m + 1) * VIT)
        upstream = recv_ref[0, :, cols].astype(F32)
        for k in range(1, SIDE):
            upstream = upstream + recv_ref[k, :, cols].astype(F32)
        inputs = patches_ref[:, cols].astype(F32)
        scaled = upstream * gain_ref[...][None]
        inverse = lax.rsqrt(jnp.mean(inputs * inputs, axis=-1, keepdims=True) + 1e-06)
        inner = jnp.mean(scaled * inputs, axis=-1, keepdims=True)
        result = inverse * scaled - inputs * inverse * inverse * inverse * inner
        out_ref[:, cols] = result.astype(BF16)


VMEM = pl.BlockSpec(memory_space=pltpu.VMEM)
SMEM = pl.BlockSpec(memory_space=pltpu.SMEM)
ANY = pl.BlockSpec(memory_space=pl.ANY)


def call(kernel, shape, in_specs, flops=0, moved=0, vmem=16, scratch=(), fast=False):
    return pl.pallas_call(
        kernel,
        out_shape=pltpu.VMEM(shape, BF16) if fast else jax.ShapeDtypeStruct(shape, BF16),
        in_specs=in_specs,
        out_specs=VMEM,
        scratch_shapes=list(scratch),
        cost_estimate=pl.CostEstimate(flops=flops, bytes_accessed=moved, transcendentals=0),
        compiler_params=pltpu.CompilerParams(vmem_limit_bytes=vmem << 20),
    )


def pinned(value):
    return pltpu.with_memory_space_constraint(value, pltpu.HBM)


def per_device(row_grads, used_ids, used_count, pre_act, patches, ln_gain, w_fc2, w_fc1):
    weights = call(weights_kernel, (W_ROWS, 256), [VMEM] * 2)(w_fc2, w_fc1)
    weights = lax.all_gather(weights, "prompt", axis=0, tiled=False)

    outgoing = call(
        pack_kernel, (ROLLOUTS, PAD_SLOTS, COLS), [SMEM, VMEM, VMEM], scratch=[pltpu.VMEM((8, COLS), F32)]
    )(used_count, used_ids[0], row_grads[0, 0])
    received = lax.all_to_all(outgoing, "rollout", split_axis=0, concat_axis=0, tiled=True)
    summed = call(sum_kernel, (SIDE, ROWS, COLS), [VMEM])(received)
    line = exchange(summed, 0)
    a1, b1 = shift(line[:2], 1, 1), shift(line[2:], 1, -1)
    a2, b2 = shift(line[2:], 1, 1), shift(line[:2], 1, -1)
    a3, b3 = shift(a1, 1, 1), shift(b1, 1, -1)

    even = lax.axis_index("prompt") % 2 == 0
    slope = gelu_slope(pre_act.astype(F32)).reshape(SIDE, SIDE, OWN, HID_OWN)
    slope = jnp.where(even, slope.transpose(1, 0, 2, 3), slope).reshape(ROWS, HID_OWN)
    weights = weights.reshape(SIDE, SIDE, 2, W_ROWS, 256)
    partial = pl.pallas_call(
        mlp_kernel,
        out_shape=pltpu.VMEM((ROWS, HID), BF16),
        in_specs=[ANY] * 8 + [VMEM],
        out_specs=VMEM,
        scratch_shapes=[
            pltpu.VMEM((SIDE, SIDE, ROWS, COLS), BF16),
            pltpu.VMEM((SIDE, SIDE, 2, HID_OWN, W2_COLS), BF16),
            pltpu.VMEM((SIDE, SIDE, 2, IN_OWN, 256), BF16),
            pltpu.VMEM((SIDE, SIDE, 2, TAIL, 256), BF16),
            pltpu.SemaphoreType.DMA((SIDE, 3)),
            pltpu.SemaphoreType.DMA((SIDE, 2)),
        ],
        cost_estimate=pl.CostEstimate(flops=3 << 30, bytes_accessed=16 << 20, transcendentals=0),
        compiler_params=pltpu.CompilerParams(vmem_limit_bytes=24 << 20),
    )(pinned(weights), line, a1, a2, b1, b2, a3, b3, slope)

    halfway = exchange(partial.reshape(SIDE, SIDE * OWN, HID), 0)
    halfway = call(add_kernel, (SIDE * OWN, HID), [VMEM], moved=5 << 20, fast=True)(halfway)
    last = exchange(halfway.reshape(SIDE, OWN, HID), 1)
    return call(
        norm_kernel,
        (OWN, HID),
        [VMEM, ANY, ANY],
        scratch=[
            pltpu.VMEM((OWN, HID), BF16),
            pltpu.VMEM((VIT,), F32),
            pltpu.SemaphoreType.DMA((2,)),
        ],
    )(last, pinned(patches), pinned(ln_gain))


def solution(mesh):
    return jax.shard_map(
        per_device,
        mesh=mesh,
        in_specs=(
            P("prompt", "rollout", None, None),
            P("prompt", "rollout", None),
            P("prompt", "rollout"),
            P("prompt", "rollout"),
            P(("prompt", "rollout"), None),
            P(),
            P("rollout", "prompt"),
            P("prompt", "rollout"),
        ),
        out_specs=P(("prompt", "rollout"), None),
        check_vma=False,
    )
```

```python
import jax
import jax.numpy as jnp
from jax import lax
from jax.experimental import pallas as pl
from jax.experimental.pallas import tpu as pltpu
from jax.sharding import PartitionSpec as P

VIT = 1280
MERGE = 4
PROMPTS = 32
ROLLOUTS = 16
SIDE = 4
SLOTS = 50
PAD_SLOTS = 64
OWN = 24
ROWS = OWN * ROLLOUTS
D_LLM = 8192
COLS = D_LLM // ROLLOUTS
HID = 5120
HID_OWN = HID // ROLLOUTS
IN_OWN = HID // PROMPTS
W2_COLS = D_LLM // PROMPTS
TAIL = IN_OWN // 2
W_ROWS = HID_OWN + IN_OWN + TAIL
AXES = ("prompt", "rollout")
F32 = jnp.float32
BF16 = jnp.bfloat16


def gelu_slope(value):
    return (
        0.5 * (1.0 + jax.scipy.special.erf(value * 0.7071067811865476))
        + value * jnp.exp(-0.5 * value * value) * 0.3989422804014327
    )


def dot_t(left, right):
    return lax.dot_general(left, right, (((1,), (1,)), ((), ())), preferred_element_type=F32)


def line_groups(phase):
    groups = []
    for prompt in range(PROMPTS):
        for other in range(SIDE):
            along_x = (prompt % 2 == 0) == (phase == 0)
            line = [(other * SIDE + i) if along_x else (i * SIDE + other) for i in range(SIDE)]
            groups.append([prompt * ROLLOUTS + r for r in line])
    return groups


def exchange(blocks, phase):
    return lax.all_to_all(
        blocks, AXES, split_axis=0, concat_axis=0, axis_index_groups=line_groups(phase), tiled=True
    )


def shift(value, phase, by):
    pairs = []
    for line in line_groups(phase):
        pairs += [(line[i], line[(i + by) % SIDE]) for i in range(SIDE)]
    return lax.ppermute(value, AXES, pairs)


def place_in_plane():
    rollout = lax.axis_index("rollout")
    even = lax.axis_index("prompt") % 2 == 0
    return even, jnp.where(even, rollout // SIDE, rollout % SIDE)


def pack_kernel(count_ref, ids_ref, grads_ref, w2_ref, w1_ref, out_ref, weights_ref, weights, w1, meta, sems):
    base = HID_OWN + IN_OWN
    from_w2 = pltpu.make_async_copy(w2_ref, weights.at[0:HID_OWN], sems.at[0])
    from_w1 = pltpu.make_async_copy(w1_ref, w1, sems.at[1])
    from_w2.start()
    from_w1.start()
    from_w1.wait()
    weights[HID_OWN:base, :] = w1[:, 0:256]
    weights[base:W_ROWS, :] = jnp.zeros((TAIL, 256), BF16)
    weights[base:W_ROWS, 0:64] = w1[0:TAIL, 256:320]
    weights[base:W_ROWS, 128:192] = w1[TAIL:IN_OWN, 256:320]
    from_w2.wait()
    to_weights = pltpu.make_async_copy(weights, weights_ref, sems.at[2])
    to_weights.start()

    even, _ = place_in_plane()
    ids = ids_ref[...]
    owner = (ids * 2731) >> 16
    turned = (owner & 3) * SIDE + (owner >> 2)
    place = jnp.where(even, turned, owner) * OWN + ids - owner * OWN + 1
    live = lax.broadcasted_iota(jnp.int32, (1, SLOTS), 1) < count_ref[0, 0]
    place = jnp.where(live, place, 0)
    meta[...] = jnp.zeros((8, COLS), F32)
    meta[2:3, 0:SLOTS] = (place >> 4).astype(F32)
    meta[3:4, 0:SLOTS] = (place & 15).astype(F32)
    codes = meta[...]
    zeros = jnp.zeros((8, COLS), F32)
    for k in range(ROLLOUTS):
        cols = pl.ds(k * COLS, COLS)
        out_ref[k, 0:48, :] = grads_ref[0:48, cols]
        two = jnp.concatenate([grads_ref[48:SLOTS, cols].astype(F32), zeros[0:6]], axis=0)
        out_ref[k, 48:64, :] = jnp.concatenate([two + codes, zeros], axis=0).astype(BF16)
    to_weights.wait()


def sum_kernel(recv_ref, out_ref):
    rows = (lax.broadcasted_iota(jnp.int32, (ROWS, 4 * PAD_SLOTS), 0) + 1).astype(F32)
    total = jnp.zeros((ROWS, COLS), F32)
    for g in range(ROLLOUTS // 4):
        codes = jnp.zeros((8, 4 * PAD_SLOTS), F32)
        for k in range(4):
            tile = recv_ref[4 * g + k, 48:64, 0 : 4 * PAD_SLOTS].astype(F32)[0:8]
            codes = codes + (pltpu.roll(tile, PAD_SLOTS * k, 1) if k else tile)
        row = codes[2:3] * 16.0 + codes[3:4]
        onehot = jnp.where(rows == row, 1.0, 0.0).astype(BF16)
        block = recv_ref[4 * g : 4 * g + 4].reshape(4 * PAD_SLOTS, COLS)
        total = total + jnp.dot(onehot, block, preferred_element_type=F32)
    value = total.astype(BF16)
    for k in range(SIDE):
        out_ref[k] = value


GATHERED = (
    (0, ((0, 0),)),
    (3, ((1, 0), (2, 2))),
    (1, ((4, 0), (3, 2))),
    (2, ((5, 0), (6, 2))),
)


def mlp_kernel(w_ref, *refs):
    sums, (slope_ref, out_ref, s, w2, w1, w1_tail, sems2, sems1) = refs[:7], refs[7:]
    even, second = place_in_plane()
    base = HID_OWN + IN_OWN
    copies, late = [], []
    for n, (offset, parts) in enumerate(GATHERED):
        other = lax.rem(second + offset, SIDE)
        by_row = pltpu.make_async_copy(w_ref.at[other, :, :, 0:HID_OWN], w2.at[n], sems2.at[n, 0])
        by_col = pltpu.make_async_copy(w_ref.at[:, other, :, 0:HID_OWN], w2.at[n], sems2.at[n, 0])
        pl.when(even)(by_row.start)
        pl.when(jnp.logical_not(even))(by_col.start)
        group = [by_row]
        for h, (operand, k) in enumerate(parts):
            count = SIDE // len(parts)
            copy = pltpu.make_async_copy(sums[operand], s.at[n, k : k + count], sems2.at[n, h + 1])
            copy.start()
            group.append(copy)
        copies.append(group)
    for q in range(SIDE):
        pair = [
            pltpu.make_async_copy(w_ref.at[q, :, :, HID_OWN:base], w1.at[q], sems1.at[q, 0]),
            pltpu.make_async_copy(w_ref.at[q, :, :, base:W_ROWS], w1_tail.at[q], sems1.at[q, 1]),
        ]
        for copy in pair:
            copy.start()
        late.append(pair)
    hidden = None
    for n in range(SIDE):
        for copy in copies[n]:
            copy.wait()
        for k in range(SIDE):
            block = s[n, k]
            part = dot_t(w2[n, k, 0], block[:, :W2_COLS]) + dot_t(w2[n, k, 1], block[:, W2_COLS:])
            hidden = part if hidden is None else hidden + part
    act = (hidden.T * slope_ref[...]).astype(BF16)
    width = HID // SIDE
    for q in range(SIDE):
        for copy in late[q]:
            copy.wait()
        fold = w1_tail[q]
        tail = jnp.concatenate([fold[..., 0:128], fold[..., 128:256]], axis=2).reshape(width, 128)
        part = dot_t(act[:, 0:256], w1[q].reshape(width, 256)) + dot_t(act[:, 256:], tail[:, 0:64])
        out_ref[:, width * q : width * (q + 1)] = part.astype(BF16)


def add_kernel(recv_ref, out_ref):
    total = recv_ref[0].astype(F32)
    for k in range(1, SIDE):
        total = total + recv_ref[k].astype(F32)
    out_ref[...] = total.astype(BF16)


def norm_kernel(recv_ref, patches_hbm, gain_hbm, out_ref, patches_ref, gain_ref, sems):
    copies = [
        pltpu.make_async_copy(patches_hbm, patches_ref, sems.at[0]),
        pltpu.make_async_copy(gain_hbm, gain_ref, sems.at[1]),
    ]
    for copy in copies:
        copy.start()
    sums = []
    for m in range(MERGE):
        cols = slice(m * VIT, (m + 1) * VIT)
        upstream = recv_ref[0, :, cols].astype(F32)
        for k in range(1, SIDE):
            upstream = upstream + recv_ref[k, :, cols].astype(F32)
        sums.append(upstream)
    for copy in copies:
        copy.wait()
    gain = gain_ref[...][None]
    for m in range(MERGE):
        cols = slice(m * VIT, (m + 1) * VIT)
        inputs = patches_ref[:, cols].astype(F32)
        scaled = sums[m] * gain
        inverse = lax.rsqrt(jnp.mean(inputs * inputs, axis=-1, keepdims=True) + 1e-06)
        inner = jnp.mean(scaled * inputs, axis=-1, keepdims=True)
        result = inverse * scaled - inputs * inverse * inverse * inverse * inner
        out_ref[:, cols] = result.astype(BF16)


VMEM = pl.BlockSpec(memory_space=pltpu.VMEM)
SMEM = pl.BlockSpec(memory_space=pltpu.SMEM)
ANY = pl.BlockSpec(memory_space=pl.ANY)


def call(kernel, shape, in_specs, flops=0, moved=0, vmem=16, scratch=(), fast=False):
    return pl.pallas_call(
        kernel,
        out_shape=pltpu.VMEM(shape, BF16) if fast else jax.ShapeDtypeStruct(shape, BF16),
        in_specs=in_specs,
        out_specs=VMEM,
        scratch_shapes=list(scratch),
        cost_estimate=pl.CostEstimate(flops=flops, bytes_accessed=moved, transcendentals=0),
        compiler_params=pltpu.CompilerParams(vmem_limit_bytes=vmem << 20),
    )


def pinned(value):
    return pltpu.with_memory_space_constraint(value, pltpu.HBM)


def per_device(row_grads, used_ids, used_count, pre_act, patches, ln_gain, w_fc2, w_fc1):
    outgoing, weights = pl.pallas_call(
        pack_kernel,
        out_shape=[
            jax.ShapeDtypeStruct((ROLLOUTS, PAD_SLOTS, COLS), BF16),
            jax.ShapeDtypeStruct((W_ROWS, 256), BF16),
        ],
        in_specs=[SMEM, VMEM, VMEM, ANY, ANY],
        out_specs=[VMEM, ANY],
        scratch_shapes=[
            pltpu.VMEM((W_ROWS, 256), BF16),
            pltpu.VMEM((IN_OWN, HID_OWN), BF16),
            pltpu.VMEM((8, COLS), F32),
            pltpu.SemaphoreType.DMA((3,)),
        ],
        compiler_params=pltpu.CompilerParams(vmem_limit_bytes=16 << 20),
    )(used_count, used_ids[0], row_grads[0, 0], pinned(w_fc2), pinned(w_fc1))
    groups = [[p * ROLLOUTS + r for p in range(PROMPTS)] for r in range(ROLLOUTS)]
    weights = lax.all_gather(weights, AXES, axis=0, tiled=False, axis_index_groups=groups)

    received = lax.all_to_all(outgoing, "rollout", split_axis=0, concat_axis=0, tiled=True)
    summed = call(sum_kernel, (SIDE, ROWS, COLS), [VMEM])(received)
    line = exchange(summed, 0)
    a1, b1 = shift(line[:2], 1, 1), shift(line[2:], 1, -1)
    a2, b2 = shift(line[2:], 1, 1), shift(line[:2], 1, -1)
    a3, b3 = shift(a1, 1, 1), shift(b1, 1, -1)

    even = lax.axis_index("prompt") % 2 == 0
    slope = gelu_slope(pre_act.astype(F32)).reshape(SIDE, SIDE, OWN, HID_OWN)
    slope = jnp.where(even, slope.transpose(1, 0, 2, 3), slope).reshape(ROWS, HID_OWN)
    weights = weights.reshape(SIDE, SIDE, 2, W_ROWS, 256)
    partial = pl.pallas_call(
        mlp_kernel,
        out_shape=pltpu.VMEM((ROWS, HID), BF16),
        in_specs=[ANY] * 8 + [VMEM],
        out_specs=VMEM,
        scratch_shapes=[
            pltpu.VMEM((SIDE, SIDE, ROWS, COLS), BF16),
            pltpu.VMEM((SIDE, SIDE, 2, HID_OWN, W2_COLS), BF16),
            pltpu.VMEM((SIDE, SIDE, 2, IN_OWN, 256), BF16),
            pltpu.VMEM((SIDE, SIDE, 2, TAIL, 256), BF16),
            pltpu.SemaphoreType.DMA((SIDE, 3)),
            pltpu.SemaphoreType.DMA((SIDE, 2)),
        ],
        cost_estimate=pl.CostEstimate(flops=3 << 30, bytes_accessed=16 << 20, transcendentals=0),
        compiler_params=pltpu.CompilerParams(vmem_limit_bytes=24 << 20),
    )(pinned(weights), line, a1, a2, b1, b2, a3, b3, slope)

    halfway = exchange(partial.reshape(SIDE, SIDE * OWN, HID), 0)
    halfway = call(add_kernel, (SIDE * OWN, HID), [VMEM], moved=5 << 20, fast=True)(halfway)
    last = exchange(halfway.reshape(SIDE, OWN, HID), 1)
    return call(
        norm_kernel,
        (OWN, HID),
        [VMEM, ANY, ANY],
        scratch=[
            pltpu.VMEM((OWN, HID), BF16),
            pltpu.VMEM((VIT,), F32),
            pltpu.SemaphoreType.DMA((2,)),
        ],
    )(last, pinned(patches), pinned(ln_gain))


def solution(mesh):
    return jax.shard_map(
        per_device,
        mesh=mesh,
        in_specs=(
            P("prompt", "rollout", None, None),
            P("prompt", "rollout", None),
            P("prompt", "rollout"),
            P("prompt", "rollout"),
            P(("prompt", "rollout"), None),
            P(),
            P("rollout", "prompt"),
            P("prompt", "rollout"),
        ),
        out_specs=P(("prompt", "rollout"), None),
        check_vma=False,
    )
```

```python
import jax
import jax.numpy as jnp
from jax import lax
from jax.experimental import pallas as pl
from jax.experimental.pallas import tpu as pltpu
from jax.sharding import PartitionSpec as P

VIT = 1280
MERGE = 4
PROMPTS = 32
ROLLOUTS = 16
SIDE = 4
SLOTS = 50
PAD_SLOTS = 64
OWN = 24
ROWS = OWN * ROLLOUTS
D_LLM = 8192
COLS = D_LLM // ROLLOUTS
HID = 5120
HID_OWN = HID // ROLLOUTS
IN_OWN = HID // PROMPTS
W2_COLS = D_LLM // PROMPTS
RUNS = (48, 48, 32, 32)
TAIL = 48
W_ROWS = HID_OWN + IN_OWN + TAIL
AXES = ("prompt", "rollout")
F32 = jnp.float32
BF16 = jnp.bfloat16


def gelu_slope(value):
    return (
        0.5 * (1.0 + jax.scipy.special.erf(value * 0.7071067811865476))
        + value * jnp.exp(-0.5 * value * value) * 0.3989422804014327
    )


def dot_t(left, right):
    return lax.dot_general(left, right, (((1,), (1,)), ((), ())), preferred_element_type=F32)


def line_groups(phase):
    groups = []
    for prompt in range(PROMPTS):
        for other in range(SIDE):
            along_x = (prompt % 2 == 0) == (phase == 0)
            line = [(other * SIDE + i) if along_x else (i * SIDE + other) for i in range(SIDE)]
            groups.append([prompt * ROLLOUTS + r for r in line])
    return groups


def exchange(blocks, phase):
    return lax.all_to_all(
        blocks, AXES, split_axis=0, concat_axis=0, axis_index_groups=line_groups(phase), tiled=True
    )


def shift(value, phase, by):
    pairs = []
    for line in line_groups(phase):
        pairs += [(line[i], line[(i + by) % SIDE]) for i in range(SIDE)]
    return lax.ppermute(value, AXES, pairs)


def place_in_plane():
    rollout = lax.axis_index("rollout")
    even = lax.axis_index("prompt") % 2 == 0
    return even, jnp.where(even, rollout // SIDE, rollout % SIDE)


def weights_kernel(w2_ref, w1_ref, out_ref, block, w1, sems):
    base = HID_OWN + IN_OWN
    from_w2 = pltpu.make_async_copy(w2_ref, block.at[0:HID_OWN], sems.at[0])
    from_w1 = pltpu.make_async_copy(w1_ref, w1, sems.at[1])
    from_w2.start()
    from_w1.start()
    block[base:W_ROWS, :] = jnp.zeros((TAIL, 256), BF16)
    from_w1.wait()
    block[HID_OWN:base, :] = w1[:, 0:256]
    at = 0
    for n, rows in enumerate(RUNS):
        block[base : base + rows, 64 * n : 64 * n + 64] = w1[at : at + rows, 256:HID_OWN]
        at += rows
    from_w2.wait()
    to_out = pltpu.make_async_copy(block, out_ref, sems.at[2])
    to_out.start()
    to_out.wait()


def pack_kernel(count_ref, ids_ref, grads_ref, out_ref, meta):
    even, _ = place_in_plane()
    ids = ids_ref[...]
    owner = (ids * 2731) >> 16
    turned = (owner & 3) * SIDE + (owner >> 2)
    place = jnp.where(even, turned, owner) * OWN + ids - owner * OWN + 1
    live = lax.broadcasted_iota(jnp.int32, (1, SLOTS), 1) < count_ref[0, 0]
    place = jnp.where(live, place, 0)
    meta[...] = jnp.zeros((8, COLS), F32)
    meta[2:3, 0:SLOTS] = (place >> 4).astype(F32)
    meta[3:4, 0:SLOTS] = (place & 15).astype(F32)
    codes = meta[...]
    zeros = jnp.zeros((8, COLS), F32)
    for k in range(ROLLOUTS):
        cols = pl.ds(k * COLS, COLS)
        out_ref[k, 0:48, :] = grads_ref[0:48, cols]
        two = jnp.concatenate([grads_ref[48:SLOTS, cols].astype(F32), zeros[0:6]], axis=0)
        out_ref[k, 48:64, :] = jnp.concatenate([two + codes, zeros], axis=0).astype(BF16)


def sum_kernel(recv_ref, out_ref):
    rows = (lax.broadcasted_iota(jnp.int32, (ROWS, 4 * PAD_SLOTS), 0) + 1).astype(F32)
    total = jnp.zeros((ROWS, COLS), F32)
    for g in range(ROLLOUTS // 4):
        codes = jnp.zeros((8, 4 * PAD_SLOTS), F32)
        for k in range(4):
            tile = recv_ref[4 * g + k, 48:64, 0 : 4 * PAD_SLOTS].astype(F32)[0:8]
            codes = codes + (pltpu.roll(tile, PAD_SLOTS * k, 1) if k else tile)
        row = codes[2:3] * 16.0 + codes[3:4]
        onehot = jnp.where(rows == row, 1.0, 0.0).astype(BF16)
        block = recv_ref[4 * g : 4 * g + 4].reshape(4 * PAD_SLOTS, COLS)
        total = total + jnp.dot(onehot, block, preferred_element_type=F32)
    value = total.astype(BF16)
    for k in range(SIDE):
        out_ref[k] = value


GATHERED = (
    (0, ((0, 0),)),
    (3, ((1, 0), (2, 2))),
    (1, ((4, 0), (3, 2))),
    (2, ((5, 0), (6, 2))),
)


def mlp_kernel(w_ref, *refs):
    sums, (slope_ref, out_ref, s, w2, w1, w1_tail, sems2, sems1) = refs[:7], refs[7:]
    even, second = place_in_plane()
    base = HID_OWN + IN_OWN
    copies, late = [], []
    for n, (offset, parts) in enumerate(GATHERED):
        other = lax.rem(second + offset, SIDE)
        by_row = pltpu.make_async_copy(w_ref.at[other, :, :, 0:HID_OWN], w2.at[n], sems2.at[n, 0])
        by_col = pltpu.make_async_copy(w_ref.at[:, other, :, 0:HID_OWN], w2.at[n], sems2.at[n, 0])
        pl.when(even)(by_row.start)
        pl.when(jnp.logical_not(even))(by_col.start)
        group = [by_row]
        for h, (operand, k) in enumerate(parts):
            count = SIDE // len(parts)
            copy = pltpu.make_async_copy(sums[operand], s.at[n, k : k + count], sems2.at[n, h + 1])
            copy.start()
            group.append(copy)
        copies.append(group)
    for q in range(SIDE):
        pair = [
            pltpu.make_async_copy(w_ref.at[q, :, :, HID_OWN:base], w1.at[q], sems1.at[q, 0]),
            pltpu.make_async_copy(w_ref.at[q, :, :, base:W_ROWS], w1_tail.at[q], sems1.at[q, 1]),
        ]
        for copy in pair:
            copy.start()
        late.append(pair)
    hidden = None
    for n in range(SIDE):
        for copy in copies[n]:
            copy.wait()
        for k in range(SIDE):
            block = s[n, k]
            part = dot_t(w2[n, k, 0], block[:, :W2_COLS]) + dot_t(w2[n, k, 1], block[:, W2_COLS:])
            hidden = part if hidden is None else hidden + part
    act = (hidden.T * slope_ref[...]).astype(BF16)
    width = HID // SIDE
    for q in range(SIDE):
        for copy in late[q]:
            copy.wait()
        fold = w1_tail[q]
        runs = [fold[:, :, :rows, 64 * n : 64 * n + 64] for n, rows in enumerate(RUNS)]
        tail = jnp.concatenate(runs, axis=2).reshape(width, 64)
        part = dot_t(act[:, 0:256], w1[q].reshape(width, 256)) + dot_t(act[:, 256:], tail)
        out_ref[:, width * q : width * (q + 1)] = part.astype(BF16)


def add_kernel(recv_ref, out_ref):
    total = recv_ref[0].astype(F32)
    for k in range(1, SIDE):
        total = total + recv_ref[k].astype(F32)
    out_ref[...] = total.astype(BF16)


def norm_kernel(recv_ref, patches_hbm, gain_hbm, out_ref, patches_ref, gain_ref, sems):
    copies = [
        pltpu.make_async_copy(patches_hbm, patches_ref, sems.at[0]),
        pltpu.make_async_copy(gain_hbm, gain_ref, sems.at[1]),
    ]
    for copy in copies:
        copy.start()
    sums = []
    for m in range(MERGE):
        cols = slice(m * VIT, (m + 1) * VIT)
        upstream = recv_ref[0, :, cols].astype(F32)
        for k in range(1, SIDE):
            upstream = upstream + recv_ref[k, :, cols].astype(F32)
        sums.append(upstream)
    for copy in copies:
        copy.wait()
    gain = gain_ref[...][None]
    for m in range(MERGE):
        cols = slice(m * VIT, (m + 1) * VIT)
        inputs = patches_ref[:, cols].astype(F32)
        scaled = sums[m] * gain
        inverse = lax.rsqrt(jnp.mean(inputs * inputs, axis=-1, keepdims=True) + 1e-06)
        inner = jnp.mean(scaled * inputs, axis=-1, keepdims=True)
        result = inverse * scaled - inputs * inverse * inverse * inverse * inner
        out_ref[:, cols] = result.astype(BF16)


VMEM = pl.BlockSpec(memory_space=pltpu.VMEM)
SMEM = pl.BlockSpec(memory_space=pltpu.SMEM)
ANY = pl.BlockSpec(memory_space=pl.ANY)


def call(kernel, shape, in_specs, flops=0, moved=0, vmem=16, scratch=(), fast=False, out_spec=VMEM):
    return pl.pallas_call(
        kernel,
        out_shape=pltpu.VMEM(shape, BF16) if fast else jax.ShapeDtypeStruct(shape, BF16),
        in_specs=in_specs,
        out_specs=out_spec,
        scratch_shapes=list(scratch),
        cost_estimate=pl.CostEstimate(flops=flops, bytes_accessed=moved, transcendentals=0),
        compiler_params=pltpu.CompilerParams(vmem_limit_bytes=vmem << 20),
    )


def pinned(value):
    return pltpu.with_memory_space_constraint(value, pltpu.HBM)


def per_device(row_grads, used_ids, used_count, pre_act, patches, ln_gain, w_fc2, w_fc1):
    weights = call(
        weights_kernel,
        (W_ROWS, 256),
        [ANY, ANY],
        out_spec=ANY,
        scratch=[
            pltpu.VMEM((W_ROWS, 256), BF16),
            pltpu.VMEM((IN_OWN, HID_OWN), BF16),
            pltpu.SemaphoreType.DMA((3,)),
        ],
    )(pinned(w_fc2), pinned(w_fc1))
    weights = lax.all_gather(weights, "prompt", axis=0, tiled=False)

    outgoing = call(
        pack_kernel, (ROLLOUTS, PAD_SLOTS, COLS), [SMEM, VMEM, VMEM], scratch=[pltpu.VMEM((8, COLS), F32)]
    )(used_count, used_ids[0], row_grads[0, 0])
    received = lax.all_to_all(outgoing, "rollout", split_axis=0, concat_axis=0, tiled=True)
    summed = call(sum_kernel, (SIDE, ROWS, COLS), [VMEM])(received)
    line = exchange(summed, 0)
    a1, b1 = shift(line[:2], 1, 1), shift(line[2:], 1, -1)
    a2, b2 = shift(line[2:], 1, 1), shift(line[:2], 1, -1)
    a3, b3 = shift(a1, 1, 1), shift(b1, 1, -1)

    even = lax.axis_index("prompt") % 2 == 0
    slope = gelu_slope(pre_act.astype(F32)).reshape(SIDE, SIDE, OWN, HID_OWN)
    slope = jnp.where(even, slope.transpose(1, 0, 2, 3), slope).reshape(ROWS, HID_OWN)
    weights = weights.reshape(SIDE, SIDE, 2, W_ROWS, 256)
    partial = pl.pallas_call(
        mlp_kernel,
        out_shape=pltpu.VMEM((ROWS, HID), BF16),
        in_specs=[ANY] * 8 + [VMEM],
        out_specs=VMEM,
        scratch_shapes=[
            pltpu.VMEM((SIDE, SIDE, ROWS, COLS), BF16),
            pltpu.VMEM((SIDE, SIDE, 2, HID_OWN, W2_COLS), BF16),
            pltpu.VMEM((SIDE, SIDE, 2, IN_OWN, 256), BF16),
            pltpu.VMEM((SIDE, SIDE, 2, TAIL, 256), BF16),
            pltpu.SemaphoreType.DMA((SIDE, 3)),
            pltpu.SemaphoreType.DMA((SIDE, 2)),
        ],
        cost_estimate=pl.CostEstimate(flops=3 << 30, bytes_accessed=16 << 20, transcendentals=0),
        compiler_params=pltpu.CompilerParams(vmem_limit_bytes=24 << 20),
    )(pinned(weights), line, a1, a2, b1, b2, a3, b3, slope)

    halfway = exchange(partial.reshape(SIDE, SIDE * OWN, HID), 0)
    halfway = call(add_kernel, (SIDE * OWN, HID), [VMEM], moved=5 << 20, fast=True)(halfway)
    last = exchange(halfway.reshape(SIDE, OWN, HID), 1)
    return call(
        norm_kernel,
        (OWN, HID),
        [VMEM, ANY, ANY],
        scratch=[
            pltpu.VMEM((OWN, HID), BF16),
            pltpu.VMEM((VIT,), F32),
            pltpu.SemaphoreType.DMA((2,)),
        ],
    )(last, pinned(patches), pinned(ln_gain))


def solution(mesh):
    return jax.shard_map(
        per_device,
        mesh=mesh,
        in_specs=(
            P("prompt", "rollout", None, None),
            P("prompt", "rollout", None),
            P("prompt", "rollout"),
            P("prompt", "rollout"),
            P(("prompt", "rollout"), None),
            P(),
            P("rollout", "prompt"),
            P("prompt", "rollout"),
        ),
        out_specs=P(("prompt", "rollout"), None),
        check_vma=False,
    )
```

```python
import jax
import jax.numpy as jnp
from jax import lax
from jax.experimental import pallas as pl
from jax.experimental.pallas import tpu as pltpu
from jax.sharding import PartitionSpec as P

VIT = 1280
MERGE = 4
PROMPTS = 32
ROLLOUTS = 16
SIDE = 4
SLOTS = 50
PAD_SLOTS = 64
OWN = 24
ROWS = OWN * ROLLOUTS
D_LLM = 8192
COLS = D_LLM // ROLLOUTS
HID = 5120
HID_OWN = HID // ROLLOUTS
IN_OWN = HID // PROMPTS
W2_COLS = D_LLM // PROMPTS
RUNS = (48, 48, 32, 32)
TAIL = 48
W_ROWS = HID_OWN + IN_OWN + TAIL
AXES = ("prompt", "rollout")
F32 = jnp.float32
BF16 = jnp.bfloat16


def gelu_slope(value):
    return (
        0.5 * (1.0 + jax.scipy.special.erf(value * 0.7071067811865476))
        + value * jnp.exp(-0.5 * value * value) * 0.3989422804014327
    )


def dot_t(left, right):
    return lax.dot_general(left, right, (((1,), (1,)), ((), ())), preferred_element_type=F32)


def line_groups(phase):
    groups = []
    for prompt in range(PROMPTS):
        for other in range(SIDE):
            along_x = (prompt % 2 == 0) == (phase == 0)
            line = [(other * SIDE + i) if along_x else (i * SIDE + other) for i in range(SIDE)]
            groups.append([prompt * ROLLOUTS + r for r in line])
    return groups


def exchange(blocks, phase):
    return lax.all_to_all(
        blocks, AXES, split_axis=0, concat_axis=0, axis_index_groups=line_groups(phase), tiled=True
    )


def shift(value, phase, by):
    pairs = []
    for line in line_groups(phase):
        pairs += [(line[i], line[(i + by) % SIDE]) for i in range(SIDE)]
    return lax.ppermute(value, AXES, pairs)


def place_in_plane():
    rollout = lax.axis_index("rollout")
    even = lax.axis_index("prompt") % 2 == 0
    return even, jnp.where(even, rollout // SIDE, rollout % SIDE)


def weights_kernel(w2_ref, w1_ref, out_ref, block, w1, sems):
    base = HID_OWN + IN_OWN
    from_w2 = pltpu.make_async_copy(w2_ref, block.at[0:HID_OWN], sems.at[0])
    from_w1 = pltpu.make_async_copy(w1_ref, w1, sems.at[1])
    from_w2.start()
    from_w1.start()
    block[base:W_ROWS, :] = jnp.zeros((TAIL, 256), BF16)
    from_w1.wait()
    block[HID_OWN:base, :] = w1[:, 0:256]
    at = 0
    for n, rows in enumerate(RUNS):
        block[base : base + rows, 64 * n : 64 * n + 64] = w1[at : at + rows, 256:HID_OWN]
        at += rows
    from_w2.wait()
    to_out = pltpu.make_async_copy(block, out_ref, sems.at[2])
    to_out.start()
    to_out.wait()


def pack_kernel(count_ref, ids_ref, grads_ref, out_ref, meta):
    even, _ = place_in_plane()
    ids = ids_ref[...]
    owner = (ids * 2731) >> 16
    turned = (owner & 3) * SIDE + (owner >> 2)
    place = jnp.where(even, turned, owner) * OWN + ids - owner * OWN + 1
    live = lax.broadcasted_iota(jnp.int32, (1, SLOTS), 1) < count_ref[0, 0]
    place = jnp.where(live, place, 0)
    meta[...] = jnp.zeros((8, COLS), F32)
    meta[2:3, 0:SLOTS] = (place >> 4).astype(F32)
    meta[3:4, 0:SLOTS] = (place & 15).astype(F32)
    codes = meta[...]
    zeros = jnp.zeros((8, COLS), F32)
    for k in range(ROLLOUTS):
        cols = pl.ds(k * COLS, COLS)
        out_ref[k, 0:48, :] = grads_ref[0:48, cols]
        two = jnp.concatenate([grads_ref[48:SLOTS, cols].astype(F32), zeros[0:6]], axis=0)
        out_ref[k, 48:64, :] = jnp.concatenate([two + codes, zeros], axis=0).astype(BF16)


def sum_kernel(recv_ref, out_ref):
    rows = (lax.broadcasted_iota(jnp.int32, (ROWS, 4 * PAD_SLOTS), 0) + 1).astype(F32)
    total = jnp.zeros((ROWS, COLS), F32)
    for g in range(ROLLOUTS // 4):
        codes = jnp.zeros((8, 4 * PAD_SLOTS), F32)
        for k in range(4):
            tile = recv_ref[4 * g + k, 48:64, 0 : 4 * PAD_SLOTS].astype(F32)[0:8]
            codes = codes + (pltpu.roll(tile, PAD_SLOTS * k, 1) if k else tile)
        row = codes[2:3] * 16.0 + codes[3:4]
        onehot = jnp.where(rows == row, 1.0, 0.0).astype(BF16)
        block = recv_ref[4 * g : 4 * g + 4].reshape(4 * PAD_SLOTS, COLS)
        total = total + jnp.dot(onehot, block, preferred_element_type=F32)
    value = total.astype(BF16)
    for k in range(SIDE):
        out_ref[k] = value


GATHERED = (
    (0, ((0, 0),)),
    (3, ((1, 0), (2, 2))),
    (1, ((4, 0), (3, 2))),
    (2, ((5, 0), (6, 2))),
)


def mlp_kernel(w_ref, *refs):
    sums, (slope_ref, out_ref, s, w2, w1, w1_tail, sems2, sems1) = refs[:7], refs[7:]
    even, second = place_in_plane()
    base = HID_OWN + IN_OWN
    copies, late = [], []
    for n, (offset, parts) in enumerate(GATHERED):
        other = lax.rem(second + offset, SIDE)
        count = SIDE // len(parts)
        for h, (operand, k) in enumerate(parts):
            span = slice(k, k + count)
            by_row = pltpu.make_async_copy(w_ref.at[other, span, :, 0:HID_OWN], w2.at[n, span], sems2.at[n, h])
            by_col = pltpu.make_async_copy(w_ref.at[span, other, :, 0:HID_OWN], w2.at[n, span], sems2.at[n, h])
            pl.when(even)(by_row.start)
            pl.when(jnp.logical_not(even))(by_col.start)
            copy = pltpu.make_async_copy(sums[operand], s.at[n, span], sems2.at[n, h + 2])
            copy.start()
            copies.append((n, span, by_row, copy))
    for q in range(SIDE):
        pair = [
            pltpu.make_async_copy(w_ref.at[q, :, :, HID_OWN:base], w1.at[q], sems1.at[q, 0]),
            pltpu.make_async_copy(w_ref.at[q, :, :, base:W_ROWS], w1_tail.at[q], sems1.at[q, 1]),
        ]
        for copy in pair:
            copy.start()
        late.append(pair)
    hidden = None
    for n, span, *group in copies:
        for copy in group:
            copy.wait()
        for k in range(span.start, span.stop):
            block = s[n, k]
            part = dot_t(w2[n, k, 0], block[:, :W2_COLS]) + dot_t(w2[n, k, 1], block[:, W2_COLS:])
            hidden = part if hidden is None else hidden + part
    act = (hidden.T * slope_ref[...]).astype(BF16)
    width = HID // SIDE
    for q in range(SIDE):
        for copy in late[q]:
            copy.wait()
        fold = w1_tail[q]
        runs = [fold[:, :, :rows, 64 * n : 64 * n + 64] for n, rows in enumerate(RUNS)]
        tail = jnp.concatenate(runs, axis=2).reshape(width, 64)
        part = dot_t(act[:, 0:256], w1[q].reshape(width, 256)) + dot_t(act[:, 256:], tail)
        out_ref[:, width * q : width * (q + 1)] = part.astype(BF16)


def add_kernel(recv_ref, patches_ref, gain_ref, out_ref, near_patches_ref, near_gain_ref):
    total = recv_ref[0].astype(F32)
    for k in range(1, SIDE):
        total = total + recv_ref[k].astype(F32)
    out_ref[...] = total.astype(BF16)
    near_patches_ref[...] = patches_ref[...]
    near_gain_ref[...] = gain_ref[...]


def norm_kernel(recv_ref, patches_ref, gain_ref, out_ref):
    sums = []
    for m in range(MERGE):
        cols = slice(m * VIT, (m + 1) * VIT)
        upstream = recv_ref[0, :, cols].astype(F32)
        for k in range(1, SIDE):
            upstream = upstream + recv_ref[k, :, cols].astype(F32)
        sums.append(upstream)
    gain = gain_ref[...][None]
    for m in range(MERGE):
        cols = slice(m * VIT, (m + 1) * VIT)
        inputs = patches_ref[:, cols].astype(F32)
        scaled = sums[m] * gain
        inverse = lax.rsqrt(jnp.mean(inputs * inputs, axis=-1, keepdims=True) + 1e-06)
        inner = jnp.mean(scaled * inputs, axis=-1, keepdims=True)
        result = inverse * scaled - inputs * inverse * inverse * inverse * inner
        out_ref[:, cols] = result.astype(BF16)


VMEM = pl.BlockSpec(memory_space=pltpu.VMEM)
SMEM = pl.BlockSpec(memory_space=pltpu.SMEM)
ANY = pl.BlockSpec(memory_space=pl.ANY)


def call(kernel, shape, in_specs, flops=0, moved=0, vmem=16, scratch=(), fast=False, out_spec=VMEM):
    return pl.pallas_call(
        kernel,
        out_shape=pltpu.VMEM(shape, BF16) if fast else jax.ShapeDtypeStruct(shape, BF16),
        in_specs=in_specs,
        out_specs=out_spec,
        scratch_shapes=list(scratch),
        cost_estimate=pl.CostEstimate(flops=flops, bytes_accessed=moved, transcendentals=0),
        compiler_params=pltpu.CompilerParams(vmem_limit_bytes=vmem << 20),
    )


def pinned(value):
    return pltpu.with_memory_space_constraint(value, pltpu.HBM)


def per_device(row_grads, used_ids, used_count, pre_act, patches, ln_gain, w_fc2, w_fc1):
    weights = call(
        weights_kernel,
        (W_ROWS, 256),
        [ANY, ANY],
        out_spec=ANY,
        scratch=[
            pltpu.VMEM((W_ROWS, 256), BF16),
            pltpu.VMEM((IN_OWN, HID_OWN), BF16),
            pltpu.SemaphoreType.DMA((3,)),
        ],
    )(pinned(w_fc2), pinned(w_fc1))
    weights = lax.all_gather(weights, "prompt", axis=0, tiled=False)

    outgoing = call(
        pack_kernel, (ROLLOUTS, PAD_SLOTS, COLS), [SMEM, VMEM, VMEM], scratch=[pltpu.VMEM((8, COLS), F32)]
    )(used_count, used_ids[0], row_grads[0, 0])
    received = lax.all_to_all(outgoing, "rollout", split_axis=0, concat_axis=0, tiled=True)
    summed = call(sum_kernel, (SIDE, ROWS, COLS), [VMEM])(received)
    line = exchange(summed, 0)
    a1, b1 = shift(line[:2], 1, 1), shift(line[2:], 1, -1)
    a2, b2 = shift(line[2:], 1, 1), shift(line[:2], 1, -1)
    a3, b3 = shift(a1, 1, 1), shift(b1, 1, -1)

    even = lax.axis_index("prompt") % 2 == 0
    slope = gelu_slope(pre_act.astype(F32)).reshape(SIDE, SIDE, OWN, HID_OWN)
    slope = jnp.where(even, slope.transpose(1, 0, 2, 3), slope).reshape(ROWS, HID_OWN)
    weights = weights.reshape(SIDE, SIDE, 2, W_ROWS, 256)
    partial = pl.pallas_call(
        mlp_kernel,
        out_shape=pltpu.VMEM((ROWS, HID), BF16),
        in_specs=[ANY] * 8 + [VMEM],
        out_specs=VMEM,
        scratch_shapes=[
            pltpu.VMEM((SIDE, SIDE, ROWS, COLS), BF16),
            pltpu.VMEM((SIDE, SIDE, 2, HID_OWN, W2_COLS), BF16),
            pltpu.VMEM((SIDE, SIDE, 2, IN_OWN, 256), BF16),
            pltpu.VMEM((SIDE, SIDE, 2, TAIL, 256), BF16),
            pltpu.SemaphoreType.DMA((SIDE, 4)),
            pltpu.SemaphoreType.DMA((SIDE, 2)),
        ],
        cost_estimate=pl.CostEstimate(flops=3 << 30, bytes_accessed=16 << 20, transcendentals=0),
        compiler_params=pltpu.CompilerParams(vmem_limit_bytes=24 << 20),
    )(pinned(weights), line, a1, a2, b1, b2, a3, b3, slope)

    halfway = exchange(partial.reshape(SIDE, SIDE * OWN, HID), 0)
    halfway, near_patches, near_gain = pl.pallas_call(
        add_kernel,
        out_shape=[pltpu.VMEM((SIDE * OWN, HID), BF16), pltpu.VMEM((OWN, HID), BF16), pltpu.VMEM((VIT,), F32)],
        in_specs=[VMEM] * 3,
        out_specs=[VMEM] * 3,
        compiler_params=pltpu.CompilerParams(vmem_limit_bytes=16 << 20),
    )(halfway, patches, ln_gain)
    last = exchange(halfway.reshape(SIDE, OWN, HID), 1)
    return call(norm_kernel, (OWN, HID), [VMEM] * 3)(last, near_patches, near_gain)


def solution(mesh):
    return jax.shard_map(
        per_device,
        mesh=mesh,
        in_specs=(
            P("prompt", "rollout", None, None),
            P("prompt", "rollout", None),
            P("prompt", "rollout"),
            P("prompt", "rollout"),
            P(("prompt", "rollout"), None),
            P(),
            P("rollout", "prompt"),
            P("prompt", "rollout"),
        ),
        out_specs=P(("prompt", "rollout"), None),
        check_vma=False,
    )
```

```python
import jax
import jax.numpy as jnp
from jax import lax
from jax.experimental import pallas as pl
from jax.experimental.pallas import tpu as pltpu
from jax.sharding import PartitionSpec as P

VIT = 1280
MERGE = 4
PROMPTS = 32
ROLLOUTS = 16
SIDE = 4
SLOTS = 50
PAD_SLOTS = 64
OWN = 24
ROWS = OWN * ROLLOUTS
D_LLM = 8192
COLS = D_LLM // ROLLOUTS
HID = 5120
HID_OWN = HID // ROLLOUTS
IN_OWN = HID // PROMPTS
W2_COLS = D_LLM // PROMPTS
RUNS = (48, 48, 32, 32)
TAIL = 48
W_ROWS = HID_OWN + IN_OWN + TAIL
AXES = ("prompt", "rollout")
F32 = jnp.float32
BF16 = jnp.bfloat16


def gelu_slope(value):
    return (
        0.5 * (1.0 + jax.scipy.special.erf(value * 0.7071067811865476))
        + value * jnp.exp(-0.5 * value * value) * 0.3989422804014327
    )


def dot_t(left, right):
    return lax.dot_general(left, right, (((1,), (1,)), ((), ())), preferred_element_type=F32)


def line_groups(phase):
    groups = []
    for prompt in range(PROMPTS):
        for other in range(SIDE):
            along_x = (prompt % 2 == 1) == (phase == 0)
            line = [(other * SIDE + i) if along_x else (i * SIDE + other) for i in range(SIDE)]
            groups.append([prompt * ROLLOUTS + r for r in line])
    return groups


def exchange(blocks, phase):
    return lax.all_to_all(
        blocks, AXES, split_axis=0, concat_axis=0, axis_index_groups=line_groups(phase), tiled=True
    )


def shift(value, phase, by):
    pairs = []
    for line in line_groups(phase):
        pairs += [(line[i], line[(i + by) % SIDE]) for i in range(SIDE)]
    return lax.ppermute(value, AXES, pairs)


def place_in_plane():
    rollout = lax.axis_index("rollout")
    x_first = lax.axis_index("prompt") % 2 == 1
    return x_first, jnp.where(x_first, rollout // SIDE, rollout % SIDE)


def weights_kernel(w2_ref, w1_ref, out_ref, block, w1, sems):
    base = HID_OWN + IN_OWN
    from_w2 = pltpu.make_async_copy(w2_ref, block.at[0:HID_OWN], sems.at[0])
    from_w1 = pltpu.make_async_copy(w1_ref, w1, sems.at[1])
    from_w2.start()
    from_w1.start()
    block[base:W_ROWS, :] = jnp.zeros((TAIL, 256), BF16)
    from_w1.wait()
    block[HID_OWN:base, :] = w1[:, 0:256]
    at = 0
    for n, rows in enumerate(RUNS):
        block[base : base + rows, 64 * n : 64 * n + 64] = w1[at : at + rows, 256:HID_OWN]
        at += rows
    from_w2.wait()
    to_out = pltpu.make_async_copy(block, out_ref, sems.at[2])
    to_out.start()
    to_out.wait()


def pack_kernel(count_ref, ids_ref, grads_ref, out_ref, meta):
    x_first, _ = place_in_plane()
    ids = ids_ref[...]
    owner = (ids * 2731) >> 16
    turned = (owner & 3) * SIDE + (owner >> 2)
    place = jnp.where(x_first, turned, owner) * OWN + ids - owner * OWN + 1
    live = lax.broadcasted_iota(jnp.int32, (1, SLOTS), 1) < count_ref[0, 0]
    place = jnp.where(live, place, 0)
    meta[...] = jnp.zeros((8, COLS), F32)
    meta[2:3, 0:SLOTS] = (place >> 4).astype(F32)
    meta[3:4, 0:SLOTS] = (place & 15).astype(F32)
    codes = meta[...]
    zeros = jnp.zeros((8, COLS), F32)
    for k in range(ROLLOUTS):
        cols = pl.ds(k * COLS, COLS)
        out_ref[k, 0:48, :] = grads_ref[0:48, cols]
        two = jnp.concatenate([grads_ref[48:SLOTS, cols].astype(F32), zeros[0:6]], axis=0)
        out_ref[k, 48:64, :] = jnp.concatenate([two + codes, zeros], axis=0).astype(BF16)


def sum_kernel(recv_ref, out_ref):
    rows = (lax.broadcasted_iota(jnp.int32, (ROWS, 4 * PAD_SLOTS), 0) + 1).astype(F32)
    total = jnp.zeros((ROWS, COLS), F32)
    for g in range(ROLLOUTS // 4):
        codes = jnp.zeros((8, 4 * PAD_SLOTS), F32)
        for k in range(4):
            tile = recv_ref[4 * g + k, 48:64, 0 : 4 * PAD_SLOTS].astype(F32)[0:8]
            codes = codes + (pltpu.roll(tile, PAD_SLOTS * k, 1) if k else tile)
        row = codes[2:3] * 16.0 + codes[3:4]
        onehot = jnp.where(rows == row, 1.0, 0.0).astype(BF16)
        block = recv_ref[4 * g : 4 * g + 4].reshape(4 * PAD_SLOTS, COLS)
        total = total + jnp.dot(onehot, block, preferred_element_type=F32)
    value = total.astype(BF16)
    for k in range(SIDE):
        out_ref[k] = value


GATHERED = (
    (0, ((0, 0),)),
    (3, ((1, 0), (2, 2))),
    (1, ((4, 0), (3, 2))),
    (2, ((5, 0), (6, 2))),
)


def mlp_kernel(w_ref, *refs):
    sums, (slope_ref, out_ref, s, w2, w1, w1_tail, sems2, sems1) = refs[:7], refs[7:]
    x_first, second = place_in_plane()
    base = HID_OWN + IN_OWN
    copies, late = [], []
    for n, (offset, parts) in enumerate(GATHERED):
        other = lax.rem(second + offset, SIDE)
        count = SIDE // len(parts)
        for h, (operand, k) in enumerate(parts):
            span = slice(k, k + count)
            by_row = pltpu.make_async_copy(w_ref.at[other, span, :, 0:HID_OWN], w2.at[n, span], sems2.at[n, h])
            by_col = pltpu.make_async_copy(w_ref.at[span, other, :, 0:HID_OWN], w2.at[n, span], sems2.at[n, h])
            pl.when(x_first)(by_row.start)
            pl.when(jnp.logical_not(x_first))(by_col.start)
            copy = pltpu.make_async_copy(sums[operand], s.at[n, span], sems2.at[n, h + 2])
            copy.start()
            copies.append((n, span, by_row, copy))
    for q in range(SIDE):
        pair = [
            pltpu.make_async_copy(w_ref.at[q, :, :, HID_OWN:base], w1.at[q], sems1.at[q, 0]),
            pltpu.make_async_copy(w_ref.at[q, :, :, base:W_ROWS], w1_tail.at[q], sems1.at[q, 1]),
        ]
        for copy in pair:
            copy.start()
        late.append(pair)
    hidden = None
    for n, span, *group in copies:
        for copy in group:
            copy.wait()
        for k in range(span.start, span.stop):
            block = s[n, k]
            part = dot_t(w2[n, k, 0], block[:, :W2_COLS]) + dot_t(w2[n, k, 1], block[:, W2_COLS:])
            hidden = part if hidden is None else hidden + part
    act = (hidden.T * slope_ref[...]).astype(BF16)
    width = HID // SIDE
    for q in range(SIDE):
        for copy in late[q]:
            copy.wait()
        fold = w1_tail[q]
        runs = [fold[:, :, :rows, 64 * n : 64 * n + 64] for n, rows in enumerate(RUNS)]
        tail = jnp.concatenate(runs, axis=2).reshape(width, 64)
        part = dot_t(act[:, 0:256], w1[q].reshape(width, 256)) + dot_t(act[:, 256:], tail)
        out_ref[:, width * q : width * (q + 1)] = part.astype(BF16)


def add_kernel(recv_ref, patches_ref, gain_ref, out_ref, near_patches_ref, near_gain_ref):
    total = recv_ref[0].astype(F32)
    for k in range(1, SIDE):
        total = total + recv_ref[k].astype(F32)
    out_ref[...] = total.astype(BF16)
    near_patches_ref[...] = patches_ref[...]
    near_gain_ref[...] = gain_ref[...]


def norm_kernel(recv_ref, patches_ref, gain_ref, out_ref):
    sums = []
    for m in range(MERGE):
        cols = slice(m * VIT, (m + 1) * VIT)
        upstream = recv_ref[0, :, cols].astype(F32)
        for k in range(1, SIDE):
            upstream = upstream + recv_ref[k, :, cols].astype(F32)
        sums.append(upstream)
    gain = gain_ref[...][None]
    for m in range(MERGE):
        cols = slice(m * VIT, (m + 1) * VIT)
        inputs = patches_ref[:, cols].astype(F32)
        scaled = sums[m] * gain
        inverse = lax.rsqrt(jnp.mean(inputs * inputs, axis=-1, keepdims=True) + 1e-06)
        inner = jnp.mean(scaled * inputs, axis=-1, keepdims=True)
        result = inverse * scaled - inputs * inverse * inverse * inverse * inner
        out_ref[:, cols] = result.astype(BF16)


VMEM = pl.BlockSpec(memory_space=pltpu.VMEM)
SMEM = pl.BlockSpec(memory_space=pltpu.SMEM)
ANY = pl.BlockSpec(memory_space=pl.ANY)


def call(kernel, shape, in_specs, flops=0, moved=0, vmem=16, scratch=(), fast=False, out_spec=VMEM):
    return pl.pallas_call(
        kernel,
        out_shape=pltpu.VMEM(shape, BF16) if fast else jax.ShapeDtypeStruct(shape, BF16),
        in_specs=in_specs,
        out_specs=out_spec,
        scratch_shapes=list(scratch),
        cost_estimate=pl.CostEstimate(flops=flops, bytes_accessed=moved, transcendentals=0),
        compiler_params=pltpu.CompilerParams(vmem_limit_bytes=vmem << 20),
    )


def pinned(value):
    return pltpu.with_memory_space_constraint(value, pltpu.HBM)


def per_device(row_grads, used_ids, used_count, pre_act, patches, ln_gain, w_fc2, w_fc1):
    weights = call(
        weights_kernel,
        (W_ROWS, 256),
        [ANY, ANY],
        out_spec=ANY,
        scratch=[
            pltpu.VMEM((W_ROWS, 256), BF16),
            pltpu.VMEM((IN_OWN, HID_OWN), BF16),
            pltpu.SemaphoreType.DMA((3,)),
        ],
    )(pinned(w_fc2), pinned(w_fc1))
    weights = lax.all_gather(weights, "prompt", axis=0, tiled=False)

    outgoing = call(
        pack_kernel, (ROLLOUTS, PAD_SLOTS, COLS), [SMEM, VMEM, VMEM], scratch=[pltpu.VMEM((8, COLS), F32)]
    )(used_count, used_ids[0], row_grads[0, 0])
    received = lax.all_to_all(outgoing, "rollout", split_axis=0, concat_axis=0, tiled=True)
    summed = call(sum_kernel, (SIDE, ROWS, COLS), [VMEM])(received)
    line = exchange(summed, 0)
    a1, b1 = shift(line[:2], 1, 1), shift(line[2:], 1, -1)
    a2, b2 = shift(line[2:], 1, 1), shift(line[:2], 1, -1)
    a3, b3 = shift(a1, 1, 1), shift(b1, 1, -1)

    x_first = lax.axis_index("prompt") % 2 == 1
    slope = gelu_slope(pre_act.astype(F32)).reshape(SIDE, SIDE, OWN, HID_OWN)
    slope = jnp.where(x_first, slope.transpose(1, 0, 2, 3), slope).reshape(ROWS, HID_OWN)
    weights = weights.reshape(SIDE, SIDE, 2, W_ROWS, 256)
    partial = pl.pallas_call(
        mlp_kernel,
        out_shape=pltpu.VMEM((ROWS, HID), BF16),
        in_specs=[ANY] * 8 + [VMEM],
        out_specs=VMEM,
        scratch_shapes=[
            pltpu.VMEM((SIDE, SIDE, ROWS, COLS), BF16),
            pltpu.VMEM((SIDE, SIDE, 2, HID_OWN, W2_COLS), BF16),
            pltpu.VMEM((SIDE, SIDE, 2, IN_OWN, 256), BF16),
            pltpu.VMEM((SIDE, SIDE, 2, TAIL, 256), BF16),
            pltpu.SemaphoreType.DMA((SIDE, 4)),
            pltpu.SemaphoreType.DMA((SIDE, 2)),
        ],
        cost_estimate=pl.CostEstimate(flops=3 << 30, bytes_accessed=16 << 20, transcendentals=0),
        compiler_params=pltpu.CompilerParams(vmem_limit_bytes=24 << 20),
    )(pinned(weights), line, a1, a2, b1, b2, a3, b3, slope)

    halfway = exchange(partial.reshape(SIDE, SIDE * OWN, HID), 0)
    halfway, near_patches, near_gain = pl.pallas_call(
        add_kernel,
        out_shape=[pltpu.VMEM((SIDE * OWN, HID), BF16), pltpu.VMEM((OWN, HID), BF16), pltpu.VMEM((VIT,), F32)],
        in_specs=[VMEM] * 3,
        out_specs=[VMEM] * 3,
        compiler_params=pltpu.CompilerParams(vmem_limit_bytes=16 << 20),
    )(halfway, patches, ln_gain)
    last = exchange(halfway.reshape(SIDE, OWN, HID), 1)
    return call(norm_kernel, (OWN, HID), [VMEM] * 3)(last, near_patches, near_gain)


def solution(mesh):
    return jax.shard_map(
        per_device,
        mesh=mesh,
        in_specs=(
            P("prompt", "rollout", None, None),
            P("prompt", "rollout", None),
            P("prompt", "rollout"),
            P("prompt", "rollout"),
            P(("prompt", "rollout"), None),
            P(),
            P("rollout", "prompt"),
            P("prompt", "rollout"),
        ),
        out_specs=P(("prompt", "rollout"), None),
        check_vma=False,
    )
```

```python
import jax
import jax.numpy as jnp
from jax import lax
from jax.experimental import pallas as pl
from jax.experimental.pallas import tpu as pltpu
from jax.sharding import PartitionSpec as P

VIT = 1280
MERGE = 4
PROMPTS = 32
ROLLOUTS = 16
SIDE = 4
SLOTS = 50
PAD_SLOTS = 64
OWN = 24
ROWS = OWN * ROLLOUTS
D_LLM = 8192
COLS = D_LLM // ROLLOUTS
HID = 5120
HID_OWN = HID // ROLLOUTS
IN_OWN = HID // PROMPTS
W2_COLS = D_LLM // PROMPTS
RUNS = (48, 48, 32, 32)
TAIL = 48
W_ROWS = HID_OWN + IN_OWN + TAIL
LINE_ROWS = SIDE * OWN
AXES = ("prompt", "rollout")
F32 = jnp.float32
BF16 = jnp.bfloat16


def gelu_slope(value):
    return (
        0.5 * (1.0 + jax.scipy.special.erf(value * 0.7071067811865476))
        + value * jnp.exp(-0.5 * value * value) * 0.3989422804014327
    )


def dot_t(left, right):
    return lax.dot_general(left, right, (((1,), (1,)), ((), ())), preferred_element_type=F32)


def line_groups(phase):
    groups = []
    for prompt in range(PROMPTS):
        for other in range(SIDE):
            along_x = (prompt % 2 == 0) == (phase == 0)
            line = [(other * SIDE + i) if along_x else (i * SIDE + other) for i in range(SIDE)]
            groups.append([prompt * ROLLOUTS + r for r in line])
    return groups


def exchange(blocks, phase):
    return lax.all_to_all(
        blocks, AXES, split_axis=0, concat_axis=0, axis_index_groups=line_groups(phase), tiled=True
    )


def shift(value, phase, by):
    pairs = []
    for line in line_groups(phase):
        pairs += [(line[i], line[(i + by) % SIDE]) for i in range(SIDE)]
    return lax.ppermute(value, AXES, pairs)


def place_in_plane():
    rollout = lax.axis_index("rollout")
    even = lax.axis_index("prompt") % 2 == 0
    y, x = rollout // SIDE, rollout % SIDE
    return even, jnp.where(even, x, y), jnp.where(even, y, x)


def weights_kernel(w2_ref, w1_ref, out_ref, block, w1, sems):
    base = HID_OWN + IN_OWN
    from_w2 = pltpu.make_async_copy(w2_ref, block.at[0:HID_OWN], sems.at[0])
    from_w1 = pltpu.make_async_copy(w1_ref, w1, sems.at[1])
    from_w2.start()
    from_w1.start()
    block[base:W_ROWS, :] = jnp.zeros((TAIL, 256), BF16)
    from_w1.wait()
    block[HID_OWN:base, :] = w1[:, 0:256]
    at = 0
    for n, rows in enumerate(RUNS):
        block[base : base + rows, 64 * n : 64 * n + 64] = w1[at : at + rows, 256:HID_OWN]
        at += rows
    from_w2.wait()
    to_out = pltpu.make_async_copy(block, out_ref, sems.at[2])
    to_out.start()
    to_out.wait()


def pack_kernel(count_ref, ids_ref, grads_ref, out_ref, meta):
    even, _, _ = place_in_plane()
    ids = ids_ref[...]
    owner = (ids * 2731) >> 16
    turned = (owner & 3) * SIDE + (owner >> 2)
    place = jnp.where(even, turned, owner) * OWN + ids - owner * OWN + 1
    live = lax.broadcasted_iota(jnp.int32, (1, SLOTS), 1) < count_ref[0, 0]
    place = jnp.where(live, place, 0)
    meta[...] = jnp.zeros((8, COLS), F32)
    meta[2:3, 0:SLOTS] = (place >> 4).astype(F32)
    meta[3:4, 0:SLOTS] = (place & 15).astype(F32)
    codes = meta[...]
    zeros = jnp.zeros((8, COLS), F32)
    for k in range(ROLLOUTS):
        cols = pl.ds(k * COLS, COLS)
        out_ref[k, 0:48, :] = grads_ref[0:48, cols]
        two = jnp.concatenate([grads_ref[48:SLOTS, cols].astype(F32), zeros[0:6]], axis=0)
        out_ref[k, 48:64, :] = jnp.concatenate([two + codes, zeros], axis=0).astype(BF16)


def sum_kernel(recv_ref, out_ref):
    rows = (lax.broadcasted_iota(jnp.int32, (ROWS, 4 * PAD_SLOTS), 0) + 1).astype(F32)
    total = jnp.zeros((ROWS, COLS), F32)
    for g in range(ROLLOUTS // 4):
        codes = jnp.zeros((8, 4 * PAD_SLOTS), F32)
        for k in range(4):
            tile = recv_ref[4 * g + k, 48:64, 0 : 4 * PAD_SLOTS].astype(F32)[0:8]
            codes = codes + (pltpu.roll(tile, PAD_SLOTS * k, 1) if k else tile)
        row = codes[2:3] * 16.0 + codes[3:4]
        onehot = jnp.where(rows == row, 1.0, 0.0).astype(BF16)
        block = recv_ref[4 * g : 4 * g + 4].reshape(4 * PAD_SLOTS, COLS)
        total = total + jnp.dot(onehot, block, preferred_element_type=F32)
    value = total.astype(BF16)
    for k in range(SIDE):
        out_ref[k] = value


GATHERED = (
    (0, ((0, 0),)),
    (3, ((1, 0), (2, 2))),
    (1, ((4, 0), (3, 2))),
    (2, ((5, 0), (6, 2))),
)


def mlp_kernel(w_ref, *refs):
    sums, outs = refs[:7], refs[8:13]
    slope_ref, (s, w2, w1, w1_tail, act_ref, sems2, sems1) = refs[7], refs[13:]
    even, first, second = place_in_plane()
    base = HID_OWN + IN_OWN
    copies, late = [], []
    for n, (offset, parts) in enumerate(GATHERED):
        other = lax.rem(second + offset, SIDE)
        count = SIDE // len(parts)
        for h, (operand, k) in enumerate(parts):
            span = slice(k, k + count)
            by_row = pltpu.make_async_copy(w_ref.at[other, span, :, 0:HID_OWN], w2.at[n, span], sems2.at[n, h])
            by_col = pltpu.make_async_copy(w_ref.at[span, other, :, 0:HID_OWN], w2.at[n, span], sems2.at[n, h])
            pl.when(even)(by_row.start)
            pl.when(jnp.logical_not(even))(by_col.start)
            copy = pltpu.make_async_copy(sums[operand], s.at[n, span], sems2.at[n, h + 2])
            copy.start()
            copies.append((n, span, by_row, copy))
    for q in range(SIDE):
        pair = [
            pltpu.make_async_copy(w_ref.at[q, :, :, HID_OWN:base], w1.at[q], sems1.at[q, 0]),
            pltpu.make_async_copy(w_ref.at[q, :, :, base:W_ROWS], w1_tail.at[q], sems1.at[q, 1]),
        ]
        for copy in pair:
            copy.start()
        late.append(pair)
    hidden = None
    for n, span, *group in copies:
        for copy in group:
            copy.wait()
        for k in range(span.start, span.stop):
            block = s[n, k]
            part = dot_t(w2[n, k, 0], block[:, :W2_COLS]) + dot_t(w2[n, k, 1], block[:, W2_COLS:])
            hidden = part if hidden is None else hidden + part
    act_ref[...] = (hidden.T * slope_ref[...]).astype(BF16)
    blocks = []
    for by in (2, 1, 3, 0):
        at = pl.multiple_of(lax.rem(first + by, SIDE) * LINE_ROWS, LINE_ROWS)
        blocks.append(act_ref[pl.ds(at, LINE_ROWS), :])
    act = jnp.concatenate(blocks, axis=0)
    width = HID // SIDE
    for q in range(SIDE):
        for copy in late[q]:
            copy.wait()
        fold = w1_tail[q]
        runs = [fold[:, :, :rows, 64 * n : 64 * n + 64] for n, rows in enumerate(RUNS)]
        tail = jnp.concatenate(runs, axis=2).reshape(width, 64)
        part = dot_t(act[:, 0:256], w1[q].reshape(width, 256)) + dot_t(act[:, 256:], tail)
        at = 0
        for out_ref in outs:
            rows = out_ref.shape[0]
            out_ref[:, width * q : width * (q + 1)] = part[at : at + rows].astype(BF16)
            at += rows


def relay_kernel(right_ref, left_ref, low_ref, high_ref, right_out, left_out):
    half = LINE_ROWS // 2
    right_out[0:half] = (right_ref[0:half].astype(F32) + low_ref[...].astype(F32)).astype(BF16)
    right_out[half:] = right_ref[half:]
    left_out[0:half] = left_ref[0:half]
    left_out[half:] = (left_ref[half:].astype(F32) + high_ref[...].astype(F32)).astype(BF16)


def add_kernel(own_ref, a_ref, b_ref, patches_ref, gain_ref, out_ref, near_patches_ref, near_gain_ref):
    total = own_ref[...].astype(F32) + a_ref[...].astype(F32) + b_ref[...].astype(F32)
    out_ref[...] = total.astype(BF16)
    near_patches_ref[...] = patches_ref[...]
    near_gain_ref[...] = gain_ref[...]


def norm_kernel(recv_ref, patches_ref, gain_ref, out_ref):
    sums = []
    for m in range(MERGE):
        cols = slice(m * VIT, (m + 1) * VIT)
        upstream = recv_ref[0, :, cols].astype(F32)
        for k in range(1, SIDE):
            upstream = upstream + recv_ref[k, :, cols].astype(F32)
        sums.append(upstream)
    gain = gain_ref[...][None]
    for m in range(MERGE):
        cols = slice(m * VIT, (m + 1) * VIT)
        inputs = patches_ref[:, cols].astype(F32)
        scaled = sums[m] * gain
        inverse = lax.rsqrt(jnp.mean(inputs * inputs, axis=-1, keepdims=True) + 1e-06)
        inner = jnp.mean(scaled * inputs, axis=-1, keepdims=True)
        result = inverse * scaled - inputs * inverse * inverse * inverse * inner
        out_ref[:, cols] = result.astype(BF16)


VMEM = pl.BlockSpec(memory_space=pltpu.VMEM)
SMEM = pl.BlockSpec(memory_space=pltpu.SMEM)
ANY = pl.BlockSpec(memory_space=pl.ANY)


def call(kernel, shape, in_specs, flops=0, moved=0, vmem=16, scratch=(), fast=False, out_spec=VMEM):
    return pl.pallas_call(
        kernel,
        out_shape=pltpu.VMEM(shape, BF16) if fast else jax.ShapeDtypeStruct(shape, BF16),
        in_specs=in_specs,
        out_specs=out_spec,
        scratch_shapes=list(scratch),
        cost_estimate=pl.CostEstimate(flops=flops, bytes_accessed=moved, transcendentals=0),
        compiler_params=pltpu.CompilerParams(vmem_limit_bytes=vmem << 20),
    )


def pinned(value):
    return pltpu.with_memory_space_constraint(value, pltpu.HBM)


def per_device(row_grads, used_ids, used_count, pre_act, patches, ln_gain, w_fc2, w_fc1):
    weights = call(
        weights_kernel,
        (W_ROWS, 256),
        [ANY, ANY],
        out_spec=ANY,
        scratch=[
            pltpu.VMEM((W_ROWS, 256), BF16),
            pltpu.VMEM((IN_OWN, HID_OWN), BF16),
            pltpu.SemaphoreType.DMA((3,)),
        ],
    )(pinned(w_fc2), pinned(w_fc1))
    weights = lax.all_gather(weights, "prompt", axis=0, tiled=False)

    outgoing = call(
        pack_kernel, (ROLLOUTS, PAD_SLOTS, COLS), [SMEM, VMEM, VMEM], scratch=[pltpu.VMEM((8, COLS), F32)]
    )(used_count, used_ids[0], row_grads[0, 0])
    received = lax.all_to_all(outgoing, "rollout", split_axis=0, concat_axis=0, tiled=True)
    summed = call(sum_kernel, (SIDE, ROWS, COLS), [VMEM])(received)
    line = exchange(summed, 0)
    a1, b1 = shift(line[:2], 1, 1), shift(line[2:], 1, -1)
    a2, b2 = shift(line[2:], 1, 1), shift(line[:2], 1, -1)
    a3, b3 = shift(a1, 1, 1), shift(b1, 1, -1)

    even = lax.axis_index("prompt") % 2 == 0
    slope = gelu_slope(pre_act.astype(F32)).reshape(SIDE, SIDE, OWN, HID_OWN)
    slope = jnp.where(even, slope.transpose(1, 0, 2, 3), slope).reshape(ROWS, HID_OWN)
    weights = weights.reshape(SIDE, SIDE, 2, W_ROWS, 256)
    far_low, far_high, right, left, own = pl.pallas_call(
        mlp_kernel,
        out_shape=[pltpu.VMEM((rows, HID), BF16) for rows in (48, 48, 96, 96, 96)],
        in_specs=[ANY] * 8 + [VMEM],
        out_specs=[VMEM] * 5,
        scratch_shapes=[
            pltpu.VMEM((SIDE, SIDE, ROWS, COLS), BF16),
            pltpu.VMEM((SIDE, SIDE, 2, HID_OWN, W2_COLS), BF16),
            pltpu.VMEM((SIDE, SIDE, 2, IN_OWN, 256), BF16),
            pltpu.VMEM((SIDE, SIDE, 2, TAIL, 256), BF16),
            pltpu.VMEM((ROWS, HID_OWN), BF16),
            pltpu.SemaphoreType.DMA((SIDE, 4)),
            pltpu.SemaphoreType.DMA((SIDE, 2)),
        ],
        cost_estimate=pl.CostEstimate(flops=3 << 30, bytes_accessed=16 << 20, transcendentals=0),
        compiler_params=pltpu.CompilerParams(vmem_limit_bytes=24 << 20),
    )(pinned(weights), line, a1, a2, b1, b2, a3, b3, slope)

    low, high = shift(far_low, 0, 1), shift(far_high, 0, -1)
    right, left = pl.pallas_call(
        relay_kernel,
        out_shape=[pltpu.VMEM((LINE_ROWS, HID), BF16)] * 2,
        in_specs=[VMEM] * 4,
        out_specs=[VMEM] * 2,
        compiler_params=pltpu.CompilerParams(vmem_limit_bytes=16 << 20),
    )(right, left, low, high)
    from_left, from_right = shift(right, 0, 1), shift(left, 0, -1)
    halfway, near_patches, near_gain = pl.pallas_call(
        add_kernel,
        out_shape=[pltpu.VMEM((SIDE * OWN, HID), BF16), pltpu.VMEM((OWN, HID), BF16), pltpu.VMEM((VIT,), F32)],
        in_specs=[VMEM] * 5,
        out_specs=[VMEM] * 3,
        compiler_params=pltpu.CompilerParams(vmem_limit_bytes=16 << 20),
    )(own, from_left, from_right, patches, ln_gain)
    last = exchange(halfway.reshape(SIDE, OWN, HID), 1)
    return call(norm_kernel, (OWN, HID), [VMEM] * 3)(last, near_patches, near_gain)


def solution(mesh):
    return jax.shard_map(
        per_device,
        mesh=mesh,
        in_specs=(
            P("prompt", "rollout", None, None),
            P("prompt", "rollout", None),
            P("prompt", "rollout"),
            P("prompt", "rollout"),
            P(("prompt", "rollout"), None),
            P(),
            P("rollout", "prompt"),
            P("prompt", "rollout"),
        ),
        out_specs=P(("prompt", "rollout"), None),
        check_vma=False,
    )
```

```python
import jax
import jax.numpy as jnp
from jax import lax
from jax.experimental import pallas as pl
from jax.experimental.pallas import tpu as pltpu
from jax.sharding import PartitionSpec as P

VIT = 1280
MERGE = 4
PROMPTS = 32
ROLLOUTS = 16
SIDE = 4
SLOTS = 50
PAD_SLOTS = 64
OWN = 24
ROWS = OWN * ROLLOUTS
D_LLM = 8192
COLS = D_LLM // ROLLOUTS
HID = 5120
HID_OWN = HID // ROLLOUTS
IN_OWN = HID // PROMPTS
W2_COLS = D_LLM // PROMPTS
RUNS = (48, 48, 32, 32)
TAIL = 48
W_ROWS = HID_OWN + IN_OWN + TAIL
AXES = ("prompt", "rollout")
F32 = jnp.float32
BF16 = jnp.bfloat16


def gelu_slope(value):
    return (
        0.5 * (1.0 + jax.scipy.special.erf(value * 0.7071067811865476))
        + value * jnp.exp(-0.5 * value * value) * 0.3989422804014327
    )


def dot_t(left, right):
    return lax.dot_general(left, right, (((1,), (1,)), ((), ())), preferred_element_type=F32)


def line_groups(phase):
    groups = []
    for prompt in range(PROMPTS):
        for other in range(SIDE):
            along_x = (prompt % 2 == 0) == (phase == 0)
            line = [(other * SIDE + i) if along_x else (i * SIDE + other) for i in range(SIDE)]
            groups.append([prompt * ROLLOUTS + r for r in line])
    return groups


def exchange(blocks, phase):
    return lax.all_to_all(
        blocks, AXES, split_axis=0, concat_axis=0, axis_index_groups=line_groups(phase), tiled=True
    )


def shift(value, phase, by):
    pairs = []
    for line in line_groups(phase):
        pairs += [(line[i], line[(i + by) % SIDE]) for i in range(SIDE)]
    return lax.ppermute(value, AXES, pairs)


def place_in_plane():
    rollout = lax.axis_index("rollout")
    even = lax.axis_index("prompt") % 2 == 0
    return even, jnp.where(even, rollout // SIDE, rollout % SIDE)


def weights_kernel(w2_ref, w1_ref, out_ref, block, w1, sems):
    base = HID_OWN + IN_OWN
    from_w2 = pltpu.make_async_copy(w2_ref, block.at[0:HID_OWN], sems.at[0])
    from_w1 = pltpu.make_async_copy(w1_ref, w1, sems.at[1])
    from_w2.start()
    from_w1.start()
    block[base:W_ROWS, :] = jnp.zeros((TAIL, 256), BF16)
    from_w1.wait()
    block[HID_OWN:base, :] = w1[:, 0:256]
    at = 0
    for n, rows in enumerate(RUNS):
        block[base : base + rows, 64 * n : 64 * n + 64] = w1[at : at + rows, 256:HID_OWN]
        at += rows
    from_w2.wait()
    to_out = pltpu.make_async_copy(block, out_ref, sems.at[2])
    to_out.start()
    to_out.wait()


def pack_kernel(count_ref, ids_ref, grads_ref, out_ref, meta):
    even, _ = place_in_plane()
    ids = ids_ref[...]
    owner = (ids * 2731) >> 16
    turned = (owner & 3) * SIDE + (owner >> 2)
    place = jnp.where(even, turned, owner) * OWN + ids - owner * OWN + 1
    live = lax.broadcasted_iota(jnp.int32, (1, SLOTS), 1) < count_ref[0, 0]
    place = jnp.where(live, place, 0)
    meta[...] = jnp.zeros((8, COLS), F32)
    meta[2:3, 0:SLOTS] = (place >> 4).astype(F32)
    meta[3:4, 0:SLOTS] = (place & 15).astype(F32)
    codes = meta[...]
    zeros = jnp.zeros((8, COLS), F32)
    for k in range(ROLLOUTS):
        cols = pl.ds(k * COLS, COLS)
        out_ref[k, 0:48, :] = grads_ref[0:48, cols]
        two = jnp.concatenate([grads_ref[48:SLOTS, cols].astype(F32), zeros[0:6]], axis=0)
        out_ref[k, 48:64, :] = jnp.concatenate([two + codes, zeros], axis=0).astype(BF16)


def sum_kernel(recv_ref, out_ref):
    rows = (lax.broadcasted_iota(jnp.int32, (ROWS, 4 * PAD_SLOTS), 0) + 1).astype(F32)
    total = jnp.zeros((ROWS, COLS), F32)
    for g in range(ROLLOUTS // 4):
        codes = jnp.zeros((8, 4 * PAD_SLOTS), F32)
        for k in range(4):
            tile = recv_ref[4 * g + k, 48:64, 0 : 4 * PAD_SLOTS].astype(F32)[0:8]
            codes = codes + (pltpu.roll(tile, PAD_SLOTS * k, 1) if k else tile)
        row = codes[2:3] * 16.0 + codes[3:4]
        onehot = jnp.where(rows == row, 1.0, 0.0).astype(BF16)
        block = recv_ref[4 * g : 4 * g + 4].reshape(4 * PAD_SLOTS, COLS)
        total = total + jnp.dot(onehot, block, preferred_element_type=F32)
    value = total.astype(BF16)
    for k in range(SIDE):
        out_ref[k] = value


GATHERED = (
    (0, ((0, 0),)),
    (3, ((1, 0), (2, 2))),
    (1, ((4, 0), (3, 2))),
    (2, ((5, 0), (6, 2))),
)


def mlp_kernel(w_ref, *refs):
    sums, (slope_hbm, out_ref, s, w2, w1, w1_tail, slope_ref, sems2, sems1, slope_sem) = refs[:7], refs[7:]
    even, second = place_in_plane()
    base = HID_OWN + IN_OWN
    copies, late = [], []
    for n, (offset, parts) in enumerate(GATHERED):
        other = lax.rem(second + offset, SIDE)
        count = SIDE // len(parts)
        for h, (operand, k) in enumerate(parts):
            span = slice(k, k + count)
            by_row = pltpu.make_async_copy(w_ref.at[other, span, :, 0:HID_OWN], w2.at[n, span], sems2.at[n, h])
            by_col = pltpu.make_async_copy(w_ref.at[span, other, :, 0:HID_OWN], w2.at[n, span], sems2.at[n, h])
            pl.when(even)(by_row.start)
            pl.when(jnp.logical_not(even))(by_col.start)
            copy = pltpu.make_async_copy(sums[operand], s.at[n, span], sems2.at[n, h + 2])
            copy.start()
            copies.append((n, span, by_row, copy))
    get_slope = pltpu.make_async_copy(slope_hbm, slope_ref, slope_sem.at[0])
    get_slope.start()
    for q in range(SIDE):
        pair = [
            pltpu.make_async_copy(w_ref.at[q, :, :, HID_OWN:base], w1.at[q], sems1.at[q, 0]),
            pltpu.make_async_copy(w_ref.at[q, :, :, base:W_ROWS], w1_tail.at[q], sems1.at[q, 1]),
        ]
        for copy in pair:
            copy.start()
        late.append(pair)
    hidden = None
    for n, span, *group in copies:
        for copy in group:
            copy.wait()
        for k in range(span.start, span.stop):
            block = s[n, k]
            part = dot_t(w2[n, k, 0], block[:, :W2_COLS]) + dot_t(w2[n, k, 1], block[:, W2_COLS:])
            hidden = part if hidden is None else hidden + part
    get_slope.wait()
    act = (hidden.T * slope_ref[...]).astype(BF16)
    width = HID // SIDE
    for q in range(SIDE):
        for copy in late[q]:
            copy.wait()
        fold = w1_tail[q]
        runs = [fold[:, :, :rows, 64 * n : 64 * n + 64] for n, rows in enumerate(RUNS)]
        tail = jnp.concatenate(runs, axis=2).reshape(width, 64)
        part = dot_t(act[:, 0:256], w1[q].reshape(width, 256)) + dot_t(act[:, 256:], tail)
        out_ref[:, width * q : width * (q + 1)] = part.astype(BF16)


def add_kernel(recv_ref, patches_ref, gain_ref, out_ref, near_patches_ref, near_gain_ref):
    total = recv_ref[0].astype(F32)
    for k in range(1, SIDE):
        total = total + recv_ref[k].astype(F32)
    out_ref[...] = total.astype(BF16)
    near_patches_ref[...] = patches_ref[...]
    near_gain_ref[...] = gain_ref[...]


def norm_kernel(recv_ref, patches_ref, gain_ref, out_ref):
    sums = []
    for m in range(MERGE):
        cols = slice(m * VIT, (m + 1) * VIT)
        upstream = recv_ref[0, :, cols].astype(F32)
        for k in range(1, SIDE):
            upstream = upstream + recv_ref[k, :, cols].astype(F32)
        sums.append(upstream)
    gain = gain_ref[...][None]
    for m in range(MERGE):
        cols = slice(m * VIT, (m + 1) * VIT)
        inputs = patches_ref[:, cols].astype(F32)
        scaled = sums[m] * gain
        inverse = lax.rsqrt(jnp.mean(inputs * inputs, axis=-1, keepdims=True) + 1e-06)
        inner = jnp.mean(scaled * inputs, axis=-1, keepdims=True)
        result = inverse * scaled - inputs * inverse * inverse * inverse * inner
        out_ref[:, cols] = result.astype(BF16)


VMEM = pl.BlockSpec(memory_space=pltpu.VMEM)
SMEM = pl.BlockSpec(memory_space=pltpu.SMEM)
ANY = pl.BlockSpec(memory_space=pl.ANY)


def call(kernel, shape, in_specs, flops=0, moved=0, vmem=16, scratch=(), fast=False, out_spec=VMEM):
    return pl.pallas_call(
        kernel,
        out_shape=pltpu.VMEM(shape, BF16) if fast else jax.ShapeDtypeStruct(shape, BF16),
        in_specs=in_specs,
        out_specs=out_spec,
        scratch_shapes=list(scratch),
        cost_estimate=pl.CostEstimate(flops=flops, bytes_accessed=moved, transcendentals=0),
        compiler_params=pltpu.CompilerParams(vmem_limit_bytes=vmem << 20),
    )


def pinned(value):
    return pltpu.with_memory_space_constraint(value, pltpu.HBM)


def per_device(row_grads, used_ids, used_count, pre_act, patches, ln_gain, w_fc2, w_fc1):
    weights = call(
        weights_kernel,
        (W_ROWS, 256),
        [ANY, ANY],
        out_spec=ANY,
        scratch=[
            pltpu.VMEM((W_ROWS, 256), BF16),
            pltpu.VMEM((IN_OWN, HID_OWN), BF16),
            pltpu.SemaphoreType.DMA((3,)),
        ],
    )(pinned(w_fc2), pinned(w_fc1))
    weights = lax.all_gather(weights, "prompt", axis=0, tiled=False)

    outgoing = call(
        pack_kernel, (ROLLOUTS, PAD_SLOTS, COLS), [SMEM, VMEM, VMEM], scratch=[pltpu.VMEM((8, COLS), F32)]
    )(used_count, used_ids[0], row_grads[0, 0])
    received = lax.all_to_all(outgoing, "rollout", split_axis=0, concat_axis=0, tiled=True)
    summed = call(sum_kernel, (SIDE, ROWS, COLS), [VMEM])(received)
    line = exchange(summed, 0)
    a1, b1 = shift(line[:2], 1, 1), shift(line[2:], 1, -1)
    a2, b2 = shift(line[2:], 1, 1), shift(line[:2], 1, -1)
    a3, b3 = shift(a1, 1, 1), shift(b1, 1, -1)

    even = lax.axis_index("prompt") % 2 == 0
    slope = gelu_slope(pre_act.astype(F32)).reshape(SIDE, SIDE, OWN, HID_OWN)
    slope = jnp.where(even, slope.transpose(1, 0, 2, 3), slope).reshape(ROWS, HID_OWN)
    weights = weights.reshape(SIDE, SIDE, 2, W_ROWS, 256)
    partial = pl.pallas_call(
        mlp_kernel,
        out_shape=pltpu.VMEM((ROWS, HID), BF16),
        in_specs=[ANY] * 9,
        out_specs=VMEM,
        scratch_shapes=[
            pltpu.VMEM((SIDE, SIDE, ROWS, COLS), BF16),
            pltpu.VMEM((SIDE, SIDE, 2, HID_OWN, W2_COLS), BF16),
            pltpu.VMEM((SIDE, SIDE, 2, IN_OWN, 256), BF16),
            pltpu.VMEM((SIDE, SIDE, 2, TAIL, 256), BF16),
            pltpu.VMEM((ROWS, HID_OWN), F32),
            pltpu.SemaphoreType.DMA((SIDE, 4)),
            pltpu.SemaphoreType.DMA((SIDE, 2)),
            pltpu.SemaphoreType.DMA((1,)),
        ],
        cost_estimate=pl.CostEstimate(flops=3 << 30, bytes_accessed=16 << 20, transcendentals=0),
        compiler_params=pltpu.CompilerParams(vmem_limit_bytes=24 << 20),
    )(pinned(weights), line, a1, a2, b1, b2, a3, b3, slope)

    halfway = exchange(partial.reshape(SIDE, SIDE * OWN, HID), 0)
    halfway, near_patches, near_gain = pl.pallas_call(
        add_kernel,
        out_shape=[pltpu.VMEM((SIDE * OWN, HID), BF16), pltpu.VMEM((OWN, HID), BF16), pltpu.VMEM((VIT,), F32)],
        in_specs=[VMEM] * 3,
        out_specs=[VMEM] * 3,
        compiler_params=pltpu.CompilerParams(vmem_limit_bytes=16 << 20),
    )(halfway, patches, ln_gain)
    last = exchange(halfway.reshape(SIDE, OWN, HID), 1)
    return call(norm_kernel, (OWN, HID), [VMEM] * 3)(last, near_patches, near_gain)


def solution(mesh):
    return jax.shard_map(
        per_device,
        mesh=mesh,
        in_specs=(
            P("prompt", "rollout", None, None),
            P("prompt", "rollout", None),
            P("prompt", "rollout"),
            P("prompt", "rollout"),
            P(("prompt", "rollout"), None),
            P(),
            P("rollout", "prompt"),
            P("prompt", "rollout"),
        ),
        out_specs=P(("prompt", "rollout"), None),
        check_vma=False,
    )
```
